32 devices in a mesh: dp: 16 (over z, y, x), row: 2 (over core).
Axes of the slice: x: 2, y: 2, z: 4, core: 2. Of those that a mesh axis runs over, the one named last changes fastest.
Arguments:
- frames: bfloat16 [32, 16, 32, 256], P('dp', 'row'), may hold values from -6 to 6
- enc_w1: bfloat16 [3, 3, 256, 512], replicated, may hold values from -0.125 to 0.125
- enc_gain1: float32 [512], replicated, may hold values from 0.1 to 1.9
- enc_bias1: float32 [512], replicated, may hold values from -3 to 3
- enc_w2: bfloat16 [3, 3, 512, 512], replicated, may hold values from -0.09375 to 0.09375
- enc_gain2: float32 [512], replicated, may hold values from 0.1 to 1.9
- enc_bias2: float32 [512], replicated, may hold values from -3 to 3
- att_w1: bfloat16 [3, 512, 512], replicated, may hold values from -0.25 to 0.25
- att_gain: float32 [512], replicated, may hold values from 0.1 to 1.9
- att_bias: float32 [512], replicated, may hold values from -3 to 3
- att_w: bfloat16 [3, 512, 512], replicated, may hold values from -0.25 to 0.25
- dec_w1: bfloat16 [3, 3, 512, 512], P(None, None, 'row'), may hold values from -0.1875 to 0.1875
- dec_gain1: float32 [512], P('row'), may hold values from 0.1 to 1.9
- dec_bias1: float32 [512], P('row'), may hold values from -3 to 3
- dec_w2: bfloat16 [3, 3, 512, 512], P(None, None, 'row'), may hold values from -0.09375 to 0.09375
- dec_gain2: float32 [512], P('row'), may hold values from 0.1 to 1.9
- dec_bias2: float32 [512], P('row'), may hold values from -3 to 3
- labels: int32 [32], P('dp'), may hold values from 0 to 2
- pool_index: int32 [32, 8, 16], P('dp'), may hold values from 0 to 3
- out_grad: bfloat16 [512, 32, 512], P('row', 'dp'), may hold values from -6 to 6
Outputs:
- decoded: bfloat16 [512, 32, 512], P('row', 'dp')
- frames_grad: float32 [32, 16, 32, 256], P('dp', 'row')
- enc_w1_grad: float32 [3, 3, 256, 512], P(None, None, None, 'row')
- enc_gain1_grad: float32 [512], replicated
- enc_bias1_grad: float32 [512], replicated
- enc_w2_grad: float32 [3, 3, 512, 512], P(None, None, None, 'row')
- enc_gain2_grad: float32 [512], replicated
- enc_bias2_grad: float32 [512], replicated
- att_w1_grad: float32 [3, 512, 512], P(None, None, 'row')
- att_gain_grad: float32 [512], replicated
- att_bias_grad: float32 [512], replicated
- att_w_grad: float32 [3, 512, 512], P(None, None, 'row')
- dec_w1_grad: float32 [3, 3, 512, 512], P(None, None, 'row')
- dec_gain1_grad: float32 [512], P('row')
- dec_bias1_grad: float32 [512], P('row')
- dec_w2_grad: float32 [3, 3, 512, 512], P(None, None, 'row')
- dec_gain2_grad: float32 [512], P('row')
- dec_bias2_grad: float32 [512], P('row')
The draws below stay inside these ranges and needn't reach their ends.
All inputs are finite; a program needn't handle non-finite values.
Results may differ from the reference program's by a relative error of at most 0.02.
Values may be sent and summed in bfloat16 or wider, within the bound.
No kernel may reach another device: no remote copies, remote signals or barrier semaphores. Data moves between devices by JAX's collectives and lax.ppermute only.
A program may use at most 192 MiB of HBM per device.

```python
import jax
import jax.numpy as jnp
from jax import lax

C0 = 256
C1 = 512
TASKS = 3
H = 16
W = 32
MICRO = 2
FR_MB = 1
FRAMES = 32
N_DP = 16


def place_ends(values, stream_key, least, top_value):
    place = [jax.random.randint(jax.random.fold_in(stream_key, axis), (), 0, length) for axis, length in enumerate(values.shape)]
    main_axis = values.shape.index(max(values.shape))
    neighbour = place[:main_axis] + [(place[main_axis] + 1) % values.shape[main_axis]] + place[main_axis + 1:]
    return values.at[tuple(place)].set(least).at[tuple(neighbour)].set(top_value)


def level_of(own_key, extent, shards, smallest, top_value):
    level, own = 1.0, jax.random.fold_in(own_key, 6)
    for axis_at, parts in shards:
        draws = jnp.exp(jax.random.uniform(jax.random.fold_in(own, axis_at), (parts,), jnp.float32, smallest / len(shards), top_value / len(shards)))
        level = level * jnp.repeat(draws, extent[axis_at] // parts).reshape([-1 if axis == axis_at else 1 for axis in range(len(extent))])
    return level


def bell_draw(stream_key, extent, spread, bound, shards=(), kind=jnp.bfloat16):
    loudness = level_of(stream_key, extent, shards, -0.22, 0.18) if shards else 1.0
    values = jax.random.normal(stream_key, extent, jnp.float32) * spread * loudness
    return jnp.minimum(jnp.maximum(values, -bound), bound).astype(kind)


def setup_inputs(seed: int = 0) -> dict:
    key_list = jax.random.split(jax.random.key(seed), 21)
    return {
        "frames": bell_draw(key_list[0], (FRAMES, H, W, C0), 1.0, 6.0, ((0, 16), (1, 2))),
        "enc_w1": bell_draw(key_list[1], (3, 3, C0, C1), (9 * C0) ** -0.5, 0.125),
        "enc_gain1": jnp.clip(1.0 + 0.18 * jax.random.normal(key_list[2], (C1,), jnp.float32), 0.1, 1.9),
        "enc_bias1": bell_draw(key_list[3], (C1,), 0.5, 3.0, (), jnp.float32),
        "enc_w2": bell_draw(key_list[4], (3, 3, C1, C1), (9 * C1) ** -0.5, 0.09375),
        "enc_gain2": jnp.clip(1.0 + 0.18 * jax.random.normal(key_list[5], (C1,), jnp.float32), 0.1, 1.9),
        "enc_bias2": bell_draw(key_list[6], (C1,), 0.5, 3.0, (), jnp.float32),
        "att_w1": bell_draw(key_list[7], (TASKS, C1, C1), C1 ** -0.5, 0.25),
        "att_gain": jnp.clip(1.0 + 0.18 * jax.random.normal(key_list[8], (C1,), jnp.float32), 0.1, 1.9),
        "att_bias": bell_draw(key_list[9], (C1,), 0.5, 3.0, (), jnp.float32),
        "att_w": bell_draw(key_list[10], (TASKS, C1, C1), C1 ** -0.5, 0.25),
        "dec_w1": bell_draw(key_list[11], (3, 3, C1, C1), (9 * C1 // 4) ** -0.5, 0.1875, ((2, 2),)),
        "dec_gain1": jnp.clip(1.0 + 0.18 * jax.random.normal(key_list[12], (C1,), jnp.float32), 0.1, 1.9),
        "dec_bias1": bell_draw(key_list[13], (C1,), 0.5, 3.0, ((0, 2),), jnp.float32),
        "dec_w2": bell_draw(key_list[14], (3, 3, C1, C1), (9 * C1) ** -0.5, 0.09375, ((2, 2),)),
        "dec_gain2": jnp.clip(1.0 + 0.18 * jax.random.normal(key_list[15], (C1,), jnp.float32), 0.1, 1.9),
        "dec_bias2": bell_draw(key_list[16], (C1,), 0.5, 3.0, ((0, 2),), jnp.float32),
        "labels": place_ends(jax.random.randint(key_list[17], (FRAMES,), 0, TASKS), jax.random.fold_in(key_list[17], 1), 0, TASKS - 1).astype(jnp.int32),
        "pool_index": place_ends(jax.random.randint(key_list[18], (FRAMES, H // 2, W // 2), 0, 4), jax.random.fold_in(key_list[18], 1), 0, 3).astype(jnp.int32),
        "out_grad": bell_draw(key_list[19], (C1, FRAMES, H * W), 1.0, 6.0, ((0, 2), (1, 16))),
    }


EPS = 1e-05

@jax.custom_vjp
def low(v):
    return lax.optimization_barrier(v.astype(jnp.bfloat16)).astype(jnp.float32)

@jax.custom_vjp
def low_back(v):
    return v

def low_keep(v):
    return (low(v), None)

def low_pass(kept, grad):
    return (grad,)

def back_keep(v):
    return (v, None)

def back_low(kept, grad):
    return (low(grad),)
low.defvjp(low_keep, low_pass)
low_back.defvjp(back_keep, back_low)

def conv_same(source, weight):
    padded = jnp.pad(source, ((0, 0), (1, 1), (1, 1), (0, 0)))
    row_count = source.shape[1]
    col_count = source.shape[2]
    total = jnp.zeros(source.shape[:3] + (weight.shape[3],), jnp.float32)
    for offset_row in range(3):
        for offset_col in range(3):
            window = padded[:, offset_row:offset_row + row_count, offset_col:offset_col + col_count, :]
            total = total + jnp.einsum('bhwc,cd->bhwd', window, weight[offset_row, offset_col], precision=lax.Precision.HIGHEST)
    return total

def batch_norm(pre_act, gain, bias):
    mean_value = lax.optimization_barrier(jnp.mean(pre_act, axis=(0, 1, 2)))
    square_mean = lax.optimization_barrier(jnp.mean(pre_act * pre_act, axis=(0, 1, 2)))
    inv_scale = lax.rsqrt(square_mean - mean_value * mean_value + EPS)
    return (pre_act - mean_value) * inv_scale * gain + bias

def forward(source, params, label_ids, index_ids):
    enc_w1, enc_gain1, enc_bias1, enc_w2, enc_gain2, enc_bias2, att_w1, att_gain, att_bias, att_w, dec_w1, dec_gain1, dec_bias1, dec_w2, dec_gain2, dec_bias2 = params
    pre_one = low_back(conv_same(source, enc_w1))
    hidden_one = low(jax.nn.silu(batch_norm(pre_one, enc_gain1, enc_bias1)))
    pre_two = low_back(conv_same(hidden_one, enc_w2))
    shared = jax.nn.silu(batch_norm(pre_two, enc_gain2, enc_bias2))
    task_pick = (label_ids[:, None] == jnp.arange(TASKS, dtype=jnp.int32)[None, :]).astype(jnp.float32)
    picked_w1 = jnp.einsum('bk,kcd->bcd', task_pick, att_w1, precision=lax.Precision.HIGHEST)
    att_pre = low_back(jnp.einsum('bhwc,bcd->bhwd', hidden_one, picked_w1, precision=lax.Precision.HIGHEST))
    att_hidden = low(jax.nn.silu(batch_norm(att_pre, att_gain, att_bias)))
    picked_w = jnp.einsum('bk,kcd->bcd', task_pick, att_w, precision=lax.Precision.HIGHEST)
    logits = low_back(jnp.einsum('bhwc,bcd->bhwd', att_hidden, picked_w, precision=lax.Precision.HIGHEST))
    attended = jax.nn.sigmoid(logits) * shared
    batch = source.shape[0]
    grid = attended.reshape(batch, H // 2, 2, W // 2, 2, C1)
    masks = [(index_ids == slot_id).astype(jnp.float32)[..., None] for slot_id in range(4)]
    pooled = masks[0] * grid[:, :, 0, :, 0, :] + masks[1] * grid[:, :, 0, :, 1, :] + masks[2] * grid[:, :, 1, :, 0, :] + masks[3] * grid[:, :, 1, :, 1, :]
    pooled = low_back(low(pooled))
    upper = jnp.stack([pooled * masks[0], pooled * masks[1]], axis=3)
    lower = jnp.stack([pooled * masks[2], pooled * masks[3]], axis=3)
    unpooled = jnp.stack([upper, lower], axis=2).reshape(batch, H, W, C1)
    pre_three = low_back(conv_same(unpooled, dec_w1))
    hidden_three = low(jax.nn.silu(batch_norm(pre_three, dec_gain1, dec_bias1)))
    pre_four = low_back(conv_same(hidden_three, dec_w2))
    return jax.nn.silu(batch_norm(pre_four, dec_gain2, dec_bias2))

def reference(frames, enc_w1, enc_gain1, enc_bias1, enc_w2, enc_gain2, enc_bias2, att_w1, att_gain, att_bias, att_w, dec_w1, dec_gain1, dec_bias1, dec_w2, dec_gain2, dec_bias2, labels, pool_index, out_grad):
    params = tuple((item.astype(jnp.float32) for item in (enc_w1, enc_gain1, enc_bias1, enc_w2, enc_gain2, enc_bias2, att_w1, att_gain, att_bias, att_w, dec_w1, dec_gain1, dec_bias1, dec_w2, dec_gain2, dec_bias2)))
    frame_view = frames.astype(jnp.float32).reshape(N_DP, MICRO, FR_MB, H, W, C0)
    cot_view = out_grad.astype(jnp.float32).reshape(C1, N_DP, MICRO, FR_MB, H, W)
    label_view = labels.reshape(N_DP, MICRO, FR_MB)
    index_view = pool_index.reshape(N_DP, MICRO, FR_MB, H // 2, W // 2)
    decoded_parts = []
    input_parts = []
    totals = [jnp.zeros_like(item) for item in params]
    for micro in range(MICRO):
        source = frame_view[:, micro].reshape(-1, H, W, C0)
        label_ids = label_view[:, micro].reshape(-1)
        index_ids = index_view[:, micro].reshape(-1, H // 2, W // 2)
        cot_micro = jnp.transpose(cot_view[:, :, micro].reshape(C1, -1, H, W), (1, 2, 3, 0))

        def run_micro(source_in, *weights):
            return forward(source_in, weights, label_ids, index_ids)
        result, pullback = jax.vjp(run_micro, source, *params)
        grads = pullback(cot_micro)
        input_parts.append(grads[0].reshape(N_DP, FR_MB, H, W, C0))
        totals = [total + grad_item for total, grad_item in zip(totals, grads[1:])]
        decoded_parts.append(jnp.transpose(result, (3, 0, 1, 2)).reshape(C1, N_DP, FR_MB, H * W))
    decoded = jnp.stack(decoded_parts, axis=2).reshape(C1, N_DP * MICRO * FR_MB, H * W).astype(jnp.bfloat16)
    frames_grad = jnp.stack(input_parts, axis=1).reshape(N_DP * MICRO * FR_MB, H, W, C0)
    return (decoded, frames_grad, totals[0], totals[1], totals[2], totals[3], totals[4], totals[5], totals[6], totals[7], totals[8], totals[9], totals[10], totals[11], totals[12], totals[13], totals[14], totals[15])
```

```python
import functools

import jax
import jax.numpy as jnp
from jax import lax
from jax.experimental import pallas as pl
from jax.experimental.pallas import tpu as pltpu
from jax.sharding import PartitionSpec as P

EPS = 1e-05
F32 = jnp.float32
BF16 = jnp.bfloat16
SLABS = 16
MIB = 2**20


def dot(left, right):
    return jnp.dot(left, right, preferred_element_type=F32)


def dot_nt(left, right):
    return lax.dot_general(left, right, (((1,), (1,)), ((), ())), preferred_element_type=F32)


def slope(act):
    sig = jax.nn.sigmoid(act)
    return sig * (1.0 + act * (1.0 - sig))


def silu(act):
    return act * jax.nn.sigmoid(act)


def clear_rims(buf, width):
    rows, lanes = buf.shape
    rim = jnp.zeros((width, lanes), BF16)
    buf[0:width, :] = rim
    buf[rows - width : rows, :] = rim


def fill(buf, value, width, lane, step):
    pixels, chans = value.shape
    col = lax.broadcasted_iota(jnp.int32, (pixels, 1), 0) & (width - 1)
    before = jnp.where(col == 0, 0.0, pltpu.roll(value, 1, 0))
    after = jnp.where(col == width - 1, 0.0, pltpu.roll(value, pixels - 1, 0))
    for at, part in enumerate((before, value, after)):
        start = lane + at * step
        buf[width : width + pixels, start : start + chans] = part.astype(BF16)


def conv(buf, weights, pixels, width):
    total, lane = None, 0
    for ref in weights:
        depth = ref.shape[1]
        for i in range(3):
            term = dot(buf[i * width : i * width + pixels, lane : lane + depth], ref[i])
            total = term if total is None else total + term
        lane += depth
    return total


def shifted(buf, i, j, pixels, width, chans):
    return buf[(2 - i) * width : (2 - i) * width + pixels, (2 - j) * chans : (3 - j) * chans]


def conv_back(buf, ref, pixels, width):
    chans = ref.shape[2]
    depth = ref.shape[1] // 3
    total = None
    for i in range(3):
        for j in range(3):
            term = dot_nt(
                shifted(buf, i, j, pixels, width, chans), ref[i, j * depth : (j + 1) * depth, :]
            )
            total = term if total is None else total + term
    return total


def put_sums(ref, terms):
    for at, term in enumerate(terms):
        row = jnp.sum(term, axis=0, keepdims=True)
        ref[:, at : at + 1, :] = jnp.broadcast_to(row[None], (ref.shape[0], 1, ref.shape[2]))


def gather_sums(ref):
    return jnp.sum(ref[...], axis=0)


def moments(ref, at, count):
    total = gather_sums(ref)
    mean = total[at : at + 1] / count
    square = total[at + 1 : at + 2] / count
    return mean, lax.rsqrt(square - mean * mean + EPS)


def normed(pre, mom):
    return (pre - mom[0]) * mom[1]


def norm_back(grad, pre, mom, gain, total, at, count):
    xhat = normed(pre, mom)
    return (gain * mom[1]) * (
        grad - total[at : at + 1] / count - xhat * (total[at + 1 : at + 2] / count)
    )


def row_of(ref):
    return ref[...].reshape(1, -1)


def half_at(ids, other, half):
    side = ids[0]
    if other:
        side = 1 - side
    return pl.ds(pl.multiple_of(side * half, half), half)


def enc_one_kernel(width, ids, own, far, w_ref, pre_ref, sum_ref, flat, buf):
    pixels, chans = flat.shape
    band = pixels // 2
    side = ids[0]
    flat[half_at(ids, False, band), :] = own[side].astype(F32)
    flat[half_at(ids, True, band), :] = far[side].astype(F32)
    clear_rims(buf, width)
    fill(buf, flat[...], width, 0, chans)
    pre = conv(buf, (w_ref,), pixels, width)
    pre_ref[...] = pre
    put_sums(sum_ref, (pre, pre * pre))


def enc_two_kernel(
    width, count, ids, labels, st1, pre1, gain1, bias1, w_ref, aw_ref, hid_ref, pre2_ref, att_ref, sum_ref, buf
):
    pixels, chans = pre1.shape
    mom = moments(st1, 0, count)
    hidden = silu(normed(pre1[...], mom) * row_of(gain1) + row_of(bias1))
    clear_rims(buf, width)
    fill(buf, hidden, width, 0, chans)
    hid_ref[...] = hidden.astype(BF16)
    att = dot(hid_ref[...], aw_ref[labels[ids[0]]])
    att_ref[...] = att
    pre = conv(buf, (w_ref,), pixels, width)
    pre2_ref[...] = pre
    put_sums(sum_ref, (pre, pre * pre, att, att * att))


def dec_one_kernel(
    width, count, ids, labels, st2, pre2, att_pre, gain2, bias2, gain_a, bias_a, aw_ref, mask, w_own, w_far,
    hid_ref, shared_ref, gate_ref, pre3_ref, sum_ref, keep_ref, send_ref, flat, buf,
):
    pixels, chans = pre2.shape
    half = chans // 2
    shared = silu(normed(pre2[...], moments(st2, 0, count)) * row_of(gain2) + row_of(bias2))
    shared_ref[...] = shared
    hid = silu(normed(att_pre[...], moments(st2, 2, count)) * row_of(gain_a) + row_of(bias_a))
    hid_ref[...] = hid.astype(BF16)
    gate = jax.nn.sigmoid(dot(hid_ref[...], aw_ref[labels[ids[0]]]))
    gate_ref[...] = gate
    flat[...] = gate * shared * mask[...]
    clear_rims(buf, width)
    for other, ref in ((False, keep_ref), (True, send_ref)):
        part = flat[:, half_at(ids, other, half)]
        fill(buf, part, width, 3 * half * other, half)
        ref[...] = part.astype(BF16)
    pre = conv(buf, (w_own, w_far), pixels, width)
    pre3_ref[...] = pre
    put_sums(sum_ref, (pre, pre * pre))


def dec_two_kernel(
    width, count, ids, st3, pre3, params, w_own, w_far, pre4_ref, sum_ref, keep_ref, send_ref, flat, buf
):
    pixels, chans = pre3.shape
    half = chans // 2
    flat[...] = silu(normed(pre3[...], moments(st3, 0, count)) * params[0:1, :] + params[1:2, :])
    clear_rims(buf, width)
    for other, ref in ((False, keep_ref), (True, send_ref)):
        part = flat[:, half_at(ids, other, half)]
        fill(buf, part, width, 3 * half * other, half)
        ref[...] = part.astype(BF16)
    pre = conv(buf, (w_own, w_far), pixels, width)
    pre4_ref[...] = pre
    put_sums(sum_ref, (pre, pre * pre))


def top_kernel(count, ids, st4, pre4, params, og_own, og_far, dact_ref, sum_ref, keep_ref, send_ref, cot, out):
    pixels, chans = pre4.shape
    half = chans // 2
    cot[:, half_at(ids, False, half)] = og_own[...].astype(F32).T
    cot[:, half_at(ids, True, half)] = og_far[...].astype(F32).T
    xhat = normed(pre4[...], moments(st4, 0, count))
    act = xhat * params[2:3, :] + params[3:4, :]
    sig = jax.nn.sigmoid(act)
    out[...] = act * sig
    dact = cot[...] * (sig * (1.0 + act * (1.0 - sig)))
    dact_ref[...] = dact
    put_sums(sum_ref, (dact, dact * xhat))
    for other, ref in ((False, keep_ref), (True, send_ref)):
        ref[...] = out[:, half_at(ids, other, half)].T.astype(BF16)


def dec_two_back_kernel(
    width, count, ids, st4, st4b, pre4, dact4, params, w_own, w_far, st3, pre3,
    dz_ref, dact_ref, sum_ref, tot_ref, flat, buf,
):
    pixels, chans = pre4.shape
    half = chans // 2
    total = gather_sums(st4b)
    tot_ref[...] = total
    dz = norm_back(dact4[...], pre4[...], moments(st4, 0, count), params[2:3, :], total, 0, count)
    dz_ref[...] = dz.astype(BF16)
    clear_rims(buf, width)
    fill(buf, dz, width, 0, chans)
    for other, ref in ((False, w_own), (True, w_far)):
        flat[:, half_at(ids, other, half)] = conv_back(buf, ref, pixels, width)
    xhat = normed(pre3[...], moments(st3, 0, count))
    dact = flat[...] * slope(xhat * params[0:1, :] + params[1:2, :])
    dact_ref[...] = dact
    put_sums(sum_ref, (dact, dact * xhat))


def dec_one_back_kernel(
    width, count, ids, labels, st3, st3b, pre3, dact3, params, w_own, w_far, mask, gate_ref, shared_ref, aw_ref,
    st2, att_pre, pre2, gain_a, bias_a, gain2, bias2,
    dz_ref, dlog_keep, dlog_send, datt_ref, dact2_ref, sum_ref, tot_ref, flat, dlog, buf,
):
    pixels, chans = pre3.shape
    half = chans // 2
    total = gather_sums(st3b)
    tot_ref[...] = total
    dz = norm_back(dact3[...], pre3[...], moments(st3, 0, count), params[0:1, :], total, 0, count)
    dz_ref[...] = dz.astype(BF16)
    clear_rims(buf, width)
    fill(buf, dz, width, 0, chans)
    for other, ref in ((False, w_own), (True, w_far)):
        flat[:, half_at(ids, other, half)] = conv_back(buf, ref, pixels, width)
    grad = (flat[...] * mask[...]).astype(BF16).astype(F32)
    gate = gate_ref[...]
    dlog[...] = grad * shared_ref[...] * gate * (1.0 - gate)
    for other, ref in ((False, dlog_keep), (True, dlog_send)):
        ref[...] = dlog[:, half_at(ids, other, half)].astype(BF16)
    dhid = dot_nt(dlog[...].astype(BF16), aw_ref[labels[ids[0]]])
    att_hat = normed(att_pre[...], moments(st2, 2, count))
    datt = dhid * slope(att_hat * row_of(gain_a) + row_of(bias_a))
    datt_ref[...] = datt
    xhat2 = normed(pre2[...], moments(st2, 0, count))
    dact2 = grad * gate * slope(xhat2 * row_of(gain2) + row_of(bias2))
    dact2_ref[...] = dact2
    put_sums(sum_ref, (dact2, dact2 * xhat2, datt, datt * att_hat))


def enc_two_back_kernel(
    width, count, ids, labels, st2, st2b, att_pre, datt_ref, gain_a, pre2, dact2, gain2, aw_ref, w_ref,
    st1, pre1, gain1, bias1,
    datt_keep, datt_send, dz_keep, dz_send, dact_ref, sum_ref, tot_ref, flat, datt, buf,
):
    pixels, chans = pre2.shape
    half = chans // 2
    total = gather_sums(st2b)
    tot_ref[...] = total
    dz = norm_back(dact2[...], pre2[...], moments(st2, 0, count), row_of(gain2), total, 0, count)
    flat[...] = dz
    for other, ref in ((False, dz_keep), (True, dz_send)):
        ref[...] = flat[:, half_at(ids, other, half)].astype(BF16)
    clear_rims(buf, width)
    fill(buf, dz, width, 0, chans)
    datt[...] = norm_back(
        datt_ref[...], att_pre[...], moments(st2, 2, count), row_of(gain_a), total, 2, count
    )
    for other, ref in ((False, datt_keep), (True, datt_send)):
        ref[...] = datt[:, half_at(ids, other, half)].astype(BF16)
    dhid = dot_nt(datt[...].astype(BF16), aw_ref[labels[ids[0]]])
    dhid = dhid + conv_back(buf, w_ref, pixels, width)
    xhat = normed(pre1[...], moments(st1, 0, count))
    dact = dhid * slope(xhat * row_of(gain1) + row_of(bias1))
    dact_ref[...] = dact
    put_sums(sum_ref, (dact, dact * xhat))


def enc_one_back_kernel(
    width, count, ids, st1, st1b, pre1, dact1, gain1, w_ref, dz_keep, dz_send, fg_keep, fg_send, tot_ref, flat, back, buf
):
    pixels, chans = pre1.shape
    half = chans // 2
    total = gather_sums(st1b)
    tot_ref[...] = total
    dz = norm_back(dact1[...], pre1[...], moments(st1, 0, count), row_of(gain1), total, 0, count)
    flat[...] = dz
    for other, ref in ((False, dz_keep), (True, dz_send)):
        ref[...] = flat[:, half_at(ids, other, half)].astype(BF16)
    clear_rims(buf, width)
    fill(buf, dz, width, 0, chans)
    back[...] = conv_back(buf, w_ref, pixels, width)
    for other, ref in ((False, fg_keep), (True, fg_send)):
        ref[...] = back[half_at(ids, other, pixels // 2), :]


def lay_rows(ids, value, at, tmp, slot, turned):
    rows = turned.shape[1]
    part = rows // SLABS
    tmp[slot, 0:rows, :] = value.astype(F32).T.astype(BF16)
    for t in range(SLABS):
        start = pl.multiple_of((ids[1] ^ t) * part, part)
        turned[at, t * part : (t + 1) * part, :] = tmp[slot, pl.ds(start, part), :]


def store_slabs(keep_ref, send_ref, row, part, lane, value):
    low = value.astype(BF16)
    mid = SLABS // 2
    lanes = value.shape[1]
    for t in range(SLABS):
        ref, at = (keep_ref, t) if t < mid else (send_ref, t - mid)
        ref[at, row : row + part, lane : lane + lanes] = low[t * part : (t + 1) * part]


def conv_weights(ids, width, values, grads, keep_ref, send_ref, tmp, turned, bufs):
    pixels, chans = grads[0].shape
    part = turned.shape[1] // SLABS
    for at in range(2):
        lay_rows(ids, values[at], at, tmp, at, turned)
        clear_rims(bufs.at[at], width)
        fill(bufs.at[at], grads[at][...].astype(F32), width, 0, chans)
    for i in range(3):
        for j in range(3):
            total = dot(turned[0], shifted(bufs.at[0], i, j, pixels, width, chans))
            total = total + dot(turned[1], shifted(bufs.at[1], i, j, pixels, width, chans))
            store_slabs(keep_ref, send_ref, (3 * i + j) * part, part, 0, total)


def task_weights(ids, labels, tasks, values, grads, tmp, turned):
    for at in range(2):
        lay_rows(ids, values[at], at, tmp, 2 + at, turned)
    side = ids[0]
    near = dot(turned[0], grads[0])
    far = dot(turned[1], grads[1])
    sums = []
    for task in range(tasks):
        take_near = (labels[side] == task).astype(F32)
        take_far = (labels[1 - side] == task).astype(F32)
        sums.append(near * take_near + far * take_far)
    return sums


def grad_dec_two_kernel(width, ids, v_own, v_far, dz_own, dz_far, keep_ref, send_ref, tmp, turned, bufs):
    conv_weights(ids, width, (v_own[...], v_far[...]), (dz_own, dz_far), keep_ref, send_ref, tmp, turned, bufs)


def grad_dec_one_kernel(
    width, tasks, ids, labels, v_own, v_far, dz_own, dz_far, h_own, h_far, dl_own, dl_far,
    keep_ref, send_ref, tmp, turned, turned_att, bufs,
):
    conv_weights(ids, width, (v_own[...], v_far[...]), (dz_own, dz_far), keep_ref, send_ref, tmp, turned, bufs)
    sums = task_weights(
        ids, labels, tasks, (h_own[...], h_far[...]), (dl_own[...], dl_far[...]), tmp, turned_att
    )
    base = 9 * (turned.shape[1] // SLABS)
    part = turned_att.shape[1] // SLABS
    lanes = dl_own.shape[1]
    fold = tasks * part // 2
    mid = SLABS // 2
    for task, total in enumerate(sums):
        low = total.astype(BF16)
        for t in range(SLABS):
            ref, at = (keep_ref, t) if t < mid else (send_ref, t - mid)
            for piece in range(0, part, 16):
                row = task * part + piece
                side, line = row // fold, row % fold
                ref[at, base + line : base + line + 16, side * lanes : (side + 1) * lanes] = low[
                    t * part + piece : t * part + piece + 16
                ]


def grad_enc_two_kernel(
    width, tasks, ids, labels, h_own, h_far, dz_own, dz_far, da_own, da_far, keep_ref, send_ref, tmp, turned, bufs
):
    values = (h_own[...], h_far[...])
    conv_weights(ids, width, values, (dz_own, dz_far), keep_ref, send_ref, tmp, turned, bufs)
    part = turned.shape[1] // SLABS
    side = ids[0]
    near = dot(turned[0], da_own[...])
    far = dot(turned[1], da_far[...])
    for task in range(tasks):
        take_near = (labels[side] == task).astype(F32)
        take_far = (labels[1 - side] == task).astype(F32)
        total = near * take_near + far * take_far
        store_slabs(keep_ref, send_ref, (9 + task) * part, part, 0, total)


def grad_enc_one_kernel(width, ids, own, far, dz_own, dz_far, keep_ref, send_ref, flat, tmp, turned, bufs):
    band = flat.shape[1] // 2
    side = ids[0]
    values = []
    for at, frame in enumerate((side, 1 - side)):
        flat[at, half_at(ids, False, band), :] = own[frame].astype(F32)
        flat[at, half_at(ids, True, band), :] = far[frame].astype(F32)
        values.append(flat[at])
    conv_weights(ids, width, values, (dz_own, dz_far), keep_ref, send_ref, tmp, turned, bufs)


def slab_of(parts, t):
    for ref in parts:
        if t < ref.shape[0]:
            return ref, t
        t -= ref.shape[0]
    raise IndexError(t)


def spread_kernel(folded, n_parts, ids, *refs):
    parts, outs = refs[:n_parts], refs[n_parts:]
    taps, rows, lanes = outs[0].shape
    part = rows // SLABS
    for t in range(SLABS):
        ref, at = slab_of(parts, t)
        place = pl.ds(pl.multiple_of((ids[1] ^ t) * part, part), part)
        for tap in range(taps):
            outs[0][tap, place, :] = ref[at, tap * part : (tap + 1) * part, :].astype(F32)
        if len(outs) == 1:
            continue
        tasks, more, narrow = outs[1].shape
        step = more // SLABS
        base = taps * part
        start = pl.multiple_of((ids[1] ^ t) * step, step)
        fold = tasks * step // 2
        for task in range(tasks):
            if not folded:
                outs[1][task, pl.ds(start, step), :] = ref[
                    at, base + task * step : base + (task + 1) * step, :
                ].astype(F32)
                continue
            for piece in range(0, step, 16):
                row = task * step + piece
                side, line = row // fold, row % fold
                outs[1][task, pl.ds(start + piece, 16), :] = ref[
                    at, base + line : base + line + 16, side * narrow : (side + 1) * narrow
                ].astype(F32)


def arr(shape, kind=F32):
    return jax.ShapeDtypeStruct(shape, kind)


def call(body, name, n_scalars, args, outs, scratch=(), flops=0):
    smem = pl.BlockSpec(memory_space=pltpu.SMEM)
    vmem = pl.BlockSpec(memory_space=pltpu.VMEM)
    moved = sum(a.size * a.dtype.itemsize for a in list(args) + list(outs))
    return pl.pallas_call(
        body,
        out_shape=outs,
        in_specs=[smem] * n_scalars + [vmem] * (len(args) - n_scalars),
        out_specs=[vmem] * len(outs),
        scratch_shapes=list(scratch),
        name=name,
        compiler_params=pltpu.CompilerParams(vmem_limit_bytes=40 * MIB),
        cost_estimate=pl.CostEstimate(flops=flops, bytes_accessed=moved, transcendentals=0),
    )(*args)


def swap_cores(value):
    return lax.ppermute(value, "row", [(0, 1), (1, 0)])


def exchange(value, masks):
    count, cores = lax.axis_size("dp"), lax.axis_size("row")
    pairs = [
        (d * cores + r, (d ^ masks[r]) * cores + r) for d in range(count) for r in range(cores)
    ]
    return lax.ppermute(value, ("dp", "row"), pairs)


FIRST, SECOND = (1, 2), (2, 1)


def far_mask(k):
    mask = 4 * (k & 1) + 8 * (k >> 1)
    return (mask, mask)


def add(*terms):
    total = terms[0].astype(F32)
    for term in terms[1:]:
        total = total + term.astype(F32)
    return total


def share(keep, send):
    half = SLABS // 4
    got = exchange(send, FIRST)
    low = add(keep[:half], got[:half]).astype(BF16)
    high = add(keep[half:], got[half:]).astype(BF16)
    quarter = add(low, exchange(high, SECOND)).astype(BF16)
    far = [exchange(quarter[k], far_mask(k)) for k in (1, 2, 3)]
    own = add(quarter[0], *far)
    bit = 16
    while bit < lax.axis_size("dp"):
        own = own + exchange(own, (bit, bit))
        bit *= 2
    own = own.astype(BF16)
    first = jnp.stack([own] + [exchange(own, far_mask(k)) for k in (1, 2, 3)])
    second = exchange(first, SECOND)
    eight = jnp.concatenate([first, second])
    third = exchange(eight, FIRST)
    return eight, third


def spread(ids, parts, outs, folded, name):
    return call(
        functools.partial(spread_kernel, folded, len(parts)), name, 1, (ids,) + tuple(parts), outs
    )


def all_sums(value):
    return lax.all_to_all(value, "dp", 0, 0, tiled=False)


def shards(
    frames,
    enc_w1,
    enc_gain1,
    enc_bias1,
    enc_w2,
    enc_gain2,
    enc_bias2,
    att_w1,
    att_gain,
    att_bias,
    att_w,
    dec_w1,
    dec_gain1,
    dec_bias1,
    dec_w2,
    dec_gain2,
    dec_bias2,
    labels,
    pool_index,
    out_grad,
):
    band_rows, width, in_chan = frames.shape[1:]
    chans = enc_w1.shape[3]
    half = dec_w1.shape[2]
    height = 2 * pool_index.shape[1]
    pixels = height * width
    band = band_rows * width
    tasks = att_w.shape[0]
    n_dp = lax.axis_size("dp")
    count = float(pixels * n_dp)
    core = lax.axis_index("row")
    chip = lax.axis_index("dp")
    bit_x, bit_y = chip & 1, (chip >> 1) & 1
    place = (
        8 * jnp.where(core == 0, bit_x, bit_y)
        + 4 * jnp.where(core == 0, bit_y, bit_x)
        + ((chip >> 2) & 3)
    )
    ids = jnp.stack([core, place]).astype(jnp.int32)

    own_bands = frames.reshape(2, band, in_chan)
    far_bands = swap_cores(own_bands)
    d1_own = dec_w1.reshape(3, 3 * half, chans)
    d2_own = dec_w2.reshape(3, 3 * half, chans)
    d1_far = swap_cores(d1_own)
    d2_far = swap_cores(d2_own)
    params_own = jnp.stack([dec_gain1, dec_bias1, dec_gain2, dec_bias2])
    params_far = swap_cores(params_own)
    params = jnp.where(
        core == 0,
        jnp.concatenate([params_own, params_far], axis=1),
        jnp.concatenate([params_far, params_own], axis=1),
    )
    og_own = lax.dynamic_index_in_dim(out_grad, core, 1, keepdims=False)
    og_far = swap_cores(lax.dynamic_index_in_dim(out_grad, 1 - core, 1, keepdims=False))
    index = lax.dynamic_index_in_dim(pool_index, core, 0, keepdims=False)
    index = jnp.repeat(jnp.repeat(index, 2, axis=0), 2, axis=1)
    cell = 2 * (jnp.arange(height)[:, None] % 2) + jnp.arange(width)[None, :] % 2
    mask = (index == cell).astype(F32).reshape(pixels, 1)
    e1 = enc_w1.reshape(3, 3 * in_chan, chans)
    e2 = enc_w2.reshape(3, 3 * chans, chans)

    full = arr((pixels, chans))
    full_low = arr((pixels, chans), BF16)
    part_low = arr((pixels, half), BF16)
    two = arr((n_dp, 2, chans))
    four = arr((n_dp, 4, chans))
    flat = pltpu.VMEM((pixels, chans), F32)
    buf = pltpu.VMEM((pixels + 2 * width, 3 * chans), BF16)
    work = 2 * pixels * 9 * chans * chans

    pre1, sums = call(
        functools.partial(enc_one_kernel, width), "enc_one", 1, (ids, own_bands, far_bands, e1),
        (full, two),
        (pltpu.VMEM((pixels, in_chan), F32), pltpu.VMEM((pixels + 2 * width, 3 * in_chan), BF16)), work // 2,
    )
    st1 = all_sums(sums)
    hidden1, pre2, att_pre, sums = call(
        functools.partial(enc_two_kernel, width, count), "enc_two", 2,
        (ids, labels, st1, pre1, enc_gain1, enc_bias1, e2, att_w1), (full_low, full, full, four), (buf,), work,
    )
    st2 = all_sums(sums)
    hidden1_far = swap_cores(hidden1)
    att_hidden, shared, gate, pre3, sums, up_own, up_send = call(
        functools.partial(dec_one_kernel, width, count), "dec_one", 2,
        (ids, labels, st2, pre2, att_pre, enc_gain2, enc_bias2, att_gain, att_bias, att_w, mask, d1_own, d1_far),
        (full_low, full, full, full, two, part_low, part_low), (flat, buf), work,
    )
    st3 = all_sums(sums)
    att_hidden_far, up_far = swap_cores(att_hidden), swap_cores(up_send)
    pre4, sums, hidden3_own, hidden3_send = call(
        functools.partial(dec_two_kernel, width, count), "dec_two", 1,
        (ids, st3, pre3, params, d2_own, d2_far), (full, two, part_low, part_low), (flat, buf), work,
    )
    st4 = all_sums(sums)
    hidden3_far = swap_cores(hidden3_send)
    turned = arr((half, pixels), BF16)
    dact4, sums, dec_own, dec_send = call(
        functools.partial(top_kernel, count), "top", 1, (ids, st4, pre4, params, og_own, og_far),
        (full, two, turned, turned), (flat, flat),
    )
    st4b = all_sums(sums)
    dec_far = swap_cores(dec_send)
    dz4, dact3, sums, tot4 = call(
        functools.partial(dec_two_back_kernel, width, count), "dec_two_back", 1,
        (ids, st4, st4b, pre4, dact4, params, d2_own, d2_far, st3, pre3),
        (full_low, full, two, arr((2, chans))), (flat, buf), work,
    )
    dz4_far = swap_cores(dz4)
    slab = half // SLABS
    tmp = pltpu.VMEM((2, chans, pixels), BF16)
    tmp_four = pltpu.VMEM((4, chans, pixels), BF16)
    bufs = pltpu.VMEM((2, pixels + 2 * width, 3 * chans), BF16)
    bufs_half = pltpu.VMEM((2, pixels + 2 * width, 3 * half), BF16)
    turned_half = pltpu.VMEM((2, half, pixels), BF16)
    turned_full = pltpu.VMEM((2, chans, pixels), BF16)

    def slabs(rows, lanes):
        return [arr((SLABS // 2, rows, lanes), BF16)] * 2

    g_dec2 = call(
        functools.partial(grad_dec_two_kernel, width), "grad_dec_two", 1,
        (ids, hidden3_own, hidden3_far, dz4, dz4_far), slabs(9 * slab, chans), (tmp, turned_half, bufs), work,
    )
    sum_dec2 = share(*g_dec2)
    st3b = all_sums(sums)
    dz3, dlog_own, dlog_send, datt, dact2, sums, tot3 = call(
        functools.partial(dec_one_back_kernel, width, count), "dec_one_back", 2,
        (ids, labels, st3, st3b, pre3, dact3, params, d1_own, d1_far, mask, gate, shared, att_w,
         st2, att_pre, pre2, att_gain, att_bias, enc_gain2, enc_bias2),
        (full_low, part_low, part_low, full, full, four, arr((2, chans))), (flat, flat, buf), work,
    )
    dz3_far, dlog_far = swap_cores(dz3), swap_cores(dlog_send)
    att_slab = chans // SLABS
    g_dec1 = call(
        functools.partial(grad_dec_one_kernel, width, tasks), "grad_dec_one", 2,
        (ids, labels, up_own, up_far, dz3, dz3_far, att_hidden, att_hidden_far, dlog_own, dlog_far),
        slabs(9 * slab + tasks * att_slab // 2, chans), (tmp_four, turned_half, turned_full, bufs), work,
    )
    sum_dec1 = share(*g_dec1)
    st2b = all_sums(sums)
    da_own, da_send, dz2_own, dz2_send, dact1, sums, tot2 = call(
        functools.partial(enc_two_back_kernel, width, count), "enc_two_back", 2,
        (ids, labels, st2, st2b, att_pre, datt, att_gain, pre2, dact2, enc_gain2, att_w1, e2,
         st1, pre1, enc_gain1, enc_bias1),
        (part_low, part_low, part_low, part_low, full, two, arr((4, chans))), (flat, flat, buf), work,
    )
    da_far, dz2_far = swap_cores(da_send), swap_cores(dz2_send)
    g_enc2 = call(
        functools.partial(grad_enc_two_kernel, width, tasks), "grad_enc_two", 2,
        (ids, labels, hidden1, hidden1_far, dz2_own, dz2_far, da_own, da_far),
        slabs((9 + tasks) * att_slab, half), (tmp, turned_full, bufs_half), work,
    )
    sum_enc2 = share(*g_enc2)
    st1b = all_sums(sums)
    band_grad = arr((band, in_chan))
    dz1_own, dz1_send, fg_own, fg_send, tot1 = call(
        functools.partial(enc_one_back_kernel, width, count), "enc_one_back", 1,
        (ids, st1, st1b, pre1, dact1, enc_gain1, e1),
        (part_low, part_low, band_grad, band_grad, arr((2, chans))),
        (flat, pltpu.VMEM((pixels, in_chan), F32), buf), work // 2,
    )
    dz1_far = swap_cores(dz1_send)
    in_slab = in_chan // SLABS
    g_enc1 = call(
        functools.partial(grad_enc_one_kernel, width), "grad_enc_one", 1,
        (ids, own_bands, far_bands, dz1_own, dz1_far), slabs(9 * in_slab, half),
        (pltpu.VMEM((2, pixels, in_chan), F32), tmp, pltpu.VMEM((2, in_chan, pixels), BF16), bufs_half), work // 2,
    )
    sum_enc1 = share(*g_enc1)

    (dec2_grad,) = spread(ids, sum_dec2, (arr((9, half, chans)),), False, "spread_dec_two")
    dec1_grad, att_grad = spread(
        ids, sum_dec1, (arr((9, half, chans)), arr((tasks, chans, half))), True, "spread_dec_one"
    )
    enc2_grad, att1_grad = spread(
        ids, sum_enc2, (arr((9, chans, half)), arr((tasks, chans, half))), False, "spread_enc_two"
    )
    (enc1_grad,) = spread(ids, sum_enc1, (arr((9, in_chan, half)),), False, "spread_enc_one")

    fg_far = swap_cores(fg_send)
    bands = jnp.where(core == 0, jnp.stack([fg_own, fg_far]), jnp.stack([fg_far, fg_own]))
    decoded = jnp.where(
        core == 0, jnp.stack([dec_own, dec_far], axis=1), jnp.stack([dec_far, dec_own], axis=1)
    )
    totals = jnp.concatenate([tot1, tot2, tot3, tot4])
    totals = totals + swap_cores(totals)
    dec_totals = lax.dynamic_slice_in_dim(totals[6:10], core * half, half, 1)
    return (
        decoded,
        bands.reshape(2, band_rows, width, in_chan),
        enc1_grad.reshape(3, 3, in_chan, half),
        totals[1],
        totals[0],
        enc2_grad.reshape(3, 3, chans, half),
        totals[3],
        totals[2],
        att1_grad,
        totals[5],
        totals[4],
        att_grad,
        dec1_grad.reshape(3, 3, half, chans),
        dec_totals[1],
        dec_totals[0],
        dec2_grad.reshape(3, 3, half, chans),
        dec_totals[3],
        dec_totals[2],
    )


def solution(mesh):
    return jax.shard_map(
        shards,
        mesh=mesh,
        in_specs=(
            P("dp", "row", None, None),
            P(),
            P(),
            P(),
            P(),
            P(),
            P(),
            P(),
            P(),
            P(),
            P(),
            P(None, None, "row", None),
            P("row"),
            P("row"),
            P(None, None, "row", None),
            P("row"),
            P("row"),
            P("dp"),
            P("dp", None, None),
            P("row", "dp", None),
        ),
        out_specs=(
            P("row", "dp", None),
            P("dp", "row", None, None),
            P(None, None, None, "row"),
            P(),
            P(),
            P(None, None, None, "row"),
            P(),
            P(),
            P(None, None, "row"),
            P(),
            P(),
            P(None, None, "row"),
            P(None, None, "row", None),
            P("row"),
            P("row"),
            P(None, None, "row", None),
            P("row"),
            P("row"),
        ),
        check_vma=False,
    )
```

```python
import functools
import math

import jax
import jax.numpy as jnp
from jax import lax
from jax.experimental import pallas as pl
from jax.experimental.pallas import tpu as pltpu
from jax.sharding import PartitionSpec as P

EPS = 1e-05
F32 = jnp.float32
BF16 = jnp.bfloat16
SLABS = 16
MIB = 2**20


def dot(left, right):
    return jnp.dot(left, right, preferred_element_type=F32)


def dot_nt(left, right):
    return lax.dot_general(left, right, (((1,), (1,)), ((), ())), preferred_element_type=F32)


def slope(act):
    sig = jax.nn.sigmoid(act)
    return sig * (1.0 + act * (1.0 - sig))


def silu(act):
    return act * jax.nn.sigmoid(act)


def clear_rims(buf, width):
    rows, lanes = buf.shape
    rim = jnp.zeros((width, lanes), BF16)
    buf[0:width, :] = rim
    buf[rows - width : rows, :] = rim


def fill(buf, value, width, lane, step):
    pixels, chans = value.shape
    col = lax.broadcasted_iota(jnp.int32, (pixels, 1), 0) & (width - 1)
    before = jnp.where(col == 0, 0.0, pltpu.roll(value, 1, 0))
    after = jnp.where(col == width - 1, 0.0, pltpu.roll(value, pixels - 1, 0))
    for at, part in enumerate((before, value, after)):
        start = lane + at * step
        buf[width : width + pixels, start : start + chans] = part.astype(BF16)


def conv(buf, weights, pixels, width, apart=None):
    total, lane = None, 0
    for ref in weights:
        depth = ref.shape[1]
        for i in range(3):
            taps = apart[0] if apart is not None and i == 0 else ref[i]
            term = dot(buf[i * width : i * width + pixels, lane : lane + depth], taps)
            total = term if total is None else total + term
        lane += depth
    return total


def shifted(buf, i, j, pixels, width, chans):
    return buf[(2 - i) * width : (2 - i) * width + pixels, (2 - j) * chans : (3 - j) * chans]


def conv_back(buf, ref, pixels, width):
    chans = ref.shape[2]
    depth = ref.shape[1] // 3
    total = None
    for i in range(3):
        for j in range(3):
            term = dot_nt(
                shifted(buf, i, j, pixels, width, chans), ref[i, j * depth : (j + 1) * depth, :]
            )
            total = term if total is None else total + term
    return total


def put_sums(ref, terms):
    for at, term in enumerate(terms):
        row = jnp.sum(term, axis=0, keepdims=True)
        ref[:, at : at + 1, :] = jnp.broadcast_to(row[None], (ref.shape[0], 1, ref.shape[2]))
    ref.flush()


def gather_sums(ref):
    return jnp.sum(ref[...], axis=0)


def moments(ref, at, count):
    total = gather_sums(ref)
    mean = total[at : at + 1] / count
    square = total[at + 1 : at + 2] / count
    return mean, lax.rsqrt(square - mean * mean + EPS)


def normed(pre, mom):
    return (pre.astype(F32) - mom[0]) * mom[1]


def norm_back(grad, pre, mom, gain, total, at, count):
    xhat = normed(pre, mom)
    return (gain * mom[1]) * (
        grad.astype(F32) - total[at : at + 1] / count - xhat * (total[at + 1 : at + 2] / count)
    )


def row_of(ref):
    return ref[...].reshape(1, -1)


def half_at(ids, other, half):
    side = ids[0]
    if other:
        side = 1 - side
    return pl.ds(pl.multiple_of(side * half, half), half)


def enc_one_kernel(width, ids, own, far, w_ref, pre_ref, sum_ref, flat, buf):
    pixels, chans = flat.shape
    band = pixels // 2
    side = ids[0]
    flat[half_at(ids, False, band), :] = own[side].astype(F32)
    flat[half_at(ids, True, band), :] = far[side].astype(F32)
    clear_rims(buf, width)
    fill(buf, flat[...], width, 0, chans)
    pre = conv(buf, (w_ref,), pixels, width)
    pre_ref[...] = pre
    pre_ref.flush()
    put_sums(sum_ref, (pre, pre * pre))


def enc_two_kernel(
    width, count, ids, labels, st1, pre1, gain1, bias1, aw_ref, w_first, w_ref, hid_ref, pre2_ref, att_ref, sum_ref, buf
):
    pixels, chans = pre1.shape
    mom = moments(st1, 0, count)
    hidden = silu(normed(pre1[...], mom) * row_of(gain1) + row_of(bias1))
    clear_rims(buf, width)
    fill(buf, hidden, width, 0, chans)
    hid_ref[...] = hidden.astype(BF16)
    hid_ref.flush()
    att = dot(hid_ref[...], aw_ref[...])
    att_ref[...] = att
    att_ref.flush()
    pre = conv(buf, (w_ref,), pixels, width, w_first)
    pre2_ref[...] = pre
    pre2_ref.flush()
    put_sums(sum_ref, (pre, pre * pre, att, att * att))


def dec_one_kernel(
    width, count, ids, labels, st2, pre2, att_pre, gain2, bias2, gain_a, bias_a, aw_ref, mask, w_own, w_far,
    hid_ref, shared_ref, gate_ref, pre3_ref, sum_ref, keep_ref, send_ref, flat, buf,
):
    pixels, chans = pre2.shape
    half = chans // 2
    shared = silu(normed(pre2[...], moments(st2, 0, count)) * row_of(gain2) + row_of(bias2))
    shared_ref[...] = shared
    shared_ref.flush()
    hid = silu(normed(att_pre[...], moments(st2, 2, count)) * row_of(gain_a) + row_of(bias_a))
    hid_ref[...] = hid.astype(BF16)
    hid_ref.flush()
    gate = jax.nn.sigmoid(dot(hid_ref[...], aw_ref[...]))
    gate_ref[...] = gate
    gate_ref.flush()
    flat[...] = gate * shared * mask[...]
    clear_rims(buf, width)
    for other, ref in ((False, keep_ref), (True, send_ref)):
        part = flat[:, half_at(ids, other, half)]
        fill(buf, part, width, 3 * half * other, half)
        ref[...] = part.astype(BF16)
        ref.flush()
    pre = conv(buf, (w_own, w_far), pixels, width)
    pre3_ref[...] = pre
    pre3_ref.flush()
    put_sums(sum_ref, (pre, pre * pre))


def dec_two_kernel(
    width, count, ids, st3, pre3, params, w_own, w_far, pre4_ref, sum_ref, keep_ref, send_ref, flat, buf
):
    pixels, chans = pre3.shape
    half = chans // 2
    flat[...] = silu(normed(pre3[...], moments(st3, 0, count)) * params[0:1, :] + params[1:2, :])
    clear_rims(buf, width)
    for other, ref in ((False, keep_ref), (True, send_ref)):
        part = flat[:, half_at(ids, other, half)]
        fill(buf, part, width, 3 * half * other, half)
        ref[...] = part.astype(BF16)
        ref.flush()
    pre = conv(buf, (w_own, w_far), pixels, width)
    pre4_ref[...] = pre
    pre4_ref.flush()
    put_sums(sum_ref, (pre, pre * pre))


def top_kernel(count, ids, st4, pre4, params, og_own, og_far, dact_ref, sum_ref, keep_ref, send_ref, cot, out):
    pixels, chans = pre4.shape
    half = chans // 2
    xhat = normed(pre4[...], moments(st4, 0, count))
    act = xhat * params[2:3, :] + params[3:4, :]
    sig = jax.nn.sigmoid(act)
    out[...] = act * sig
    cot[:, half_at(ids, False, half)] = og_own[...].astype(F32).T
    cot[:, half_at(ids, True, half)] = og_far[...].astype(F32).T
    dact = cot[...] * (sig * (1.0 + act * (1.0 - sig)))
    dact_ref[...] = dact
    dact_ref.flush()
    put_sums(sum_ref, (dact, dact * xhat))
    for other, ref in ((False, keep_ref), (True, send_ref)):
        ref[...] = out[:, half_at(ids, other, half)].T.astype(BF16)


def dec_two_back_kernel(
    width, count, ids, st4, st4b, pre4, dact4, params, w_own, w_far, st3, pre3,
    dz_ref, dact_ref, sum_ref, tot_ref, flat, buf,
):
    pixels, chans = pre4.shape
    half = chans // 2
    total = gather_sums(st4b)
    tot_ref[...] = total
    tot_ref.flush()
    dz = norm_back(dact4[...], pre4[...], moments(st4, 0, count), params[2:3, :], total, 0, count)
    dz_ref[...] = dz.astype(BF16)
    dz_ref.flush()
    clear_rims(buf, width)
    fill(buf, dz, width, 0, chans)
    for other, ref in ((False, w_own), (True, w_far)):
        flat[:, half_at(ids, other, half)] = conv_back(buf, ref, pixels, width)
    xhat = normed(pre3[...], moments(st3, 0, count))
    dact = flat[...] * slope(xhat * params[0:1, :] + params[1:2, :])
    dact_ref[...] = dact
    dact_ref.flush()
    put_sums(sum_ref, (dact, dact * xhat))


def dec_one_back_kernel(
    width, count, ids, labels, st3, st3b, pre3, dact3, params, w_own, w_far, mask, gate_ref, shared_ref, aw_ref,
    st2, att_pre, pre2, gain_a, bias_a, gain2, bias2,
    dz_ref, dlog_keep, dlog_send, datt_ref, dact2_ref, sum_ref, tot_ref, flat, dlog, buf,
):
    pixels, chans = pre3.shape
    half = chans // 2
    total = gather_sums(st3b)
    tot_ref[...] = total
    tot_ref.flush()
    dz = norm_back(dact3[...], pre3[...], moments(st3, 0, count), params[0:1, :], total, 0, count)
    dz_ref[...] = dz.astype(BF16)
    dz_ref.flush()
    clear_rims(buf, width)
    fill(buf, dz, width, 0, chans)
    for other, ref in ((False, w_own), (True, w_far)):
        flat[:, half_at(ids, other, half)] = conv_back(buf, ref, pixels, width)
    grad = (flat[...] * mask[...]).astype(BF16).astype(F32)
    gate = gate_ref[...].astype(F32)
    dlog[...] = grad * shared_ref[...].astype(F32) * gate * (1.0 - gate)
    for other, ref in ((False, dlog_keep), (True, dlog_send)):
        ref[...] = dlog[:, half_at(ids, other, half)].astype(BF16)
        ref.flush()
    dhid = dot_nt(dlog[...].astype(BF16), aw_ref[...])
    att_hat = normed(att_pre[...], moments(st2, 2, count))
    datt = dhid * slope(att_hat * row_of(gain_a) + row_of(bias_a))
    datt_ref[...] = datt
    datt_ref.flush()
    xhat2 = normed(pre2[...], moments(st2, 0, count))
    dact2 = grad * gate * slope(xhat2 * row_of(gain2) + row_of(bias2))
    dact2_ref[...] = dact2
    dact2_ref.flush()
    put_sums(sum_ref, (dact2, dact2 * xhat2, datt, datt * att_hat))


def enc_two_back_kernel(
    width, count, ids, labels, st2, st2b, att_pre, datt_ref, gain_a, pre2, dact2, gain2, aw_ref, w_ref,
    st1, pre1, gain1, bias1,
    datt_keep, datt_send, dz_keep, dz_send, dact_ref, sum_ref, tot_ref, flat, datt, buf,
):
    pixels, chans = pre2.shape
    half = chans // 2
    total = gather_sums(st2b)
    tot_ref[...] = total
    tot_ref.flush()
    dz = norm_back(dact2[...], pre2[...], moments(st2, 0, count), row_of(gain2), total, 0, count)
    flat[...] = dz
    for other, ref in ((False, dz_keep), (True, dz_send)):
        ref[...] = flat[:, half_at(ids, other, half)].astype(BF16)
        ref.flush()
    clear_rims(buf, width)
    fill(buf, dz, width, 0, chans)
    datt[...] = norm_back(
        datt_ref[...], att_pre[...], moments(st2, 2, count), row_of(gain_a), total, 2, count
    )
    for other, ref in ((False, datt_keep), (True, datt_send)):
        ref[...] = datt[:, half_at(ids, other, half)].astype(BF16)
        ref.flush()
    dhid = dot_nt(datt[...].astype(BF16), aw_ref[...])
    dhid = dhid + conv_back(buf, w_ref, pixels, width)
    xhat = normed(pre1[...], moments(st1, 0, count))
    dact = dhid * slope(xhat * row_of(gain1) + row_of(bias1))
    dact_ref[...] = dact
    dact_ref.flush()
    put_sums(sum_ref, (dact, dact * xhat))


def enc_one_back_kernel(
    width, count, ids, st1, st1b, pre1, dact1, gain1, w_ref, dz_keep, dz_send, fg_keep, fg_send, tot_ref, flat, back, buf
):
    pixels, chans = pre1.shape
    half = chans // 2
    total = gather_sums(st1b)
    tot_ref[...] = total
    tot_ref.flush()
    dz = norm_back(dact1[...], pre1[...], moments(st1, 0, count), row_of(gain1), total, 0, count)
    flat[...] = dz
    for other, ref in ((False, dz_keep), (True, dz_send)):
        ref[...] = flat[:, half_at(ids, other, half)].astype(BF16)
        ref.flush()
    clear_rims(buf, width)
    fill(buf, dz, width, 0, chans)
    back[...] = conv_back(buf, w_ref, pixels, width)
    for other, ref in ((False, fg_keep), (True, fg_send)):
        ref[...] = back[half_at(ids, other, pixels // 2), :]


def lay_rows(ids, value, at, tmp, slot, turned):
    rows = turned.shape[1]
    part = rows // SLABS
    tmp[slot, 0:rows, :] = value.astype(F32).T.astype(BF16)
    for t in range(SLABS):
        start = pl.multiple_of((ids[1] ^ t) * part, part)
        turned[at, t * part : (t + 1) * part, :] = tmp[slot, pl.ds(start, part), :]


def store_slabs(keep_ref, send_ref, row, part, lane, value):
    low = value.astype(BF16)
    mid = SLABS // 2
    lanes = value.shape[1]
    for t in range(SLABS):
        ref, at = (keep_ref, t) if t < mid else (send_ref, t - mid)
        ref[at, row : row + part, lane : lane + lanes] = low[t * part : (t + 1) * part]


def conv_weights(ids, width, values, grads, keep_ref, send_ref, tmp, turned, bufs):
    pixels, chans = grads[0].shape
    part = turned.shape[1] // SLABS
    for at in range(2):
        lay_rows(ids, values[at][...], at, tmp, at, turned)
        clear_rims(bufs.at[at], width)
        fill(bufs.at[at], grads[at][...].astype(F32), width, 0, chans)
    for i in range(3):
        for j in range(3):
            total = dot(turned[0], shifted(bufs.at[0], i, j, pixels, width, chans))
            total = total + dot(turned[1], shifted(bufs.at[1], i, j, pixels, width, chans))
            store_slabs(keep_ref, send_ref, (3 * i + j) * part, part, 0, total)


def task_weights(ids, labels, tasks, values, grads, tmp, turned):
    for at in range(2):
        lay_rows(ids, values[at][...], at, tmp, 2 + at, turned)
    side = ids[0]
    near = dot(turned[0], grads[0][...])
    far = dot(turned[1], grads[1][...])
    sums = []
    for task in range(tasks):
        take_near = (labels[side] == task).astype(F32)
        take_far = (labels[1 - side] == task).astype(F32)
        sums.append(near * take_near + far * take_far)
    return sums


def grad_dec_two_kernel(width, ids, v_own, v_far, dz_own, dz_far, keep_ref, send_ref, tmp, turned, bufs):
    conv_weights(ids, width, (v_own, v_far), (dz_own, dz_far), keep_ref, send_ref, tmp, turned, bufs)


def grad_dec_one_kernel(
    width, tasks, ids, labels, v_own, v_far, dz_own, dz_far, h_own, h_far, dl_own, dl_far,
    keep_ref, send_ref, tmp, turned, turned_att, bufs,
):
    conv_weights(ids, width, (v_own, v_far), (dz_own, dz_far), keep_ref, send_ref, tmp, turned, bufs)
    sums = task_weights(
        ids, labels, tasks, (h_own, h_far), (dl_own, dl_far), tmp, turned_att
    )
    base = 9 * (turned.shape[1] // SLABS)
    part = turned_att.shape[1] // SLABS
    lanes = dl_own.shape[1]
    fold = tasks * part // 2
    mid = SLABS // 2
    for task, total in enumerate(sums):
        low = total.astype(BF16)
        for t in range(SLABS):
            ref, at = (keep_ref, t) if t < mid else (send_ref, t - mid)
            for piece in range(0, part, 16):
                row = task * part + piece
                side, line = row // fold, row % fold
                ref[at, base + line : base + line + 16, side * lanes : (side + 1) * lanes] = low[
                    t * part + piece : t * part + piece + 16
                ]


def grad_enc_two_kernel(
    width, tasks, ids, labels, h_own, h_far, dz_own, dz_far, da_own, da_far, keep_ref, send_ref, tmp, turned, bufs
):
    values = (h_own, h_far)
    conv_weights(ids, width, values, (dz_own, dz_far), keep_ref, send_ref, tmp, turned, bufs)
    part = turned.shape[1] // SLABS
    side = ids[0]
    near = dot(turned[0], da_own[...])
    far = dot(turned[1], da_far[...])
    for task in range(tasks):
        take_near = (labels[side] == task).astype(F32)
        take_far = (labels[1 - side] == task).astype(F32)
        total = near * take_near + far * take_far
        store_slabs(keep_ref, send_ref, (9 + task) * part, part, 0, total)


def grad_enc_one_kernel(width, ids, own, far, dz_own, dz_far, keep_ref, send_ref, flat, tmp, turned, bufs):
    band = flat.shape[1] // 2
    side = ids[0]
    values = []
    for at, frame in enumerate((side, 1 - side)):
        flat[at, half_at(ids, False, band), :] = own[frame].astype(F32)
        flat[at, half_at(ids, True, band), :] = far[frame].astype(F32)
        values.append(flat[at])
    conv_weights(ids, width, values, (dz_own, dz_far), keep_ref, send_ref, tmp, turned, bufs)


def slab_of(parts, t):
    for ref in parts:
        if t < ref.shape[0]:
            return ref, t
        t -= ref.shape[0]
    raise IndexError(t)


def spread_kernel(folded, n_parts, ids, *refs):
    parts, outs = refs[:n_parts], refs[n_parts:]
    taps, rows, lanes = outs[0].shape
    part = rows // SLABS
    for tap in range(taps):
        for t in range(SLABS):
            ref, at = slab_of(parts, t)
            place = pl.ds(pl.multiple_of((ids[1] ^ t) * part, part), part)
            outs[0][tap, place, :] = ref[at, tap * part : (tap + 1) * part, :].astype(F32)
        outs[0].flush(tap)
    if len(outs) == 1:
        return
    tasks, more, narrow = outs[1].shape
    step = more // SLABS
    base = taps * part
    fold = tasks * step // 2
    for task in range(tasks):
        for t in range(SLABS):
            ref, at = slab_of(parts, t)
            start = pl.multiple_of((ids[1] ^ t) * step, step)
            if not folded:
                outs[1][task, pl.ds(start, step), :] = ref[
                    at, base + task * step : base + (task + 1) * step, :
                ].astype(F32)
                continue
            for piece in range(0, step, 16):
                row = task * step + piece
                side, line = row // fold, row % fold
                outs[1][task, pl.ds(start + piece, 16), :] = ref[
                    at, base + line : base + line + 16, side * narrow : (side + 1) * narrow
                ].astype(F32)
        outs[1].flush(task)


def arr(shape, kind=F32):
    return jax.ShapeDtypeStruct(shape, kind)


class Source:
    def __init__(self, pieces, buf):
        self.pieces, self.buf, self.shape = pieces, buf, buf.shape
        self.waiting = [True] * len(pieces)

    def start(self):
        for piece, wanted in zip(self.pieces, self.waiting, strict=True):
            if wanted:
                piece.start()

    def __getitem__(self, at):
        first = at[0] if isinstance(at, tuple) else at
        cut_one = len(self.pieces) > 1 and isinstance(first, int)
        for k in [first] if cut_one else range(len(self.pieces)):
            if self.waiting[k]:
                self.pieces[k].wait()
                self.waiting[k] = False
        return self.buf[at]

    def finish(self):
        for k, piece in enumerate(self.pieces):
            if self.waiting[k]:
                piece.wait()


class Target:
    def __init__(self, pieces, buf):
        self.pieces, self.buf, self.shape = pieces, buf, buf.shape
        self.sent = [False] * len(pieces)

    def __setitem__(self, at, value):
        self.buf[at] = value.astype(self.buf.dtype)

    def __getitem__(self, at):
        return self.buf[at]

    def flush(self, k=0):
        if k < len(self.pieces) and not self.sent[k]:
            self.pieces[k].start()
            self.sent[k] = True

    def finish(self):
        for k, piece in enumerate(self.pieces):
            self.flush(k)
        for piece in self.pieces:
            piece.wait()


def near(array):
    return array, "near"


def far(array):
    return array, "far"


def cut(array):
    return array, "cut"


def rest(array):
    return array, "rest"


def pick(array):
    return array, "pick"


def both(array):
    return array, "both"


def held(array, kind):
    return pltpu.with_memory_space_constraint(array, pltpu.VMEM if kind == "near" else pltpu.HBM)


def call(body, name, scalars, args, outs, scratch=(), flops=0):
    smem, vmem = pl.BlockSpec(memory_space=pltpu.SMEM), pl.BlockSpec(memory_space=pltpu.VMEM)
    hbm = pl.BlockSpec(memory_space=pltpu.HBM)
    moved = sum(a.size * a.dtype.itemsize for a, _ in list(args) + list(outs))
    arrays = list(args) + list(outs)
    pieces = [a.shape[0] if kind in ("cut", "rest") else 1 for a, kind in arrays]
    kinds = [kind for _, kind in arrays]
    bufs = [
        pltpu.VMEM(a.shape[1:] if kind == "pick" else a.shape, a.dtype)
        for a, kind in arrays
        if kind not in ("near", "both")
    ]
    places, shapes = [], []
    for a, kind in outs:
        if kind in ("near", "both"):
            places.append(vmem)
            shapes.append(pltpu.VMEM(a.shape, a.dtype))
        if kind != "near":
            places.append(hbm)
            shapes.append(pltpu.HBM(a.shape, a.dtype))
    held_bytes = sum(jnp.dtype(b.dtype).itemsize * math.prod(b.shape) for b in bufs + list(scratch))
    n_sems = max(1, sum(p for p, kind in zip(pieces, kinds, strict=True) if kind != "near"))

    def kernel(*refs):
        refs = list(refs)

        def take(count):
            taken = refs[:count]
            del refs[:count]
            return taken

        given = take(len(scalars))
        ins, results = take(len(args)), take(len(shapes))
        local, (sems,) = take(len(bufs)), take(1)
        items, slot = [], 0
        for k, kind in enumerate(kinds):
            is_out = k >= len(args)
            if kind == "near":
                items.append(Target((), results.pop(0)) if is_out else ins[k])
                continue
            inside = results.pop(0) if kind == "both" else local.pop(0)
            outside = results.pop(0) if is_out else ins[k]
            if kind == "pick":
                outside = outside.at[given[1][given[0][0]]]
            copies = []
            for piece in range(pieces[k]):
                apart = kind in ("cut", "rest")
                ends = (outside.at[piece], inside.at[piece]) if apart else (outside, inside)
                left, right = reversed(ends) if is_out else ends
                copies.append(pltpu.make_async_copy(left, right, sems.at[slot]))
                slot += 1
            items.append((Target if is_out else Source)(copies, inside))
            if kind == "rest":
                items[-1].waiting[0] = False
        for item in items:
            if isinstance(item, Source):
                item.start()
        body(*given, *items, *refs)
        for item in items:
            if isinstance(item, (Source, Target)):
                item.finish()

    return pl.pallas_call(
        kernel,
        out_shape=shapes,
        in_specs=[smem] * len(scalars) + [vmem if kind == "near" else hbm for _, kind in args],
        out_specs=places,
        scratch_shapes=bufs + [pltpu.SemaphoreType.DMA((n_sems,))] + list(scratch),
        name=name,
        compiler_params=pltpu.CompilerParams(vmem_limit_bytes=held_bytes + 8 * MIB),
        cost_estimate=pl.CostEstimate(flops=flops, bytes_accessed=moved, transcendentals=0),
    )(*scalars, *[held(a, kind) for a, kind in args])


def fetch_kernel(source, target, sems):
    copies = [pltpu.make_async_copy(source.at[k], target.at[k], sems.at[k]) for k in range(target.shape[0])]
    for copy in copies:
        copy.start()
    for copy in copies:
        copy.wait()


def fetch(weight, count):
    shape = (count,) + weight.shape[1:]
    return pl.pallas_call(
        fetch_kernel,
        out_shape=pltpu.VMEM(shape, weight.dtype),
        in_specs=[pl.BlockSpec(memory_space=pltpu.HBM)],
        out_specs=pl.BlockSpec(memory_space=pltpu.VMEM),
        scratch_shapes=[pltpu.SemaphoreType.DMA((count,))],
        name="fetch",
        compiler_params=pltpu.CompilerParams(vmem_limit_bytes=MIB),
        cost_estimate=pl.CostEstimate(flops=0, bytes_accessed=4 * math.prod(shape), transcendentals=0),
    )(held(weight, "far"))


def swap_cores(value):
    return lax.ppermute(value, "row", [(0, 1), (1, 0)])


def exchange(value, masks):
    count, cores = lax.axis_size("dp"), lax.axis_size("row")
    pairs = [
        (d * cores + r, (d ^ masks[r]) * cores + r) for d in range(count) for r in range(cores)
    ]
    return lax.ppermute(value, ("dp", "row"), pairs)


FIRST, SECOND = (1, 2), (2, 1)


def far_mask(k):
    mask = 4 * (k & 1) + 8 * (k >> 1)
    return (mask, mask)


def add(*terms):
    total = terms[0].astype(F32)
    for term in terms[1:]:
        total = total + term.astype(F32)
    return total


def scatter_first(slabs):
    keep, send = slabs
    got = exchange(send, FIRST)
    half = SLABS // 4
    return add(keep[:half], got[:half]).astype(BF16), add(keep[half:], got[half:]).astype(BF16)


def scatter_second(parts):
    low, high = parts
    return add(low, exchange(high, SECOND)).astype(BF16)


def scatter_far(quarter):
    own = add(quarter[0], *[exchange(quarter[k], far_mask(k)) for k in (1, 2, 3)])
    bit = 16
    while bit < lax.axis_size("dp"):
        own = own + exchange(own, (bit, bit))
        bit *= 2
    return own.astype(BF16)


def gather_far(own):
    return jnp.stack([own] + [exchange(own, far_mask(k)) for k in (1, 2, 3)])


def gather_second(four):
    return jnp.concatenate([four, exchange(four, SECOND)])


def gather_first(eight):
    return eight, exchange(eight, FIRST)


def tie(*values):
    return lax.optimization_barrier(values)


def spread(ids, parts, outs, folded, name):
    return call(
        functools.partial(spread_kernel, folded, len(parts)), name, (ids,),
        [far(part) for part in parts], [cut(out) for out in outs],
    )


def all_sums(value):
    return lax.all_to_all(value, "dp", 0, 0, tiled=False)


def shards(
    frames,
    enc_w1,
    enc_gain1,
    enc_bias1,
    enc_w2,
    enc_gain2,
    enc_bias2,
    att_w1,
    att_gain,
    att_bias,
    att_w,
    dec_w1,
    dec_gain1,
    dec_bias1,
    dec_w2,
    dec_gain2,
    dec_bias2,
    labels,
    pool_index,
    out_grad,
):
    band_rows, width, in_chan = frames.shape[1:]
    chans = enc_w1.shape[3]
    half = dec_w1.shape[2]
    height = 2 * pool_index.shape[1]
    pixels = height * width
    band = band_rows * width
    tasks = att_w.shape[0]
    n_dp = lax.axis_size("dp")
    count = float(pixels * n_dp)
    core = lax.axis_index("row")
    chip = lax.axis_index("dp")
    bit_x, bit_y = chip & 1, (chip >> 1) & 1
    place = (
        8 * jnp.where(core == 0, bit_x, bit_y)
        + 4 * jnp.where(core == 0, bit_y, bit_x)
        + ((chip >> 2) & 3)
    )
    ids = jnp.stack([core, place]).astype(jnp.int32)

    own_bands = frames.reshape(2, band, in_chan)
    far_bands = swap_cores(own_bands)
    d1_own = dec_w1.reshape(3, 3 * half, chans)
    d2_own = dec_w2.reshape(3, 3 * half, chans)
    d1_far = swap_cores(d1_own)
    d2_far = swap_cores(d2_own)
    params_own = jnp.stack([dec_gain1, dec_bias1, dec_gain2, dec_bias2])
    params_far = swap_cores(params_own)
    params = jnp.where(
        core == 0,
        jnp.concatenate([params_own, params_far], axis=1),
        jnp.concatenate([params_far, params_own], axis=1),
    )
    og_own = lax.dynamic_index_in_dim(out_grad, core, 1, keepdims=False)
    og_far = swap_cores(lax.dynamic_index_in_dim(out_grad, 1 - core, 1, keepdims=False))
    index = lax.dynamic_index_in_dim(pool_index, core, 0, keepdims=False)
    index = jnp.repeat(jnp.repeat(index, 2, axis=0), 2, axis=1)
    cell = 2 * (jnp.arange(height)[:, None] % 2) + jnp.arange(width)[None, :] % 2
    mask = (index == cell).astype(F32).reshape(pixels, 1)
    e1 = enc_w1.reshape(3, 3 * in_chan, chans)
    e2 = enc_w2.reshape(3, 3 * chans, chans)

    full = arr((pixels, chans), BF16)
    part = arr((pixels, half), BF16)
    two = arr((n_dp, 2, chans))
    four = arr((n_dp, 4, chans))
    flat = pltpu.VMEM((pixels, chans), F32)
    buf = pltpu.VMEM((pixels + 2 * width, 3 * chans), BF16)
    work = 2 * pixels * 9 * chans * chans

    pre1, sums = call(
        functools.partial(enc_one_kernel, width), "enc_one", (ids,),
        [far(own_bands), far(far_bands), near(fetch(e1, 3))], [far(full), near(two)],
        (pltpu.VMEM((pixels, in_chan), F32), pltpu.VMEM((pixels + 2 * width, 3 * in_chan), BF16)), work // 2,
    )
    sums, w_near = tie(sums, e2)
    st1 = all_sums(sums)
    hidden1, pre2, att_pre, sums = call(
        functools.partial(enc_two_kernel, width, count), "enc_two", (ids, labels),
        [near(st1), far(pre1), near(enc_gain1), near(enc_bias1), pick(att_w1), near(fetch(w_near, 1)), rest(e2)],
        [far(full), far(full), far(full), near(four)], (buf,), work,
    )
    sums, w_own = tie(sums, d1_own)
    st2 = all_sums(sums)
    hidden1_far = swap_cores(hidden1)
    att_hidden, shared, gate, pre3, sums, up_own, up_send = call(
        functools.partial(dec_one_kernel, width, count), "dec_one", (ids, labels),
        [near(st2), far(pre2), far(att_pre), near(enc_gain2), near(enc_bias2), near(att_gain), near(att_bias),
         pick(att_w), near(mask), near(fetch(w_own, 3)), cut(d1_far)],
        [far(full), far(full), far(full), far(full), near(two), far(part), far(part)], (flat, buf), work,
    )
    sums, w_own = tie(sums, d2_own)
    st3 = all_sums(sums)
    att_hidden_far, up_far = swap_cores(att_hidden), swap_cores(up_send)
    pre4, sums, hidden3_own, hidden3_send = call(
        functools.partial(dec_two_kernel, width, count), "dec_two", (ids,),
        [near(st3), far(pre3), near(params), near(fetch(w_own, 3)), cut(d2_far)],
        [near(full), near(two), far(part), far(part)], (flat, buf), work,
    )
    st4 = all_sums(sums)
    hidden3_far = swap_cores(hidden3_send)
    turned = arr((half, pixels), BF16)
    dact4, sums, dec_own, dec_send = call(
        functools.partial(top_kernel, count), "top", (ids,),
        [near(st4), near(pre4), near(params), far(og_own), far(og_far)],
        [near(full), near(two), far(turned), far(turned)], (flat, flat),
    )
    st4b = all_sums(sums)
    dec_far = swap_cores(dec_send)
    dz4, dz4_out, dact3, sums, tot4 = call(
        functools.partial(dec_two_back_kernel, width, count), "dec_two_back", (ids,),
        [near(st4), near(st4b), near(pre4), near(dact4), near(params), cut(d2_own), cut(d2_far), near(st3),
         far(pre3)],
        [both(full), near(full), near(two), far(arr((2, chans)))], (flat, buf), work,
    )
    dz4_far = swap_cores(dz4_out)
    slab = half // SLABS
    tmp = pltpu.VMEM((2, chans, pixels), BF16)
    tmp_four = pltpu.VMEM((4, chans, pixels), BF16)
    bufs = pltpu.VMEM((2, pixels + 2 * width, 3 * chans), BF16)
    bufs_half = pltpu.VMEM((2, pixels + 2 * width, 3 * half), BF16)
    turned_half = pltpu.VMEM((2, half, pixels), BF16)
    turned_full = pltpu.VMEM((2, chans, pixels), BF16)

    def slabs(rows, lanes):
        return [far(arr((SLABS // 2, rows, lanes), BF16))] * 2

    g_dec2 = call(
        functools.partial(grad_dec_two_kernel, width), "grad_dec_two", (ids,),
        [far(hidden3_own), far(hidden3_far), near(dz4), far(dz4_far)],
        slabs(9 * slab, chans), (tmp, turned_half, bufs), work,
    )
    st3b, a = tie(all_sums(sums), g_dec2)
    a = scatter_first(a)
    dz3, dz3_out, dlog_own, dlog_send, datt, dact2, sums, tot3 = call(
        functools.partial(dec_one_back_kernel, width, count), "dec_one_back", (ids, labels),
        [near(st3), near(st3b), far(pre3), near(dact3), near(params), cut(d1_own), cut(d1_far), near(mask),
         far(gate), far(shared), pick(att_w), near(st2), far(att_pre), far(pre2),
         near(att_gain), near(att_bias), near(enc_gain2), near(enc_bias2)],
        [both(full), near(part), far(part), near(full), near(full), near(four), far(arr((2, chans)))],
        (flat, flat, buf), work,
    )
    dz3_far, dlog_far = swap_cores(dz3_out), swap_cores(dlog_send)
    att_slab = chans // SLABS
    g_dec1 = call(
        functools.partial(grad_dec_one_kernel, width, tasks), "grad_dec_one", (ids, labels),
        [far(up_own), far(up_far), near(dz3), far(dz3_far), far(att_hidden), far(att_hidden_far), near(dlog_own),
         far(dlog_far)],
        slabs(9 * slab + tasks * att_slab // 2, chans), (tmp_four, turned_half, turned_full, bufs), work,
    )
    st2b, a, b = tie(all_sums(sums), a, g_dec1)
    a, b = scatter_second(a), scatter_first(b)
    da_own, da_send, dz2_own, dz2_send, dact1, sums, tot2 = call(
        functools.partial(enc_two_back_kernel, width, count), "enc_two_back", (ids, labels),
        [near(st2), near(st2b), far(att_pre), near(datt), near(att_gain), far(pre2), near(dact2),
         near(enc_gain2), pick(att_w1), cut(e2), near(st1), far(pre1), near(enc_gain1), near(enc_bias1)],
        [near(part), far(part), near(part), far(part), near(full), near(two), far(arr((4, chans)))],
        (flat, flat, buf), work,
    )
    da_far, dz2_far = swap_cores(da_send), swap_cores(dz2_send)
    g_enc2 = call(
        functools.partial(grad_enc_two_kernel, width, tasks), "grad_enc_two", (ids, labels),
        [far(hidden1), far(hidden1_far), near(dz2_own), far(dz2_far), near(da_own), far(da_far)],
        slabs((9 + tasks) * att_slab, half), (tmp, turned_full, bufs_half), work,
    )
    st1b, a, b, c = tie(all_sums(sums), a, b, g_enc2)
    a, b, c = scatter_far(a), scatter_second(b), scatter_first(c)
    band_grad = arr((band, in_chan))
    dz1_own, dz1_send, fg_own, fg_send, tot1 = call(
        functools.partial(enc_one_back_kernel, width, count), "enc_one_back", (ids,),
        [near(st1), near(st1b), far(pre1), near(dact1), near(enc_gain1), cut(e1)],
        [near(part), far(part), far(band_grad), far(band_grad), far(arr((2, chans)))],
        (flat, pltpu.VMEM((pixels, in_chan), F32), buf), work // 2,
    )
    dz1_far = swap_cores(dz1_send)
    in_slab = in_chan // SLABS
    g_enc1 = call(
        functools.partial(grad_enc_one_kernel, width), "grad_enc_one", (ids,),
        [far(own_bands), far(far_bands), near(dz1_own), far(dz1_far)], slabs(9 * in_slab, half),
        (pltpu.VMEM((2, pixels, in_chan), F32), tmp, pltpu.VMEM((2, in_chan, pixels), BF16), bufs_half), work // 2,
    )
    a, b, c, d = tie(a, b, c, g_enc1)
    a, b, c, d = gather_far(a), scatter_far(b), scatter_second(c), scatter_first(d)
    a, b, c, d = tie(a, b, c, d)
    a, b, c, d = gather_second(a), gather_far(b), scatter_far(c), scatter_second(d)
    a, b, c, d = tie(a, b, c, d)
    a, b, c, d = gather_first(a), gather_second(b), gather_far(c), scatter_far(d)
    a, b, c, d = tie(a, b, c, d)
    b, c, d = gather_first(b), gather_second(c), gather_far(d)
    (dec2_grad,) = spread(ids, a, (arr((9, half, chans)),), False, "spread_dec_two")
    dec2_grad, b, c, d = tie(dec2_grad, b, c, d)
    c, d = gather_first(c), gather_second(d)
    dec1_grad, att_grad = spread(
        ids, b, (arr((9, half, chans)), arr((tasks, chans, half))), True, "spread_dec_one"
    )
    dec1_grad, c, d = tie(dec1_grad, c, d)
    d = gather_first(d)
    enc2_grad, att1_grad = spread(
        ids, c, (arr((9, chans, half)), arr((tasks, chans, half))), False, "spread_enc_two"
    )
    enc2_grad, d = tie(enc2_grad, d)
    (enc1_grad,) = spread(ids, d, (arr((9, in_chan, half)),), False, "spread_enc_one")

    fg_far = swap_cores(fg_send)
    bands = jnp.where(core == 0, jnp.stack([fg_own, fg_far]), jnp.stack([fg_far, fg_own]))
    decoded = jnp.where(
        core == 0, jnp.stack([dec_own, dec_far], axis=1), jnp.stack([dec_far, dec_own], axis=1)
    )
    totals = jnp.concatenate([tot1, tot2, tot3, tot4])
    totals = totals + swap_cores(totals)
    dec_totals = lax.dynamic_slice_in_dim(totals[6:10], core * half, half, 1)
    return (
        decoded,
        bands.reshape(2, band_rows, width, in_chan),
        enc1_grad.reshape(3, 3, in_chan, half),
        totals[1],
        totals[0],
        enc2_grad.reshape(3, 3, chans, half),
        totals[3],
        totals[2],
        att1_grad,
        totals[5],
        totals[4],
        att_grad,
        dec1_grad.reshape(3, 3, half, chans),
        dec_totals[1],
        dec_totals[0],
        dec2_grad.reshape(3, 3, half, chans),
        dec_totals[3],
        dec_totals[2],
    )


def solution(mesh):
    return jax.shard_map(
        shards,
        mesh=mesh,
        in_specs=(
            P("dp", "row", None, None),
            P(),
            P(),
            P(),
            P(),
            P(),
            P(),
            P(),
            P(),
            P(),
            P(),
            P(None, None, "row", None),
            P("row"),
            P("row"),
            P(None, None, "row", None),
            P("row"),
            P("row"),
            P("dp"),
            P("dp", None, None),
            P("row", "dp", None),
        ),
        out_specs=(
            P("row", "dp", None),
            P("dp", "row", None, None),
            P(None, None, None, "row"),
            P(),
            P(),
            P(None, None, None, "row"),
            P(),
            P(),
            P(None, None, "row"),
            P(),
            P(),
            P(None, None, "row"),
            P(None, None, "row", None),
            P("row"),
            P("row"),
            P(None, None, "row", None),
            P("row"),
            P("row"),
        ),
        check_vma=False,
    )
```

```python
import functools
import math

import jax
import jax.numpy as jnp
from jax import lax
from jax.experimental import pallas as pl
from jax.experimental.pallas import tpu as pltpu
from jax.sharding import PartitionSpec as P

EPS = 1e-05
F32 = jnp.float32
BF16 = jnp.bfloat16
SLABS = 8
SENT = (2, 3, 6, 7)
KEPT = (0, 1, 4, 5)
MIB = 2**20


def dot(left, right):
    return jnp.dot(left, right, preferred_element_type=F32)


def dot_nt(left, right):
    return lax.dot_general(left, right, (((1,), (1,)), ((), ())), preferred_element_type=F32)


def slope(act):
    sig = jax.nn.sigmoid(act)
    return sig * (1.0 + act * (1.0 - sig))


def silu(act):
    return act * jax.nn.sigmoid(act)


def clear_rims(buf, width):
    rows, lanes = buf.shape
    rim = jnp.zeros((width, lanes), BF16)
    buf[0:width, :] = rim
    buf[rows - width : rows, :] = rim


def fill(buf, value, width, lane, step):
    pixels, chans = value.shape
    col = lax.broadcasted_iota(jnp.int32, (pixels, 1), 0) & (width - 1)
    before = jnp.where(col == 0, 0.0, pltpu.roll(value, 1, 0))
    after = jnp.where(col == width - 1, 0.0, pltpu.roll(value, pixels - 1, 0))
    for at, part in enumerate((before, value, after)):
        start = lane + at * step
        buf[width : width + pixels, start : start + chans] = part.astype(BF16)


def conv(buf, weights, pixels, width, apart=None):
    total, lane = None, 0
    for ref in weights:
        depth = ref.shape[1]
        for i in range(3):
            taps = apart[0] if apart is not None and i == 0 else ref[i]
            term = dot(buf[i * width : i * width + pixels, lane : lane + depth], taps)
            total = term if total is None else total + term
        lane += depth
    return total


def shifted(buf, i, j, pixels, width, chans):
    return buf[(2 - i) * width : (2 - i) * width + pixels, (2 - j) * chans : (3 - j) * chans]


def conv_back(buf, weights, pixels, width):
    chans = weights[0].shape[2]
    depth = weights[0].shape[1] // 3
    total = None
    for i in range(3):
        for j in range(3):
            taps = [ref[i, j * depth : (j + 1) * depth, :] for ref in weights]
            taps = taps[0] if len(taps) == 1 else jnp.concatenate(taps, axis=0)
            term = dot_nt(shifted(buf, i, j, pixels, width, chans), taps)
            total = term if total is None else total + term
    return total


def put_sums(ref, terms):
    for at, term in enumerate(terms):
        row = jnp.sum(term, axis=0, keepdims=True)
        ref[:, at : at + 1, :] = jnp.broadcast_to(row[None], (ref.shape[0], 1, ref.shape[2]))
    ref.flush()


def gather_sums(ref):
    return jnp.sum(ref[...], axis=0)


def moments(ref, at, count):
    total = gather_sums(ref)
    mean = total[at : at + 1] / count
    square = total[at + 1 : at + 2] / count
    return mean, lax.rsqrt(square - mean * mean + EPS)


def normed(pre, mom):
    return (pre.astype(F32) - mom[0]) * mom[1]


def norm_back(grad, pre, mom, gain, total, at, count):
    xhat = normed(pre, mom)
    return (gain * mom[1]) * (
        grad.astype(F32) - total[at : at + 1] / count - xhat * (total[at + 1 : at + 2] / count)
    )


def row_of(ref):
    return ref[...].reshape(1, -1)


def half_at(ids, other, half, which=0):
    side = ids[which]
    if other:
        side = 1 - side
    return pl.ds(pl.multiple_of(side * half, half), half)


CORES = ((0, False), (0, False), (0, True), (0, True))
PLACES = ((2, False), (2, True), (3, False), (3, True))


def deal(refs, at, flat, ids, plan):
    half = flat.shape[1] // 2
    for ref, (which, other) in zip(refs, plan, strict=True):
        part = flat[:, half_at(ids, other, half, which)]
        if at is None:
            ref[...] = part
        else:
            ref[at] = part


def enc_one_kernel(width, ids, own, far, w_ref, pre_ref, sum_ref, flat, buf):
    pixels, chans = flat.shape
    band = pixels // 2
    side = ids[0]
    flat[half_at(ids, False, band), :] = own[side].astype(F32)
    flat[half_at(ids, True, band), :] = far[side].astype(F32)
    clear_rims(buf, width)
    fill(buf, flat[...], width, 0, chans)
    pre = conv(buf, (w_ref,), pixels, width)
    pre_ref[...] = pre
    pre_ref.flush()
    put_sums(sum_ref, (pre, pre * pre))


def enc_two_kernel(
    width, count, ids, labels, st1, pre1, gain1, bias1, aw_ref, w_first, w_ref,
    hid_own, hid_next, hid_core, hid_cross, pre2_ref, att_ref, sum_ref, flat, buf,
):
    pixels, chans = pre1.shape
    mom = moments(st1, 0, count)
    hidden = silu(normed(pre1[...], mom) * row_of(gain1) + row_of(bias1))
    clear_rims(buf, width)
    fill(buf, hidden, width, 0, chans)
    flat[...] = hidden
    hids = (hid_own, hid_next, hid_core, hid_cross)
    deal(hids, None, flat, ids, PLACES)
    for ref in hids:
        ref.flush()
    att = dot(hidden.astype(BF16), aw_ref[...])
    att_ref[...] = att
    att_ref.flush()
    pre = conv(buf, (w_ref,), pixels, width, w_first)
    pre2_ref[...] = pre
    pre2_ref.flush()
    put_sums(sum_ref, (pre, pre * pre, att, att * att))


def dec_one_kernel(
    width, count, ids, labels, st2, pre2, att_pre, gain2, bias2, gain_a, bias_a, aw_ref, mask, w_own, w_far,
    own, following, core, cross, shared_ref, gate_ref, pre3_ref, sum_ref, flat, hid, buf,
):
    pixels, chans = pre2.shape
    half = chans // 2
    shared = silu(normed(pre2[...], moments(st2, 0, count)) * row_of(gain2) + row_of(bias2))
    shared_ref[...] = shared
    shared_ref.flush()
    hid[...] = silu(normed(att_pre[...], moments(st2, 2, count)) * row_of(gain_a) + row_of(bias_a))
    gate = jax.nn.sigmoid(dot(hid[...].astype(BF16), aw_ref[...]))
    gate_ref[...] = gate
    gate_ref.flush()
    flat[...] = gate * shared * mask[...]
    clear_rims(buf, width)
    for other in (False, True):
        fill(buf, flat[:, half_at(ids, other, half)], width, 3 * half * other, half)
    parts = (own, following, core, cross)
    deal(parts, 0, flat, ids, CORES)
    deal(parts, 1, hid, ids, PLACES)
    for ref in parts:
        ref.flush()
    pre = conv(buf, (w_own, w_far), pixels, width)
    pre3_ref[...] = pre
    pre3_ref.flush()
    put_sums(sum_ref, (pre, pre * pre))


def dec_two_kernel(
    width, count, ids, st3, pre3, params, w_own, w_far, pre4_ref, sum_ref, keep_ref, send_ref, flat, buf
):
    pixels, chans = pre3.shape
    half = chans // 2
    flat[...] = silu(normed(pre3[...], moments(st3, 0, count)) * params[0:1, :] + params[1:2, :])
    clear_rims(buf, width)
    for other, ref in ((False, keep_ref), (True, send_ref)):
        part = flat[:, half_at(ids, other, half)]
        fill(buf, part, width, 3 * half * other, half)
        ref[...] = part.astype(BF16)
        ref.flush()
    pre = conv(buf, (w_own, w_far), pixels, width)
    pre4_ref[...] = pre
    pre4_ref.flush()
    put_sums(sum_ref, (pre, pre * pre))


def top_kernel(count, ids, st4, pre4, params, og_own, og_far, dact_ref, sum_ref, keep_ref, send_ref, cot, out):
    pixels, chans = pre4.shape
    half = chans // 2
    xhat = normed(pre4[...], moments(st4, 0, count))
    act = xhat * params[2:3, :] + params[3:4, :]
    sig = jax.nn.sigmoid(act)
    out[...] = act * sig
    cot[:, half_at(ids, False, half)] = og_own[...].astype(F32).T
    cot[:, half_at(ids, True, half)] = og_far[...].astype(F32).T
    dact = cot[...] * (sig * (1.0 + act * (1.0 - sig)))
    dact_ref[...] = dact
    dact_ref.flush()
    put_sums(sum_ref, (dact, dact * xhat))
    for other, ref in ((False, keep_ref), (True, send_ref)):
        ref[...] = out[:, half_at(ids, other, half)].T.astype(BF16)


def dec_two_back_kernel(
    width, count, ids, st4, st4b, pre4, dact4, params, w_own, w_far, st3, pre3,
    dz_own, dz_next, dz_core, dz_cross, dact_ref, sum_ref, tot_ref, flat, dz_flat, buf,
):
    pixels, chans = pre4.shape
    half = chans // 2
    total = gather_sums(st4b)
    tot_ref[...] = total
    tot_ref.flush()
    dz = norm_back(dact4[...], pre4[...], moments(st4, 0, count), params[2:3, :], total, 0, count)
    dz_flat[...] = dz
    parts = (dz_own, dz_next, dz_core, dz_cross)
    deal(parts, None, dz_flat, ids, PLACES)
    for ref in parts:
        ref.flush()
    clear_rims(buf, width)
    fill(buf, dz, width, 0, chans)
    back = conv_back(buf, (w_own, w_far), pixels, width)
    flat[:, half_at(ids, False, half)] = back[:, :half]
    flat[:, half_at(ids, True, half)] = back[:, half:]
    xhat = normed(pre3[...], moments(st3, 0, count))
    dact = flat[...] * slope(xhat * params[0:1, :] + params[1:2, :])
    dact_ref[...] = dact
    dact_ref.flush()
    put_sums(sum_ref, (dact, dact * xhat))


def dec_one_back_kernel(
    width, count, ids, labels, st3, st3b, pre3, dact3, params, w_own, w_far, mask, gate_ref, shared_ref, aw_ref,
    st2, att_pre, pre2, gain_a, bias_a, gain2, bias2,
    own, following, core, cross, datt_ref, dact2_ref, sum_ref, tot_ref, flat, dlog, dz_flat, buf,
):
    pixels, chans = pre3.shape
    half = chans // 2
    total = gather_sums(st3b)
    tot_ref[...] = total
    tot_ref.flush()
    dz = norm_back(dact3[...], pre3[...], moments(st3, 0, count), params[0:1, :], total, 0, count)
    dz_flat[...] = dz
    parts = (own, following, core, cross)
    deal(parts, 0, dz_flat, ids, PLACES)
    clear_rims(buf, width)
    fill(buf, dz, width, 0, chans)
    back = conv_back(buf, (w_own, w_far), pixels, width)
    flat[:, half_at(ids, False, half)] = back[:, :half]
    flat[:, half_at(ids, True, half)] = back[:, half:]
    grad = (flat[...] * mask[...]).astype(BF16).astype(F32)
    gate = gate_ref[...].astype(F32)
    dlog[...] = grad * shared_ref[...].astype(F32) * gate * (1.0 - gate)
    deal(parts, 1, dlog, ids, CORES)
    for ref in parts:
        ref.flush()
    dhid = dot_nt(dlog[...].astype(BF16), aw_ref[...])
    att_hat = normed(att_pre[...], moments(st2, 2, count))
    datt = dhid * slope(att_hat * row_of(gain_a) + row_of(bias_a))
    datt_ref[...] = datt
    datt_ref.flush()
    xhat2 = normed(pre2[...], moments(st2, 0, count))
    dact2 = grad * gate * slope(xhat2 * row_of(gain2) + row_of(bias2))
    dact2_ref[...] = dact2
    dact2_ref.flush()
    put_sums(sum_ref, (dact2, dact2 * xhat2, datt, datt * att_hat))


def enc_two_back_kernel(
    width, count, ids, labels, st2, st2b, att_pre, datt_ref, gain_a, pre2, dact2, gain2, aw_ref, w_ref,
    st1, pre1, gain1, bias1,
    own, core, dact_ref, sum_ref, tot_ref, flat, datt, buf,
):
    pixels, chans = pre2.shape
    total = gather_sums(st2b)
    tot_ref[...] = total
    tot_ref.flush()
    dz = norm_back(dact2[...], pre2[...], moments(st2, 0, count), row_of(gain2), total, 0, count)
    flat[...] = dz
    deal((own, core), 0, flat, ids, CORES[1:3])
    clear_rims(buf, width)
    fill(buf, dz, width, 0, chans)
    datt[...] = norm_back(
        datt_ref[...], att_pre[...], moments(st2, 2, count), row_of(gain_a), total, 2, count
    )
    deal((own, core), 1, datt, ids, CORES[1:3])
    own.flush()
    core.flush()
    dhid = dot_nt(datt[...].astype(BF16), aw_ref[...])
    dhid = dhid + conv_back(buf, (w_ref,), pixels, width)
    xhat = normed(pre1[...], moments(st1, 0, count))
    dact = dhid * slope(xhat * row_of(gain1) + row_of(bias1))
    dact_ref[...] = dact
    dact_ref.flush()
    put_sums(sum_ref, (dact, dact * xhat))


def enc_one_back_kernel(
    width, count, ids, st1, st1b, pre1, dact1, gain1, w_ref, dz_keep, dz_send, fg_keep, fg_send, tot_ref, flat, back, buf
):
    pixels, chans = pre1.shape
    half = chans // 2
    total = gather_sums(st1b)
    tot_ref[...] = total
    tot_ref.flush()
    dz = norm_back(dact1[...], pre1[...], moments(st1, 0, count), row_of(gain1), total, 0, count)
    flat[...] = dz
    for other, ref in ((False, dz_keep), (True, dz_send)):
        ref[...] = flat[:, half_at(ids, other, half)].astype(BF16)
        ref.flush()
    clear_rims(buf, width)
    fill(buf, dz, width, 0, chans)
    back[...] = conv_back(buf, (w_ref,), pixels, width)
    for other, ref in ((False, fg_keep), (True, fg_send)):
        ref[...] = back[half_at(ids, other, pixels // 2), :]


def lay_rows(ids, value, at, tmp, turned):
    rows = turned.shape[1]
    part = rows // SLABS
    tmp[at] = value.astype(F32).T.astype(BF16)
    for slot, t in enumerate(KEPT + SENT):
        start = pl.multiple_of((ids[1] ^ t) * part, part)
        turned[at, slot * part : (slot + 1) * part, :] = tmp[at, pl.ds(start, part), :]


def store_slabs(pieces, row, part, value):
    low = value.astype(BF16)
    for kept, sent in pieces:
        if row < kept.shape[1]:
            break
        row -= kept.shape[1]
    for slot in range(SLABS):
        ref, at = (kept, slot) if slot < SLABS // 2 else (sent, slot - SLABS // 2)
        ref[at, row : row + part, :] = low[slot * part : (slot + 1) * part]


def conv_weights(ids, width, values, grads, pieces, tmp, turned, bufs):
    count, _, pixels = turned.shape
    chans = bufs.shape[2] // 3
    part = turned.shape[1] // SLABS
    for at in range(count):
        lay_rows(ids, values[at](), at, tmp, turned)
        clear_rims(bufs.at[at], width)
        fill(bufs.at[at], grads[at]().astype(F32), width, 0, chans)
    for i in range(3):
        for j in range(3):
            total = None
            for at in range(count):
                term = dot(turned[at], shifted(bufs.at[at], i, j, pixels, width, chans))
                total = term if total is None else total + term
            store_slabs(pieces, (3 * i + j) * part, part, total)


def task_weights(marks, tasks, turned, grads, pieces):
    part = turned.shape[1] // SLABS
    terms = [dot(turned[at], grad()) for at, grad in enumerate(grads)]
    for task in range(tasks):
        total = None
        for mark, term in zip(marks, terms, strict=True):
            term = term * (mark == task).astype(F32)
            total = term if total is None else total + term
        store_slabs(pieces, (9 + task) * part, part, total)


def frame_marks(ids, labels, labels_next):
    side = ids[0]
    return labels[side], labels[1 - side], labels_next[side], labels_next[1 - side]


def whole_of(ref):
    return lambda: ref[...]


def layer_of(ref, k):
    return lambda: ref[k]


def grad_dec_two_kernel(width, ids, *refs):
    kept, sent, tmp, turned, bufs = refs[8:]
    values, grads = [whole_of(r) for r in refs[:4]], [whole_of(r) for r in refs[4:8]]
    conv_weights(ids, width, values, grads, ((kept, sent),), tmp, turned, bufs)


def grad_dec_one_kernel(width, tasks, ids, labels, labels_next, *refs):
    values, grads = refs[:4], refs[4:8]
    pieces = (refs[8:10], refs[10:12])
    tmp, turned, tmp_att, turned_att, bufs = refs[12:]
    conv_weights(
        ids, width, [layer_of(r, 0) for r in values], [layer_of(r, 0) for r in grads],
        pieces, tmp, turned, bufs,
    )
    for at in range(4):
        lay_rows(ids, values[at][1], at, tmp_att, turned_att)
    marks = frame_marks(ids, labels, labels_next)
    task_weights(marks, tasks, turned_att, [layer_of(r, 1) for r in grads], pieces)


def grad_enc_two_kernel(width, tasks, ids, labels, labels_next, *refs):
    values, grads = refs[:4], refs[4:8]
    pieces = (refs[8:10], refs[10:12])
    tmp, turned, bufs = refs[12:]
    conv_weights(
        ids, width, [whole_of(r) for r in values], [layer_of(r, 0) for r in grads],
        pieces, tmp, turned, bufs,
    )
    marks = frame_marks(ids, labels, labels_next)
    task_weights(marks, tasks, turned, [layer_of(r, 1) for r in grads], pieces)


def grad_enc_one_kernel(width, ids, own, far, own_next, far_next, *refs):
    grads = [whole_of(r) for r in refs[:4]]
    kept, sent, flat, tmp, turned, bufs = refs[4:]
    band, chans = flat.shape[1] // 2, flat.shape[2]
    side = ids[0]

    def frame(at, near_band, far_band, which):
        def read():
            flat[at, half_at(ids, False, band), :] = near_band[which].astype(F32)
            flat[at, half_at(ids, True, band), :] = far_band[which].astype(F32)
            return flat[at, :, half_at(ids, False, chans // 2, 2)]

        return read

    values = [
        frame(0, own, far, side),
        frame(1, own, far, 1 - side),
        frame(2, own_next, far_next, side),
        frame(3, own_next, far_next, 1 - side),
    ]
    conv_weights(ids, width, values, grads, ((kept, sent),), tmp, turned, bufs)


def spread_kernel(by_lanes, n_pieces, ids, *refs):
    outs = refs[2 * n_pieces :]
    base = 0
    for out, lanes_too in zip(outs, (by_lanes, False), strict=False):
        layers, rows, lanes = out.shape
        split = lanes // 2 if lanes_too else lanes
        height = rows if lanes_too else rows // 2
        part = height // SLABS
        for layer in range(layers):
            line, piece = base + layer * part, 0
            while line >= refs[piece].shape[1]:
                line -= refs[piece].shape[1]
                piece += 1
            for other in (False, True):
                ref = refs[n_pieces + piece] if other else refs[piece]
                side = 1 - ids[2] if other else ids[2]
                for t in range(SLABS):
                    start = (ids[1] ^ t) * part
                    if not lanes_too:
                        start = start + side * height
                    where = pl.ds(pl.multiple_of(start, part), part)
                    span = pl.ds(pl.multiple_of(side * split, split), split) if lanes_too else slice(None)
                    out[layer, where, span] = ref[t, line : line + part, :].astype(F32)
            out.flush(layer)
        base += layers * part


def arr(shape, kind=F32):
    return jax.ShapeDtypeStruct(shape, kind)


class Source:
    def __init__(self, pieces, buf):
        self.pieces, self.buf, self.shape = pieces, buf, buf.shape
        self.waiting = [True] * len(pieces)

    def start(self):
        for piece, wanted in zip(self.pieces, self.waiting, strict=True):
            if wanted:
                piece.start()

    def __getitem__(self, at):
        first = at[0] if isinstance(at, tuple) else at
        cut_one = len(self.pieces) > 1 and isinstance(first, int)
        for k in [first] if cut_one else range(len(self.pieces)):
            if self.waiting[k]:
                self.pieces[k].wait()
                self.waiting[k] = False
        return self.buf[at]

    def finish(self):
        for k, piece in enumerate(self.pieces):
            if self.waiting[k]:
                piece.wait()


class Target:
    def __init__(self, pieces, buf):
        self.pieces, self.buf, self.shape = pieces, buf, buf.shape
        self.sent = [False] * len(pieces)

    def __setitem__(self, at, value):
        self.buf[at] = value.astype(self.buf.dtype)

    def __getitem__(self, at):
        return self.buf[at]

    def flush(self, k=0):
        if k < len(self.pieces) and not self.sent[k]:
            self.pieces[k].start()
            self.sent[k] = True

    def finish(self):
        for k, piece in enumerate(self.pieces):
            self.flush(k)
        for piece in self.pieces:
            piece.wait()


def near(array):
    return array, "near"


def far(array):
    return array, "far"


def cut(array):
    return array, "cut"


def rest(array):
    return array, "rest"


def pick(array):
    return array, "pick"


def both(array):
    return array, "both"


def held(array, kind):
    return pltpu.with_memory_space_constraint(array, pltpu.VMEM if kind == "near" else pltpu.HBM)


def call(body, name, scalars, args, outs, scratch=(), flops=0):
    smem, vmem = pl.BlockSpec(memory_space=pltpu.SMEM), pl.BlockSpec(memory_space=pltpu.VMEM)
    hbm = pl.BlockSpec(memory_space=pltpu.HBM)
    moved = sum(a.size * a.dtype.itemsize for a, _ in list(args) + list(outs))
    arrays = list(args) + list(outs)
    pieces = [a.shape[0] if kind in ("cut", "rest") else 1 for a, kind in arrays]
    kinds = [kind for _, kind in arrays]
    bufs = [
        pltpu.VMEM(a.shape[1:] if kind == "pick" else a.shape, a.dtype)
        for a, kind in arrays
        if kind not in ("near", "both")
    ]
    places, shapes = [], []
    for a, kind in outs:
        if kind in ("near", "both"):
            places.append(vmem)
            shapes.append(pltpu.VMEM(a.shape, a.dtype))
        if kind != "near":
            places.append(hbm)
            shapes.append(pltpu.HBM(a.shape, a.dtype))
    held_bytes = sum(jnp.dtype(b.dtype).itemsize * math.prod(b.shape) for b in bufs + list(scratch))
    n_sems = max(1, sum(p for p, kind in zip(pieces, kinds, strict=True) if kind != "near"))

    def kernel(*refs):
        refs = list(refs)

        def take(count):
            taken = refs[:count]
            del refs[:count]
            return taken

        given = take(len(scalars))
        ins, results = take(len(args)), take(len(shapes))
        local, (sems,) = take(len(bufs)), take(1)
        items, slot = [], 0
        for k, kind in enumerate(kinds):
            is_out = k >= len(args)
            if kind == "near":
                items.append(Target((), results.pop(0)) if is_out else ins[k])
                continue
            inside = results.pop(0) if kind == "both" else local.pop(0)
            outside = results.pop(0) if is_out else ins[k]
            if kind == "pick":
                outside = outside.at[given[1][given[0][0]]]
            copies = []
            for piece in range(pieces[k]):
                apart = kind in ("cut", "rest")
                ends = (outside.at[piece], inside.at[piece]) if apart else (outside, inside)
                left, right = reversed(ends) if is_out else ends
                copies.append(pltpu.make_async_copy(left, right, sems.at[slot]))
                slot += 1
            items.append((Target if is_out else Source)(copies, inside))
            if kind == "rest":
                items[-1].waiting[0] = False
        for item in items:
            if isinstance(item, Source):
                item.start()
        body(*given, *items, *refs)
        for item in items:
            if isinstance(item, (Source, Target)):
                item.finish()

    return pl.pallas_call(
        kernel,
        out_shape=shapes,
        in_specs=[smem] * len(scalars) + [vmem if kind == "near" else hbm for _, kind in args],
        out_specs=places,
        scratch_shapes=bufs + [pltpu.SemaphoreType.DMA((n_sems,))] + list(scratch),
        name=name,
        compiler_params=pltpu.CompilerParams(vmem_limit_bytes=held_bytes + 8 * MIB),
        cost_estimate=pl.CostEstimate(flops=flops, bytes_accessed=moved, transcendentals=0),
    )(*scalars, *[held(a, kind) for a, kind in args])


def fetch_kernel(source, target, sems):
    copies = [pltpu.make_async_copy(source.at[k], target.at[k], sems.at[k]) for k in range(target.shape[0])]
    for copy in copies:
        copy.start()
    for copy in copies:
        copy.wait()


def fetch(weight, count):
    shape = (count,) + weight.shape[1:]
    return pl.pallas_call(
        fetch_kernel,
        out_shape=pltpu.VMEM(shape, weight.dtype),
        in_specs=[pl.BlockSpec(memory_space=pltpu.HBM)],
        out_specs=pl.BlockSpec(memory_space=pltpu.VMEM),
        scratch_shapes=[pltpu.SemaphoreType.DMA((count,))],
        name="fetch",
        compiler_params=pltpu.CompilerParams(vmem_limit_bytes=MIB),
        cost_estimate=pl.CostEstimate(flops=0, bytes_accessed=4 * math.prod(shape), transcendentals=0),
    )(held(weight, "far"))


def swap_cores(value):
    return lax.ppermute(value, "row", [(0, 1), (1, 0)])


def exchange(value, masks):
    count, cores = lax.axis_size("dp"), lax.axis_size("row")
    pairs = [
        (d * cores + r, (d ^ masks[r]) * cores + r) for d in range(count) for r in range(cores)
    ]
    return lax.ppermute(value, ("dp", "row"), pairs)


FIRST, SECOND, Z_NEAR, Z_FAR = (1, 2), (2, 1), (4, 4), (8, 8)


def cross(value):
    count = lax.axis_size("dp")
    pairs = [(d * 2 + r, (d ^ FIRST[1 - r]) * 2 + 1 - r) for d in range(count) for r in range(2)]
    return lax.ppermute(value, ("dp", "row"), pairs)


def dealt(to_next, to_core, to_cross):
    return swap_cores(to_core), exchange(to_next, FIRST), cross(to_cross)


def add(left, right):
    return (left.astype(F32) + right.astype(F32)).astype(BF16)


class Piece:
    def __init__(self, slabs):
        kept, sent = slabs
        self.low, self.high, self.state = kept[:2], kept[2:], 0
        self.coming = exchange(sent, SECOND)

    def step(self, order):
        got = order.after(self.coming)
        if self.state == 0:
            self.low = add(self.low, got[:2])
            self.coming = exchange(add(self.high, got[2:]), Z_NEAR)
        elif self.state == 1:
            self.low = add(self.low, got)
            self.coming = exchange(self.low, Z_FAR)
        elif self.state == 2:
            self.low = add(self.low, jnp.concatenate([got[1:], got[:1]]))
            bit = 16
            while bit < lax.axis_size("dp"):
                self.low = add(self.low, exchange(self.low, (bit, bit)))
                bit *= 2
            self.coming = exchange(self.low, SECOND)
        elif self.state < 5:
            self.low = jnp.concatenate([self.low, got])
            self.coming = exchange(self.low, (Z_NEAR, FIRST)[self.state - 3])
        else:
            self.far_half = got
        self.state += 1
        order.done(self.low if self.state < 6 else got)

    def halves(self):
        return self.low, self.far_half


TAIL = "cBbCacbBdCaBcbdCcBdCbdcBCdcCd"


class Order:
    def __init__(self):
        self.last = None

    def after(self, value):
        return value if self.last is None else tie(self.last, value)[1]

    def done(self, value):
        self.last = value


def tie(*values):
    return lax.optimization_barrier(values)


def spread(ids, pieces, outs, by_lanes, name):
    parts = [far(p[0]) for p in pieces] + [far(p[1]) for p in pieces]
    return call(
        functools.partial(spread_kernel, by_lanes, len(pieces)), name, (ids,), parts, [cut(o) for o in outs]
    )


def all_sums(value):
    return lax.all_to_all(value, "dp", 0, 0, tiled=False)


def shards(
    frames,
    enc_w1,
    enc_gain1,
    enc_bias1,
    enc_w2,
    enc_gain2,
    enc_bias2,
    att_w1,
    att_gain,
    att_bias,
    att_w,
    dec_w1,
    dec_gain1,
    dec_bias1,
    dec_w2,
    dec_gain2,
    dec_bias2,
    labels,
    pool_index,
    out_grad,
):
    band_rows, width, in_chan = frames.shape[1:]
    chans = enc_w1.shape[3]
    half = dec_w1.shape[2]
    height = 2 * pool_index.shape[1]
    pixels = height * width
    band = band_rows * width
    tasks = att_w.shape[0]
    n_dp = lax.axis_size("dp")
    count = float(pixels * n_dp)
    core = lax.axis_index("row")
    chip = lax.axis_index("dp")
    bit_x, bit_y = chip & 1, (chip >> 1) & 1
    first = jnp.where(core == 0, bit_x, bit_y)
    second = jnp.where(core == 0, bit_y, bit_x)
    place = 4 * ((chip >> 2) & 1) + 2 * second + ((chip >> 3) & 1)
    ids = jnp.stack([core, place, first, second]).astype(jnp.int32)

    own_bands = frames.reshape(2, band, in_chan)
    far_bands = swap_cores(own_bands)
    own_next, far_next = exchange(own_bands, FIRST), exchange(far_bands, FIRST)
    labels_next = exchange(labels, FIRST)
    d1_own = dec_w1.reshape(3, 3 * half, chans)
    d2_own = dec_w2.reshape(3, 3 * half, chans)
    d1_far = swap_cores(d1_own)
    d2_far = swap_cores(d2_own)
    params_own = jnp.stack([dec_gain1, dec_bias1, dec_gain2, dec_bias2])
    params_far = swap_cores(params_own)
    params = jnp.where(
        core == 0,
        jnp.concatenate([params_own, params_far], axis=1),
        jnp.concatenate([params_far, params_own], axis=1),
    )
    og_own = lax.dynamic_index_in_dim(out_grad, core, 1, keepdims=False)
    og_far = swap_cores(lax.dynamic_index_in_dim(out_grad, 1 - core, 1, keepdims=False))
    index = lax.dynamic_index_in_dim(pool_index, core, 0, keepdims=False)
    index = jnp.repeat(jnp.repeat(index, 2, axis=0), 2, axis=1)
    cell = 2 * (jnp.arange(height)[:, None] % 2) + jnp.arange(width)[None, :] % 2
    mask = (index == cell).astype(F32).reshape(pixels, 1)
    e1 = enc_w1.reshape(3, 3 * in_chan, chans)
    e2 = enc_w2.reshape(3, 3 * chans, chans)

    full = arr((pixels, chans), BF16)
    part = arr((pixels, half), BF16)
    pair = arr((2, pixels, half), BF16)
    two = arr((n_dp, 2, chans))
    four = arr((n_dp, 4, chans))
    flat = pltpu.VMEM((pixels, chans), F32)
    buf = pltpu.VMEM((pixels + 2 * width, 3 * chans), BF16)
    work = 2 * pixels * 9 * chans * chans

    pre1, sums = call(
        functools.partial(enc_one_kernel, width), "enc_one", (ids,),
        [far(own_bands), far(far_bands), near(fetch(e1, 3))], [far(full), near(two)],
        (pltpu.VMEM((pixels, in_chan), F32), pltpu.VMEM((pixels + 2 * width, 3 * in_chan), BF16)), work // 2,
    )
    sums, w_near = tie(sums, e2)
    st1 = all_sums(sums)
    hid1_own, hid1_next, hid1_core, hid1_cross, pre2, att_pre, sums = call(
        functools.partial(enc_two_kernel, width, count), "enc_two", (ids, labels),
        [near(st1), far(pre1), near(enc_gain1), near(enc_bias1), pick(att_w1), near(fetch(w_near, 1)), rest(e2)],
        [far(part)] * 4 + [far(full), far(full), near(four)], (flat, buf), work,
    )
    sums, w_own = tie(sums, d1_own)
    st2 = all_sums(sums)
    hid1_far = dealt(hid1_next, hid1_core, hid1_cross)
    up_own, up_next, up_core, up_cross, shared, gate, pre3, sums = call(
        functools.partial(dec_one_kernel, width, count), "dec_one", (ids, labels),
        [near(st2), far(pre2), far(att_pre), near(enc_gain2), near(enc_bias2), near(att_gain), near(att_bias),
         pick(att_w), near(mask), near(fetch(w_own, 3)), cut(d1_far)],
        [far(pair)] * 4 + [far(full), far(full), far(full), near(two)], (flat, flat, buf), work,
    )
    sums, w_own = tie(sums, d2_own)
    st3 = all_sums(sums)
    up_far = dealt(up_next, up_core, up_cross)
    pre4, sums, hidden3_own, hidden3_send = call(
        functools.partial(dec_two_kernel, width, count), "dec_two", (ids,),
        [near(st3), far(pre3), near(params), near(fetch(w_own, 3)), cut(d2_far)],
        [near(full), near(two), far(part), far(part)], (flat, buf), work,
    )
    st4, hid1_far, labels_next = tie(all_sums(sums), hid1_far, labels_next)
    hid3_far = dealt(hidden3_own, hidden3_send, hidden3_send)
    turned = arr((half, pixels), BF16)
    dact4, sums, dec_own, dec_send = call(
        functools.partial(top_kernel, count), "top", (ids,),
        [near(st4), near(pre4), near(params), far(og_own), far(og_far)],
        [near(full), near(two), far(turned), far(turned)], (flat, flat),
    )
    st4b, up_far, own_next, far_next = tie(all_sums(sums), up_far, own_next, far_next)
    dec_far = swap_cores(dec_send)
    dz4_own, dz4_next, dz4_core, dz4_cross, dact3, sums, tot4 = call(
        functools.partial(dec_two_back_kernel, width, count), "dec_two_back", (ids,),
        [near(st4), near(st4b), near(pre4), near(dact4), near(params), cut(d2_own), cut(d2_far), near(st3),
         far(pre3)],
        [near(part)] + [far(part)] * 3 + [near(full), near(two), far(arr((2, chans)))], (flat, flat, buf), work,
    )
    dz4_far = dealt(dz4_next, dz4_core, dz4_cross)
    tmp = pltpu.VMEM((4, half, pixels), BF16)
    bufs = pltpu.VMEM((4, pixels + 2 * width, 3 * half), BF16)

    def slabs(rows):
        return [far(arr((SLABS // 2, rows, half), BF16))] * 2

    slab = half // SLABS
    a = call(
        functools.partial(grad_dec_two_kernel, width), "grad_dec_two", (ids,),
        [far(v) for v in (hidden3_own,) + hid3_far] + [near(dz4_own)] + [far(v) for v in dz4_far],
        slabs(9 * slab), (tmp, tmp, bufs), work,
    )
    st3b, a = tie(all_sums(sums), a)
    order = Order()
    a = Piece(a)
    dz3_own, dz3_next, dz3_core, dz3_cross, datt, dact2, sums, tot3 = call(
        functools.partial(dec_one_back_kernel, width, count), "dec_one_back", (ids, labels),
        [near(st3), near(st3b), far(pre3), near(dact3), near(params), cut(d1_own), cut(d1_far), near(mask),
         far(gate), far(shared), pick(att_w), near(st2), far(att_pre), far(pre2),
         near(att_gain), near(att_bias), near(enc_gain2), near(enc_bias2)],
        [far(pair)] * 4 + [near(full), near(full), near(four), far(arr((2, chans)))],
        (flat, flat, flat, buf), work,
    )
    order.done(tot3)
    a.step(order)
    dz3_far = dealt(*(order.after(v) for v in (dz3_next, dz3_core, dz3_cross)))
    st2b, dz3_far = tie(order.after(all_sums(sums)), dz3_far)
    dz2_own, dz2_core, dact1, sums, tot2 = call(
        functools.partial(enc_two_back_kernel, width, count), "enc_two_back", (ids, labels),
        [near(st2), near(st2b), far(att_pre), near(datt), near(att_gain), far(pre2), near(dact2),
         near(enc_gain2), pick(att_w1), cut(e2), near(st1), far(pre1), near(enc_gain1), near(enc_bias1)],
        [far(pair), far(pair), near(full), near(two), far(arr((4, chans)))],
        (flat, flat, buf), work,
    )
    order.done(tot2)
    a.step(order)
    dz2_next, dz2_core = order.after(dz2_own), order.after(dz2_core)
    dz2_far = dealt(dz2_next, dz2_core, dz2_core)
    row_split = (9 + tasks) * slab // 2
    b = call(
        functools.partial(grad_dec_one_kernel, width, tasks), "grad_dec_one", (ids, labels, labels_next),
        [far(v) for v in (order.after(up_own),) + up_far + (dz3_own,) + dz3_far],
        slabs(row_split) * 2, (tmp, tmp, tmp, tmp, bufs), work,
    )
    order.done(b)
    b1, b2 = Piece(b[:2]), Piece(b[2:])
    a.step(order)
    c = call(
        functools.partial(grad_enc_two_kernel, width, tasks), "grad_enc_two", (ids, labels, labels_next),
        [far(v) for v in (order.after(hid1_own),) + hid1_far + (dz2_own,) + dz2_far],
        slabs(row_split) * 2, (tmp, tmp, bufs), work,
    )
    order.done(c)
    c1, c2 = Piece(c[:2]), Piece(c[2:])
    b1.step(order)
    st1b = order.after(all_sums(sums))
    band_grad = arr((band, in_chan))
    dz1_own, dz1_send, fg_own, fg_send, tot1 = call(
        functools.partial(enc_one_back_kernel, width, count), "enc_one_back", (ids,),
        [near(st1), near(st1b), far(pre1), near(dact1), near(enc_gain1), cut(e1)],
        [far(part), far(part), far(band_grad), far(band_grad), far(arr((2, chans)))],
        (flat, pltpu.VMEM((pixels, in_chan), F32), buf), work // 2,
    )
    order.done(tot1)
    dz1_far = dealt(dz1_own, dz1_send, dz1_send)
    for piece in (a, b2, b1):
        piece.step(order)
    low = pltpu.VMEM((4, in_chan // 2, pixels), BF16)
    d = call(
        functools.partial(grad_enc_one_kernel, width), "grad_enc_one", (ids,),
        [far(v) for v in (own_bands, far_bands, own_next, far_next, order.after(dz1_own)) + dz1_far],
        slabs(9 * slab // 2), (pltpu.VMEM((4, pixels, in_chan), F32), low, low, bufs), work // 2,
    )
    order.done(d)
    d = Piece(d)
    pieces = {"a": a, "b": b1, "B": b2, "c": c1, "C": c2, "d": d}
    dec_shape, enc_shape, task_shape = arr((9, half, chans)), arr((9, chans, half)), arr((tasks, chans, half))
    results = {
        "a": ((dec_shape,), True, "spread_dec_two"),
        "bB": ((dec_shape, task_shape), True, "spread_dec_one"),
        "cC": ((enc_shape, task_shape), False, "spread_enc_two"),
        "d": ((arr((9, in_chan, half)),), False, "spread_enc_one"),
    }
    for name in TAIL:
        pieces[name].step(order)
        for group in [g for g in results if name in g and all(pieces[n].state == 6 for n in g)]:
            shapes, by_lanes, title = results[group]
            results[group] = spread(ids, [pieces[n].halves() for n in group], shapes, by_lanes, title)
            order.done(results[group][0])
    (dec2_grad,), (dec1_grad, att_grad) = results["a"], results["bB"]
    (enc2_grad, att1_grad), (enc1_grad,) = results["cC"], results["d"]

    fg_far = swap_cores(fg_send)
    bands = jnp.where(core == 0, jnp.stack([fg_own, fg_far]), jnp.stack([fg_far, fg_own]))
    decoded = jnp.where(
        core == 0, jnp.stack([dec_own, dec_far], axis=1), jnp.stack([dec_far, dec_own], axis=1)
    )
    totals = jnp.concatenate([tot1, tot2, tot3, tot4])
    totals = totals + swap_cores(totals)
    dec_totals = lax.dynamic_slice_in_dim(totals[6:10], core * half, half, 1)
    return (
        decoded,
        bands.reshape(2, band_rows, width, in_chan),
        enc1_grad.reshape(3, 3, in_chan, half),
        totals[1],
        totals[0],
        enc2_grad.reshape(3, 3, chans, half),
        totals[3],
        totals[2],
        att1_grad,
        totals[5],
        totals[4],
        att_grad,
        dec1_grad.reshape(3, 3, half, chans),
        dec_totals[1],
        dec_totals[0],
        dec2_grad.reshape(3, 3, half, chans),
        dec_totals[3],
        dec_totals[2],
    )


def solution(mesh):
    return jax.shard_map(
        shards,
        mesh=mesh,
        in_specs=(
            P("dp", "row", None, None),
            P(),
            P(),
            P(),
            P(),
            P(),
            P(),
            P(),
            P(),
            P(),
            P(),
            P(None, None, "row", None),
            P("row"),
            P("row"),
            P(None, None, "row", None),
            P("row"),
            P("row"),
            P("dp"),
            P("dp", None, None),
            P("row", "dp", None),
        ),
        out_specs=(
            P("row", "dp", None),
            P("dp", "row", None, None),
            P(None, None, None, "row"),
            P(),
            P(),
            P(None, None, None, "row"),
            P(),
            P(),
            P(None, None, "row"),
            P(),
            P(),
            P(None, None, "row"),
            P(None, None, "row", None),
            P("row"),
            P("row"),
            P(None, None, "row", None),
            P("row"),
            P("row"),
        ),
        check_vma=False,
    )
```

```python
import functools
import math

import jax
import jax.numpy as jnp
from jax import lax
from jax.experimental import pallas as pl
from jax.experimental.pallas import tpu as pltpu
from jax.sharding import PartitionSpec as P

EPS = 1e-05
F32 = jnp.float32
BF16 = jnp.bfloat16
SLABS = 8
SENT = (2, 3, 6, 7)
KEPT = (0, 1, 4, 5)
MIB = 2**20


def dot(left, right):
    return jnp.dot(left, right, preferred_element_type=F32)


def dot_nt(left, right):
    return lax.dot_general(left, right, (((1,), (1,)), ((), ())), preferred_element_type=F32)


def slope(act):
    sig = jax.nn.sigmoid(act)
    return sig * (1.0 + act * (1.0 - sig))


def silu(act):
    return act * jax.nn.sigmoid(act)


def clear_rims(buf, width):
    rows, lanes = buf.shape
    rim = jnp.zeros((width, lanes), BF16)
    buf[0:width, :] = rim
    buf[rows - width : rows, :] = rim


def fill(buf, value, width, lane, step):
    pixels, chans = value.shape
    col = lax.broadcasted_iota(jnp.int32, (pixels, 1), 0) & (width - 1)
    before = jnp.where(col == 0, 0.0, pltpu.roll(value, 1, 0))
    after = jnp.where(col == width - 1, 0.0, pltpu.roll(value, pixels - 1, 0))
    for at, part in enumerate((before, value, after)):
        start = lane + at * step
        buf[width : width + pixels, start : start + chans] = part.astype(BF16)


def conv(buf, weights, pixels, width, apart=None):
    total, lane = None, 0
    for ref in weights:
        depth = ref.shape[1]
        for i in range(3):
            taps = apart[0] if apart is not None and i == 0 else ref[i]
            term = dot(buf[i * width : i * width + pixels, lane : lane + depth], taps)
            total = term if total is None else total + term
        lane += depth
    return total


def shifted(buf, i, j, pixels, width, chans):
    return buf[(2 - i) * width : (2 - i) * width + pixels, (2 - j) * chans : (3 - j) * chans]


def conv_back(buf, weights, pixels, width):
    chans = weights[0].shape[2]
    depth = weights[0].shape[1] // 3
    total = None
    for i in range(3):
        for j in range(3):
            taps = [ref[i, j * depth : (j + 1) * depth, :] for ref in weights]
            taps = taps[0] if len(taps) == 1 else jnp.concatenate(taps, axis=0)
            term = dot_nt(shifted(buf, i, j, pixels, width, chans), taps)
            total = term if total is None else total + term
    return total


def put_sums(ref, terms):
    for at, term in enumerate(terms):
        row = jnp.sum(term, axis=0, keepdims=True)
        ref[:, at : at + 1, :] = jnp.broadcast_to(row[None], (ref.shape[0], 1, ref.shape[2]))
    ref.flush()


def gather_sums(ref):
    return jnp.sum(ref[...], axis=0)


def moments(ref, at, count):
    total = gather_sums(ref)
    mean = total[at : at + 1] / count
    square = total[at + 1 : at + 2] / count
    return mean, lax.rsqrt(square - mean * mean + EPS)


def normed(pre, mom):
    return (pre.astype(F32) - mom[0]) * mom[1]


def norm_back(grad, pre, mom, gain, total, at, count):
    xhat = normed(pre, mom)
    return (gain * mom[1]) * (
        grad.astype(F32) - total[at : at + 1] / count - xhat * (total[at + 1 : at + 2] / count)
    )


def row_of(ref):
    return ref[...].reshape(1, -1)


def half_at(ids, other, half, which=0):
    side = ids[which]
    if other:
        side = 1 - side
    return pl.ds(pl.multiple_of(side * half, half), half)


CORES = ((0, False), (0, False), (0, True), (0, True))
PLACES = ((2, False), (2, True), (3, False), (3, True))


def deal(refs, at, flat, ids, plan):
    half = flat.shape[1] // 2
    for ref, (which, other) in zip(refs, plan, strict=True):
        part = flat[:, half_at(ids, other, half, which)]
        if at is None:
            ref[...] = part
        else:
            ref[at] = part


def enc_one_kernel(width, ids, own, far, w_ref, pre_ref, sum_ref, flat, buf):
    pixels, chans = flat.shape
    band = pixels // 2
    side = ids[0]
    flat[half_at(ids, False, band), :] = own[side].astype(F32)
    flat[half_at(ids, True, band), :] = far[side].astype(F32)
    clear_rims(buf, width)
    fill(buf, flat[...], width, 0, chans)
    pre = conv(buf, (w_ref,), pixels, width)
    pre_ref[...] = pre
    pre_ref.flush()
    put_sums(sum_ref, (pre, pre * pre))


def enc_two_kernel(
    width, count, ids, labels, st1, pre1, gain1, bias1, aw_ref, w_first, w_ref,
    hid_own, hid_next, hid_core, hid_cross, pre2_ref, att_ref, sum_ref, flat, buf,
):
    pixels, chans = pre1.shape
    mom = moments(st1, 0, count)
    hidden = silu(normed(pre1[...], mom) * row_of(gain1) + row_of(bias1))
    clear_rims(buf, width)
    fill(buf, hidden, width, 0, chans)
    flat[...] = hidden
    hids = (hid_own, hid_next, hid_core, hid_cross)
    deal(hids, None, flat, ids, PLACES)
    for ref in hids:
        ref.flush()
    att = dot(hidden.astype(BF16), aw_ref[...])
    att_ref[...] = att
    att_ref.flush()
    pre = conv(buf, (w_ref,), pixels, width, w_first)
    pre2_ref[...] = pre
    pre2_ref.flush()
    put_sums(sum_ref, (pre, pre * pre, att, att * att))


def dec_one_kernel(
    width, count, ids, labels, st2, pre2, att_pre, gain2, bias2, gain_a, bias_a, aw_ref, mask, w_own, w_far,
    own, following, core, cross, shared_ref, gate_ref, pre3_ref, sum_ref, flat, hid, buf,
):
    pixels, chans = pre2.shape
    half = chans // 2
    shared = silu(normed(pre2[...], moments(st2, 0, count)) * row_of(gain2) + row_of(bias2))
    shared_ref[...] = shared
    shared_ref.flush()
    hid[...] = silu(normed(att_pre[...], moments(st2, 2, count)) * row_of(gain_a) + row_of(bias_a))
    gate = jax.nn.sigmoid(dot(hid[...].astype(BF16), aw_ref[...]))
    gate_ref[...] = gate
    gate_ref.flush()
    flat[...] = gate * shared * mask[...]
    clear_rims(buf, width)
    for other in (False, True):
        fill(buf, flat[:, half_at(ids, other, half)], width, 3 * half * other, half)
    parts = (own, following, core, cross)
    deal(parts, 0, flat, ids, CORES)
    deal(parts, 1, hid, ids, PLACES)
    for ref in parts:
        ref.flush()
    pre = conv(buf, (w_own, w_far), pixels, width)
    pre3_ref[...] = pre
    pre3_ref.flush()
    put_sums(sum_ref, (pre, pre * pre))


def dec_two_kernel(
    width, count, ids, st3, pre3, params, w_own, w_far, pre4_ref, sum_ref, keep_ref, send_ref, flat, buf
):
    pixels, chans = pre3.shape
    half = chans // 2
    flat[...] = silu(normed(pre3[...], moments(st3, 0, count)) * params[0:1, :] + params[1:2, :])
    clear_rims(buf, width)
    for other, ref in ((False, keep_ref), (True, send_ref)):
        part = flat[:, half_at(ids, other, half)]
        fill(buf, part, width, 3 * half * other, half)
        ref[...] = part.astype(BF16)
        ref.flush()
    pre = conv(buf, (w_own, w_far), pixels, width)
    pre4_ref[...] = pre
    pre4_ref.flush()
    put_sums(sum_ref, (pre, pre * pre))


def turn_kernel(ids, og_own, og_far, cot_ref, flat):
    half = flat.shape[1] // 2
    flat[:, half_at(ids, False, half)] = og_own[...].astype(F32).T
    flat[:, half_at(ids, True, half)] = og_far[...].astype(F32).T
    cot_ref[...] = flat[...]


def top_kernel(count, ids, st4, pre4, params, cot, dact_ref, sum_ref):
    xhat = normed(pre4[...], moments(st4, 0, count))
    dact = cot[...].astype(F32) * slope(xhat * params[2:3, :] + params[3:4, :])
    put_sums(sum_ref, (dact, dact * xhat))
    dact_ref[...] = dact


def decode_kernel(count, ids, st4, pre4, params, keep_ref, send_ref, out):
    half = out.shape[1] // 2
    out[...] = silu(normed(pre4[...], moments(st4, 0, count)) * params[2:3, :] + params[3:4, :])
    for other, ref in ((False, keep_ref), (True, send_ref)):
        ref[...] = out[:, half_at(ids, other, half)].T


def dec_two_back_kernel(
    width, count, ids, st4, st4b, pre4, dact4, params, w_own, w_far, st3, pre3,
    dz_own, dz_next, dz_core, dz_cross, dact_ref, sum_ref, tot_ref, flat, dz_flat, buf,
):
    pixels, chans = pre4.shape
    half = chans // 2
    total = gather_sums(st4b)
    tot_ref[...] = total
    tot_ref.flush()
    dz = norm_back(dact4[...], pre4[...], moments(st4, 0, count), params[2:3, :], total, 0, count)
    dz_flat[...] = dz
    parts = (dz_own, dz_next, dz_core, dz_cross)
    deal(parts, None, dz_flat, ids, PLACES)
    for ref in parts:
        ref.flush()
    clear_rims(buf, width)
    fill(buf, dz, width, 0, chans)
    back = conv_back(buf, (w_own, w_far), pixels, width)
    flat[:, half_at(ids, False, half)] = back[:, :half]
    flat[:, half_at(ids, True, half)] = back[:, half:]
    xhat = normed(pre3[...], moments(st3, 0, count))
    dact = flat[...] * slope(xhat * params[0:1, :] + params[1:2, :])
    dact_ref[...] = dact
    dact_ref.flush()
    put_sums(sum_ref, (dact, dact * xhat))


def dec_one_back_kernel(
    width, count, ids, labels, st3, st3b, pre3, dact3, params, w_own, w_far, mask, gate_ref, shared_ref, aw_ref,
    st2, att_pre, pre2, gain_a, bias_a, gain2, bias2,
    own, following, core, cross, datt_ref, dact2_ref, sum_ref, tot_ref, flat, dlog, dz_flat, buf,
):
    pixels, chans = pre3.shape
    half = chans // 2
    total = gather_sums(st3b)
    tot_ref[...] = total
    tot_ref.flush()
    dz = norm_back(dact3[...], pre3[...], moments(st3, 0, count), params[0:1, :], total, 0, count)
    dz_flat[...] = dz
    parts = (own, following, core, cross)
    deal(parts, 0, dz_flat, ids, PLACES)
    clear_rims(buf, width)
    fill(buf, dz, width, 0, chans)
    back = conv_back(buf, (w_own, w_far), pixels, width)
    flat[:, half_at(ids, False, half)] = back[:, :half]
    flat[:, half_at(ids, True, half)] = back[:, half:]
    grad = (flat[...] * mask[...]).astype(BF16).astype(F32)
    gate = gate_ref[...].astype(F32)
    dlog[...] = grad * shared_ref[...].astype(F32) * gate * (1.0 - gate)
    deal(parts, 1, dlog, ids, CORES)
    for ref in parts:
        ref.flush()
    dhid = dot_nt(dlog[...].astype(BF16), aw_ref[...])
    att_hat = normed(att_pre[...], moments(st2, 2, count))
    datt = dhid * slope(att_hat * row_of(gain_a) + row_of(bias_a))
    datt_ref[...] = datt
    datt_ref.flush()
    xhat2 = normed(pre2[...], moments(st2, 0, count))
    dact2 = grad * gate * slope(xhat2 * row_of(gain2) + row_of(bias2))
    dact2_ref[...] = dact2
    dact2_ref.flush()
    put_sums(sum_ref, (dact2, dact2 * xhat2, datt, datt * att_hat))


def enc_two_back_kernel(
    width, count, ids, labels, st2, st2b, att_pre, datt_ref, gain_a, pre2, dact2, gain2, aw_ref, w_ref,
    st1, pre1, gain1, bias1,
    own, core, dact_ref, sum_ref, tot_ref, flat, datt, buf,
):
    pixels, chans = pre2.shape
    total = gather_sums(st2b)
    tot_ref[...] = total
    tot_ref.flush()
    dz = norm_back(dact2[...], pre2[...], moments(st2, 0, count), row_of(gain2), total, 0, count)
    flat[...] = dz
    deal((own, core), 0, flat, ids, CORES[1:3])
    clear_rims(buf, width)
    fill(buf, dz, width, 0, chans)
    datt[...] = norm_back(
        datt_ref[...], att_pre[...], moments(st2, 2, count), row_of(gain_a), total, 2, count
    )
    deal((own, core), 1, datt, ids, CORES[1:3])
    own.flush()
    core.flush()
    dhid = dot_nt(datt[...].astype(BF16), aw_ref[...])
    dhid = dhid + conv_back(buf, (w_ref,), pixels, width)
    xhat = normed(pre1[...], moments(st1, 0, count))
    dact = dhid * slope(xhat * row_of(gain1) + row_of(bias1))
    dact_ref[...] = dact
    dact_ref.flush()
    put_sums(sum_ref, (dact, dact * xhat))


def enc_one_back_kernel(
    width, count, ids, st1, st1b, pre1, dact1, gain1, w_ref, dz_keep, dz_send, fg_keep, fg_send, tot_ref, flat, back, buf
):
    pixels, chans = pre1.shape
    half = chans // 2
    total = gather_sums(st1b)
    tot_ref[...] = total
    tot_ref.flush()
    dz = norm_back(dact1[...], pre1[...], moments(st1, 0, count), row_of(gain1), total, 0, count)
    flat[...] = dz
    for other, ref in ((False, dz_keep), (True, dz_send)):
        ref[...] = flat[:, half_at(ids, other, half)].astype(BF16)
        ref.flush()
    clear_rims(buf, width)
    fill(buf, dz, width, 0, chans)
    back[...] = conv_back(buf, (w_ref,), pixels, width)
    for other, ref in ((False, fg_keep), (True, fg_send)):
        ref[...] = back[half_at(ids, other, pixels // 2), :]


def lay_rows(ids, value, at, tmp, turned):
    rows = turned.shape[1]
    part = rows // SLABS
    tmp[at] = value.astype(F32).T.astype(BF16)
    for slot, t in enumerate(KEPT + SENT):
        start = pl.multiple_of((ids[1] ^ t) * part, part)
        turned[at, slot * part : (slot + 1) * part, :] = tmp[at, pl.ds(start, part), :]


def store_slabs(pieces, row, part, value):
    low = value.astype(BF16)
    for kept, sent in pieces:
        if row < kept.shape[1]:
            break
        row -= kept.shape[1]
    for slot in range(SLABS):
        ref, at = (kept, slot) if slot < SLABS // 2 else (sent, slot - SLABS // 2)
        ref[at, row : row + part, :] = low[slot * part : (slot + 1) * part]


def conv_weights(ids, width, values, grads, pieces, tmp, turned, bufs):
    count, _, pixels = turned.shape
    chans = bufs.shape[2] // 3
    part = turned.shape[1] // SLABS
    for at in range(count):
        lay_rows(ids, values[at](), at, tmp, turned)
        clear_rims(bufs.at[at], width)
        fill(bufs.at[at], grads[at]().astype(F32), width, 0, chans)
    for i in range(3):
        for j in range(3):
            total = None
            for at in range(count):
                term = dot(turned[at], shifted(bufs.at[at], i, j, pixels, width, chans))
                total = term if total is None else total + term
            store_slabs(pieces, (3 * i + j) * part, part, total)


def task_weights(marks, tasks, turned, grads, pieces):
    part = turned.shape[1] // SLABS
    terms = [dot(turned[at], grad()) for at, grad in enumerate(grads)]
    for task in range(tasks):
        total = None
        for mark, term in zip(marks, terms, strict=True):
            term = term * (mark == task).astype(F32)
            total = term if total is None else total + term
        store_slabs(pieces, (9 + task) * part, part, total)


def frame_marks(ids, labels, labels_next):
    side = ids[0]
    return labels[side], labels[1 - side], labels_next[side], labels_next[1 - side]


def pairs_of(refs):
    return [refs[k : k + 2] for k in range(0, len(refs), 2)]


def whole_of(ref):
    return lambda: ref[...]


def layer_of(ref, k):
    return lambda: ref[k]


def grad_dec_two_kernel(width, ids, *refs):
    kept, sent, tmp, turned, bufs = refs[8:]
    values, grads = [whole_of(r) for r in refs[:4]], [whole_of(r) for r in refs[4:8]]
    conv_weights(ids, width, values, grads, ((kept, sent),), tmp, turned, bufs)


def grad_dec_one_kernel(width, tasks, ids, labels, labels_next, *refs):
    values, grads = refs[:4], refs[4:8]
    pieces = pairs_of(refs[8:-5])
    tmp, turned, tmp_att, turned_att, bufs = refs[-5:]
    conv_weights(
        ids, width, [layer_of(r, 0) for r in values], [layer_of(r, 0) for r in grads],
        pieces, tmp, turned, bufs,
    )
    for at in range(4):
        lay_rows(ids, values[at][1], at, tmp_att, turned_att)
    marks = frame_marks(ids, labels, labels_next)
    task_weights(marks, tasks, turned_att, [layer_of(r, 1) for r in grads], pieces)


def grad_enc_two_kernel(width, tasks, ids, labels, labels_next, *refs):
    values, grads = refs[:4], refs[4:8]
    pieces = pairs_of(refs[8:-3])
    tmp, turned, bufs = refs[-3:]
    conv_weights(
        ids, width, [whole_of(r) for r in values], [layer_of(r, 0) for r in grads],
        pieces, tmp, turned, bufs,
    )
    marks = frame_marks(ids, labels, labels_next)
    task_weights(marks, tasks, turned, [layer_of(r, 1) for r in grads], pieces)


def grad_enc_one_kernel(width, ids, own, far, own_next, far_next, *refs):
    grads = [whole_of(r) for r in refs[:4]]
    kept, sent, flat, tmp, turned, bufs = refs[4:]
    band, chans = flat.shape[1] // 2, flat.shape[2]
    side = ids[0]

    def frame(at, near_band, far_band, which):
        def read():
            flat[at, half_at(ids, False, band), :] = near_band[which].astype(F32)
            flat[at, half_at(ids, True, band), :] = far_band[which].astype(F32)
            return flat[at, :, half_at(ids, False, chans // 2, 2)]

        return read

    values = [
        frame(0, own, far, side),
        frame(1, own, far, 1 - side),
        frame(2, own_next, far_next, side),
        frame(3, own_next, far_next, 1 - side),
    ]
    conv_weights(ids, width, values, grads, ((kept, sent),), tmp, turned, bufs)


def spread_kernel(by_lanes, slots, ids, *refs):
    n_pieces = len(slots)
    outs = refs[2 * n_pieces :]
    base = 0
    for out, lanes_too in zip(outs, (by_lanes, False), strict=False):
        layers, rows, lanes = out.shape
        split = lanes // 2 if lanes_too else lanes
        height = rows if lanes_too else rows // 2
        part = height // SLABS
        for layer in range(layers):
            line, piece = base + layer * part, 0
            while line >= refs[piece].shape[1]:
                line -= refs[piece].shape[1]
                piece += 1
            for other in (False, True):
                ref = refs[n_pieces + piece] if other else refs[piece]
                side = 1 - ids[2] if other else ids[2]
                for at, t in enumerate(slots[piece]):
                    start = (ids[1] ^ t) * part
                    if not lanes_too:
                        start = start + side * height
                    where = pl.ds(pl.multiple_of(start, part), part)
                    span = pl.ds(pl.multiple_of(side * split, split), split) if lanes_too else slice(None)
                    out[layer, where, span] = ref[at, line : line + part, :].astype(F32)
            out.flush(layer)
        base += layers * part


def arr(shape, kind=F32):
    return jax.ShapeDtypeStruct(shape, kind)


class Source:
    def __init__(self, pieces, buf):
        self.pieces, self.buf, self.shape = pieces, buf, buf.shape
        self.waiting = [True] * len(pieces)

    def start(self):
        for piece, wanted in zip(self.pieces, self.waiting, strict=True):
            if wanted:
                piece.start()

    def __getitem__(self, at):
        first = at[0] if isinstance(at, tuple) else at
        cut_one = len(self.pieces) > 1 and isinstance(first, int)
        for k in [first] if cut_one else range(len(self.pieces)):
            if self.waiting[k]:
                self.pieces[k].wait()
                self.waiting[k] = False
        return self.buf[at]

    def finish(self):
        for k, piece in enumerate(self.pieces):
            if self.waiting[k]:
                piece.wait()


class Target:
    def __init__(self, pieces, buf):
        self.pieces, self.buf, self.shape = pieces, buf, buf.shape
        self.sent = [False] * len(pieces)

    def __setitem__(self, at, value):
        self.buf[at] = value.astype(self.buf.dtype)

    def __getitem__(self, at):
        return self.buf[at]

    def flush(self, k=0):
        if k < len(self.pieces) and not self.sent[k]:
            self.pieces[k].start()
            self.sent[k] = True

    def finish(self):
        for k, piece in enumerate(self.pieces):
            self.flush(k)
        for piece in self.pieces:
            piece.wait()


def near(array):
    return array, "near"


def far(array):
    return array, "far"


def cut(array):
    return array, "cut"


def rest(array):
    return array, "rest"


def pick(array):
    return array, "pick"


def both(array):
    return array, "both"


def held(array, kind):
    return pltpu.with_memory_space_constraint(array, pltpu.VMEM if kind == "near" else pltpu.HBM)


def call(body, name, scalars, args, outs, scratch=(), flops=0):
    smem, vmem = pl.BlockSpec(memory_space=pltpu.SMEM), pl.BlockSpec(memory_space=pltpu.VMEM)
    hbm = pl.BlockSpec(memory_space=pltpu.HBM)
    moved = sum(a.size * a.dtype.itemsize for a, _ in list(args) + list(outs))
    arrays = list(args) + list(outs)
    pieces = [a.shape[0] if kind in ("cut", "rest") else 1 for a, kind in arrays]
    kinds = [kind for _, kind in arrays]
    bufs = [
        pltpu.VMEM(a.shape[1:] if kind == "pick" else a.shape, a.dtype)
        for a, kind in arrays
        if kind not in ("near", "both")
    ]
    places, shapes = [], []
    for a, kind in outs:
        if kind in ("near", "both"):
            places.append(vmem)
            shapes.append(pltpu.VMEM(a.shape, a.dtype))
        if kind != "near":
            places.append(hbm)
            shapes.append(pltpu.HBM(a.shape, a.dtype))
    held_bytes = sum(jnp.dtype(b.dtype).itemsize * math.prod(b.shape) for b in bufs + list(scratch))
    n_sems = max(1, sum(p for p, kind in zip(pieces, kinds, strict=True) if kind != "near"))

    def kernel(*refs):
        refs = list(refs)

        def take(count):
            taken = refs[:count]
            del refs[:count]
            return taken

        given = take(len(scalars))
        ins, results = take(len(args)), take(len(shapes))
        local, (sems,) = take(len(bufs)), take(1)
        items, slot = [], 0
        for k, kind in enumerate(kinds):
            is_out = k >= len(args)
            if kind == "near":
                items.append(Target((), results.pop(0)) if is_out else ins[k])
                continue
            inside = results.pop(0) if kind == "both" else local.pop(0)
            outside = results.pop(0) if is_out else ins[k]
            if kind == "pick":
                outside = outside.at[given[1][given[0][0]]]
            copies = []
            for piece in range(pieces[k]):
                apart = kind in ("cut", "rest")
                ends = (outside.at[piece], inside.at[piece]) if apart else (outside, inside)
                left, right = reversed(ends) if is_out else ends
                copies.append(pltpu.make_async_copy(left, right, sems.at[slot]))
                slot += 1
            items.append((Target if is_out else Source)(copies, inside))
            if kind == "rest":
                items[-1].waiting[0] = False
        for item in items:
            if isinstance(item, Source):
                item.start()
        body(*given, *items, *refs)
        for item in items:
            if isinstance(item, (Source, Target)):
                item.finish()

    return pl.pallas_call(
        kernel,
        out_shape=shapes,
        in_specs=[smem] * len(scalars) + [vmem if kind == "near" else hbm for _, kind in args],
        out_specs=places,
        scratch_shapes=bufs + [pltpu.SemaphoreType.DMA((n_sems,))] + list(scratch),
        name=name,
        compiler_params=pltpu.CompilerParams(vmem_limit_bytes=held_bytes + 8 * MIB),
        cost_estimate=pl.CostEstimate(flops=flops, bytes_accessed=moved, transcendentals=0),
    )(*scalars, *[held(a, kind) for a, kind in args])


def fetch_kernel(source, target, sems):
    copies = [pltpu.make_async_copy(source.at[k], target.at[k], sems.at[k]) for k in range(target.shape[0])]
    for copy in copies:
        copy.start()
    for copy in copies:
        copy.wait()


def fetch(weight, count):
    shape = (count,) + weight.shape[1:]
    return pl.pallas_call(
        fetch_kernel,
        out_shape=pltpu.VMEM(shape, weight.dtype),
        in_specs=[pl.BlockSpec(memory_space=pltpu.HBM)],
        out_specs=pl.BlockSpec(memory_space=pltpu.VMEM),
        scratch_shapes=[pltpu.SemaphoreType.DMA((count,))],
        name="fetch",
        compiler_params=pltpu.CompilerParams(vmem_limit_bytes=MIB),
        cost_estimate=pl.CostEstimate(flops=0, bytes_accessed=4 * math.prod(shape), transcendentals=0),
    )(held(weight, "far"))


def swap_cores(value):
    return lax.ppermute(value, "row", [(0, 1), (1, 0)])


def exchange(value, masks):
    count, cores = lax.axis_size("dp"), lax.axis_size("row")
    pairs = [
        (d * cores + r, (d ^ masks[r]) * cores + r) for d in range(count) for r in range(cores)
    ]
    return lax.ppermute(value, ("dp", "row"), pairs)


FIRST, SECOND, Z_NEAR, Z_FAR = (1, 2), (2, 1), (4, 4), (8, 8)


def cross(value):
    count = lax.axis_size("dp")
    pairs = [(d * 2 + r, (d ^ FIRST[1 - r]) * 2 + 1 - r) for d in range(count) for r in range(2)]
    return lax.ppermute(value, ("dp", "row"), pairs)


def dealt(to_next, to_core, to_cross):
    return swap_cores(to_core), exchange(to_next, FIRST), cross(to_cross)


def add(left, right):
    return (left.astype(F32) + right.astype(F32)).astype(BF16)


class Piece:
    def __init__(self, slabs, gather):
        kept, sent = slabs
        self.gather = (SECOND, Z_NEAR) if gather == "second" else (Z_NEAR, SECOND)
        self.slots = range(SLABS) if gather == "second" else KEPT + SENT
        self.low, self.high, self.state = kept[:2], kept[2:], 0
        self.coming = exchange(sent, SECOND)

    def step(self, order):
        got = order.after(self.coming)
        if self.state == 0:
            self.low = add(self.low, got[:2])
            self.coming = exchange(add(self.high, got[2:]), Z_NEAR)
        elif self.state == 1:
            self.low = add(self.low, got)
            self.coming = exchange(self.low, Z_FAR)
        elif self.state == 2:
            self.low = add(self.low, jnp.concatenate([got[1:], got[:1]]))
            bit = 16
            while bit < lax.axis_size("dp"):
                self.low = add(self.low, exchange(self.low, (bit, bit)))
                bit *= 2
            self.coming = exchange(self.low, self.gather[0])
        elif self.state < 5:
            self.low = jnp.concatenate([self.low, got])
            self.coming = exchange(self.low, (self.gather[1], FIRST)[self.state - 3])
        else:
            self.far_half = got
        self.state += 1
        order.done(self.low if self.state < 6 else got)


B_PARTS, C_PARTS = 2, 2
GATHER = {"a": "z", "b": "z", "c": "z", "d": "z"}
MIDDLE = "baB"
TAIL = "bBcCabdBcbCaBdcbBCcbdCBcdC12cdC3d4"


class Order:
    def __init__(self):
        self.last = None

    def after(self, value):
        return value if self.last is None else tie(self.last, value)[1]

    def done(self, value):
        self.last = value


def tie(*values):
    return lax.optimization_barrier(values)


def spread(ids, pieces, outs, by_lanes, name):
    parts = [far(p.low) for p in pieces] + [far(p.far_half) for p in pieces]
    return call(
        functools.partial(spread_kernel, by_lanes, [p.slots for p in pieces]), name, (ids,), parts,
        [cut(o) for o in outs],
    )


def all_sums(value):
    return lax.all_to_all(value, "dp", 0, 0, tiled=False)


def shards(
    frames,
    enc_w1,
    enc_gain1,
    enc_bias1,
    enc_w2,
    enc_gain2,
    enc_bias2,
    att_w1,
    att_gain,
    att_bias,
    att_w,
    dec_w1,
    dec_gain1,
    dec_bias1,
    dec_w2,
    dec_gain2,
    dec_bias2,
    labels,
    pool_index,
    out_grad,
):
    band_rows, width, in_chan = frames.shape[1:]
    chans = enc_w1.shape[3]
    half = dec_w1.shape[2]
    height = 2 * pool_index.shape[1]
    pixels = height * width
    band = band_rows * width
    tasks = att_w.shape[0]
    n_dp = lax.axis_size("dp")
    count = float(pixels * n_dp)
    core = lax.axis_index("row")
    chip = lax.axis_index("dp")
    bit_x, bit_y = chip & 1, (chip >> 1) & 1
    first = jnp.where(core == 0, bit_x, bit_y)
    second = jnp.where(core == 0, bit_y, bit_x)
    place = 4 * ((chip >> 2) & 1) + 2 * second + ((chip >> 3) & 1)
    ids = jnp.stack([core, place, first, second]).astype(jnp.int32)

    own_bands = frames.reshape(2, band, in_chan)
    far_bands, w_one, w_two = tie(
        swap_cores(own_bands), dec_w1.reshape(3, 3 * half, chans), dec_w2.reshape(3, 3 * half, chans)
    )
    d1_own, d2_own = w_one, w_two
    d1_far = swap_cores(d1_own)
    d2_far = swap_cores(d2_own)
    index = lax.dynamic_index_in_dim(pool_index, core, 0, keepdims=False)
    index = jnp.repeat(jnp.repeat(index, 2, axis=0), 2, axis=1)
    cell = 2 * (jnp.arange(height)[:, None] % 2) + jnp.arange(width)[None, :] % 2
    mask = (index == cell).astype(F32).reshape(pixels, 1)
    e1 = enc_w1.reshape(3, 3 * in_chan, chans)
    e2 = enc_w2.reshape(3, 3 * chans, chans)

    full = arr((pixels, chans), BF16)
    part = arr((pixels, half), BF16)
    pair = arr((2, pixels, half), BF16)
    two = arr((n_dp, 2, chans))
    four = arr((n_dp, 4, chans))
    flat = pltpu.VMEM((pixels, chans), F32)
    buf = pltpu.VMEM((pixels + 2 * width, 3 * chans), BF16)
    work = 2 * pixels * 9 * chans * chans

    pre1, sums = call(
        functools.partial(enc_one_kernel, width), "enc_one", (ids,),
        [far(own_bands), far(far_bands), near(fetch(e1, 3))], [far(full), near(two)],
        (pltpu.VMEM((pixels, in_chan), F32), pltpu.VMEM((pixels + 2 * width, 3 * in_chan), BF16)), work // 2,
    )
    sums, w_near, labels_then, out_then, bands_then, far_then, *vectors = tie(
        sums, e2, labels, out_grad, own_bands, far_bands, dec_gain1, dec_bias1, dec_gain2, dec_bias2
    )
    st1 = all_sums(sums)
    params_own = jnp.stack(vectors)
    params_far = swap_cores(params_own)
    params = jnp.where(
        core == 0,
        jnp.concatenate([params_own, params_far], axis=1),
        jnp.concatenate([params_far, params_own], axis=1),
    )
    labels_next = exchange(labels_then, FIRST)
    own_next, far_next = exchange(bands_then, FIRST), exchange(far_then, FIRST)
    og_own = lax.dynamic_index_in_dim(out_then, core, 1, keepdims=False)
    og_far = swap_cores(lax.dynamic_index_in_dim(out_then, 1 - core, 1, keepdims=False))
    hid1_own, hid1_next, hid1_core, hid1_cross, pre2, att_pre, sums = call(
        functools.partial(enc_two_kernel, width, count), "enc_two", (ids, labels),
        [near(st1), far(pre1), near(enc_gain1), near(enc_bias1), pick(att_w1), near(fetch(w_near, 1)), rest(e2)],
        [far(part)] * 4 + [far(full), far(full), near(four)], (flat, buf), work,
    )
    sums, w_own = tie(sums, d1_own)
    st2 = all_sums(sums)
    hid1_far = dealt(hid1_next, hid1_core, hid1_cross)
    up_own, up_next, up_core, up_cross, shared, gate, pre3, sums = call(
        functools.partial(dec_one_kernel, width, count), "dec_one", (ids, labels),
        [near(st2), far(pre2), far(att_pre), near(enc_gain2), near(enc_bias2), near(att_gain), near(att_bias),
         pick(att_w), near(mask), near(fetch(w_own, 3)), cut(d1_far)],
        [far(pair)] * 4 + [far(full), far(full), far(full), near(two)], (flat, flat, buf), work,
    )
    sums, w_own = tie(sums, d2_own)
    st3 = all_sums(sums)
    up_far = dealt(up_next, up_core, up_cross)
    pre4, sums, hidden3_own, hidden3_send = call(
        functools.partial(dec_two_kernel, width, count), "dec_two", (ids,),
        [near(st3), far(pre3), near(params), near(fetch(w_own, 3)), cut(d2_far)],
        [near(full), near(two), far(part), far(part)], (flat, buf), work,
    )
    sums, og_own, og_far = tie(sums, og_own, og_far)
    st4, hid1_far, labels_next = tie(all_sums(sums), hid1_far, labels_next)
    (cot,) = call(turn_kernel, "turn", (ids,), [far(og_own), far(og_far)], [near(full)], (flat,))
    hid3_far = dealt(hidden3_own, hidden3_send, hidden3_send)
    turned = arr((half, pixels), BF16)
    dact4, sums = call(
        functools.partial(top_kernel, count), "top", (ids,),
        [near(st4), near(pre4), near(params), near(cot)], [near(full), near(two)],
    )
    st4b = all_sums(sums)
    sums_done, pre4_again = tie(sums, pre4)
    dec_own, dec_send = call(
        functools.partial(decode_kernel, count), "decode", (ids,),
        [near(st4), near(pre4_again), near(params)], [far(turned), far(turned)], (flat,),
    )
    st4b, up_far, own_next, far_next, dec_own = tie(st4b, up_far, own_next, far_next, dec_own)
    dec_far = swap_cores(dec_send)
    dz4_own, dz4_next, dz4_core, dz4_cross, dact3, sums, tot4 = call(
        functools.partial(dec_two_back_kernel, width, count), "dec_two_back", (ids,),
        [near(st4), near(st4b), near(pre4), near(dact4), near(params), cut(d2_own), cut(d2_far), near(st3),
         far(pre3)],
        [near(part)] + [far(part)] * 3 + [near(full), near(two), far(arr((2, chans)))], (flat, flat, buf), work,
    )
    dz4_far = dealt(dz4_next, dz4_core, dz4_cross)
    tmp = pltpu.VMEM((4, half, pixels), BF16)
    bufs = pltpu.VMEM((4, pixels + 2 * width, 3 * half), BF16)

    def slabs(rows):
        return [far(arr((SLABS // 2, rows, half), BF16))] * 2

    slab = half // SLABS
    a = call(
        functools.partial(grad_dec_two_kernel, width), "grad_dec_two", (ids,),
        [far(v) for v in (hidden3_own,) + hid3_far] + [near(dz4_own)] + [far(v) for v in dz4_far],
        slabs(9 * slab), (tmp, tmp, bufs), work,
    )
    st3b, a = tie(all_sums(sums), a)
    order = Order()
    a = Piece(a, GATHER["a"])
    dz3_own, dz3_next, dz3_core, dz3_cross, datt, dact2, sums, tot3 = call(
        functools.partial(dec_one_back_kernel, width, count), "dec_one_back", (ids, labels),
        [near(st3), near(st3b), far(pre3), near(dact3), near(params), cut(d1_own), cut(d1_far), near(mask),
         far(gate), far(shared), pick(att_w), near(st2), far(att_pre), far(pre2),
         near(att_gain), near(att_bias), near(enc_gain2), near(enc_bias2)],
        [far(pair)] * 4 + [near(full), near(full), near(four), far(arr((2, chans)))],
        (flat, flat, flat, buf), work,
    )
    order.done(tot3)
    st2b, dz3_next, dz3_core, dz3_cross = tie(all_sums(sums), dz3_next, dz3_core, dz3_cross)
    dz3_far = dealt(dz3_next, dz3_core, dz3_cross)
    order.done(st2b)
    a.step(order)
    dz2_own, dz2_core, dact1, sums, tot2 = call(
        functools.partial(enc_two_back_kernel, width, count), "enc_two_back", (ids, labels),
        [near(st2), near(st2b), far(att_pre), near(datt), near(att_gain), far(pre2), near(dact2),
         near(enc_gain2), pick(att_w1), cut(e2), near(st1), far(pre1), near(enc_gain1), near(enc_bias1)],
        [far(pair), far(pair), near(full), near(two), far(arr((4, chans)))],
        (flat, flat, buf), work,
    )
    order.done(tot2)
    dz2_far = dealt(dz2_own, dz2_core, dz2_core)
    a.step(order)
    rows = (9 + tasks) * slab
    b = call(
        functools.partial(grad_dec_one_kernel, width, tasks), "grad_dec_one", (ids, labels, labels_next),
        [far(v) for v in (order.after(up_own),) + up_far + (dz3_own,) + dz3_far],
        slabs(rows // B_PARTS) * B_PARTS, (tmp, tmp, tmp, tmp, bufs), work,
    )
    order.done(b)
    pieces = {"a": a}
    pieces.update(zip("bB", (Piece(pair, GATHER["b"]) for pair in pairs_of(b)), strict=False))
    st1b = order.after(all_sums(sums))
    band_grad = arr((band, in_chan))
    dz1_own, dz1_send, fg_own, fg_send, tot1 = call(
        functools.partial(enc_one_back_kernel, width, count), "enc_one_back", (ids,),
        [near(st1), near(st1b), far(pre1), near(dact1), near(enc_gain1), cut(e1)],
        [far(part), far(part), far(band_grad), far(band_grad), far(arr((2, chans)))],
        (flat, pltpu.VMEM((pixels, in_chan), F32), buf), work // 2,
    )
    order.done(tot1)
    dz1_far = dealt(dz1_own, dz1_send, dz1_send)
    a.step(order)
    c = call(
        functools.partial(grad_enc_two_kernel, width, tasks), "grad_enc_two", (ids, labels, labels_next),
        [far(v) for v in (order.after(hid1_own),) + hid1_far + (dz2_own,) + dz2_far],
        slabs(rows // C_PARTS) * C_PARTS, (tmp, tmp, bufs), work,
    )
    order.done(c)
    pieces.update(zip("cC", (Piece(pair, GATHER["c"]) for pair in pairs_of(c)), strict=False))
    for name in MIDDLE:
        pieces[name].step(order)
    low = pltpu.VMEM((4, in_chan // 2, pixels), BF16)
    d = call(
        functools.partial(grad_enc_one_kernel, width), "grad_enc_one", (ids,),
        [far(v) for v in (own_bands, far_bands, own_next, far_next, order.after(dz1_own)) + dz1_far],
        slabs(9 * slab // 2), (pltpu.VMEM((4, pixels, in_chan), F32), low, low, bufs), work // 2,
    )
    order.done(d)
    pieces["d"] = Piece(d, GATHER["d"])
    dec_shape, enc_shape, task_shape = arr((9, half, chans)), arr((9, chans, half)), arr((tasks, chans, half))
    results = {
        "1": ("a", (dec_shape,), True, "spread_dec_two"),
        "2": ("bB"[:B_PARTS], (dec_shape, task_shape), True, "spread_dec_one"),
        "3": ("cC"[:C_PARTS], (enc_shape, task_shape), False, "spread_enc_two"),
        "4": ("d", (arr((9, in_chan, half)),), False, "spread_enc_one"),
    }
    for name in TAIL:
        if name in pieces:
            pieces[name].step(order)
            continue
        names, shapes, by_lanes, title = results[name]
        results[name] = spread(order.after(ids), [pieces[n] for n in names], shapes, by_lanes, title)
        order.done(results[name][0])
    (dec2_grad,), (dec1_grad, att_grad) = results["1"], results["2"]
    (enc2_grad, att1_grad), (enc1_grad,) = results["3"], results["4"]

    fg_far = swap_cores(fg_send)
    bands = jnp.where(core == 0, jnp.stack([fg_own, fg_far]), jnp.stack([fg_far, fg_own]))
    decoded = jnp.where(
        core == 0, jnp.stack([dec_own, dec_far], axis=1), jnp.stack([dec_far, dec_own], axis=1)
    )
    totals = jnp.concatenate([tot1, tot2, tot3, tot4])
    totals = totals + swap_cores(totals)
    dec_totals = lax.dynamic_slice_in_dim(totals[6:10], core * half, half, 1)
    return (
        decoded,
        bands.reshape(2, band_rows, width, in_chan),
        enc1_grad.reshape(3, 3, in_chan, half),
        totals[1],
        totals[0],
        enc2_grad.reshape(3, 3, chans, half),
        totals[3],
        totals[2],
        att1_grad,
        totals[5],
        totals[4],
        att_grad,
        dec1_grad.reshape(3, 3, half, chans),
        dec_totals[1],
        dec_totals[0],
        dec2_grad.reshape(3, 3, half, chans),
        dec_totals[3],
        dec_totals[2],
    )


def solution(mesh):
    return jax.shard_map(
        shards,
        mesh=mesh,
        in_specs=(
            P("dp", "row", None, None),
            P(),
            P(),
            P(),
            P(),
            P(),
            P(),
            P(),
            P(),
            P(),
            P(),
            P(None, None, "row", None),
            P("row"),
            P("row"),
            P(None, None, "row", None),
            P("row"),
            P("row"),
            P("dp"),
            P("dp", None, None),
            P("row", "dp", None),
        ),
        out_specs=(
            P("row", "dp", None),
            P("dp", "row", None, None),
            P(None, None, None, "row"),
            P(),
            P(),
            P(None, None, None, "row"),
            P(),
            P(),
            P(None, None, "row"),
            P(),
            P(),
            P(None, None, "row"),
            P(None, None, "row", None),
            P("row"),
            P("row"),
            P(None, None, "row", None),
            P("row"),
            P("row"),
        ),
        check_vma=False,
    )
```

```python
import functools
import math

import jax
import jax.numpy as jnp
from jax import lax
from jax.experimental import pallas as pl
from jax.experimental.pallas import tpu as pltpu
from jax.sharding import PartitionSpec as P

EPS = 1e-05
F32 = jnp.float32
BF16 = jnp.bfloat16
SLABS = 8
SENT = (2, 3, 6, 7)
KEPT = (0, 1, 4, 5)
MIB = 2**20


def dot(left, right):
    return jnp.dot(left, right, preferred_element_type=F32)


def dot_nt(left, right):
    return lax.dot_general(left, right, (((1,), (1,)), ((), ())), preferred_element_type=F32)


def slope(act):
    sig = jax.nn.sigmoid(act)
    return sig * (1.0 + act * (1.0 - sig))


def silu(act):
    return act * jax.nn.sigmoid(act)


def clear_rims(buf, width):
    rows, lanes = buf.shape
    rim = jnp.zeros((width, lanes), BF16)
    buf[0:width, :] = rim
    buf[rows - width : rows, :] = rim


def fill(buf, value, width, lane, step):
    pixels, chans = value.shape
    col = lax.broadcasted_iota(jnp.int32, (pixels, 1), 0) & (width - 1)
    before = jnp.where(col == 0, 0.0, pltpu.roll(value, 1, 0))
    after = jnp.where(col == width - 1, 0.0, pltpu.roll(value, pixels - 1, 0))
    for at, part in enumerate((before, value, after)):
        start = lane + at * step
        buf[width : width + pixels, start : start + chans] = part.astype(BF16)


def conv(buf, weights, pixels, width, apart=None):
    total, lane = None, 0
    for ref in weights:
        depth = ref.shape[1]
        for i in range(3):
            taps = apart[0] if apart is not None and i == 0 else ref[i]
            term = dot(buf[i * width : i * width + pixels, lane : lane + depth], taps)
            total = term if total is None else total + term
        lane += depth
    return total


def shifted(buf, i, j, pixels, width, chans):
    return buf[(2 - i) * width : (2 - i) * width + pixels, (2 - j) * chans : (3 - j) * chans]


def conv_back(buf, weights, pixels, width):
    chans = weights[0].shape[2]
    depth = weights[0].shape[1] // 3
    total = None
    for i in range(3):
        for j in range(3):
            taps = [ref[i, j * depth : (j + 1) * depth, :] for ref in weights]
            taps = taps[0] if len(taps) == 1 else jnp.concatenate(taps, axis=0)
            term = dot_nt(shifted(buf, i, j, pixels, width, chans), taps)
            total = term if total is None else total + term
    return total


def put_sums(ref, terms):
    for at, term in enumerate(terms):
        row = jnp.sum(term, axis=0, keepdims=True)
        ref[:, at : at + 1, :] = jnp.broadcast_to(row[None], (ref.shape[0], 1, ref.shape[2]))
    ref.flush()


def gather_sums(ref):
    return jnp.sum(ref[...], axis=0)


def moments(ref, at, count):
    total = gather_sums(ref)
    mean = total[at : at + 1] / count
    square = total[at + 1 : at + 2] / count
    return mean, lax.rsqrt(square - mean * mean + EPS)


def normed(pre, mom):
    return (pre.astype(F32) - mom[0]) * mom[1]


def norm_back(grad, pre, mom, gain, total, at, count):
    xhat = normed(pre, mom)
    return (gain * mom[1]) * (
        grad.astype(F32) - total[at : at + 1] / count - xhat * (total[at + 1 : at + 2] / count)
    )


def row_of(ref):
    return ref[...].reshape(1, -1)


def half_at(ids, other, half, which=0):
    side = ids[which]
    if other:
        side = 1 - side
    return pl.ds(pl.multiple_of(side * half, half), half)


CORES = ((0, False), (0, False), (0, True), (0, True))
PLACES = ((2, False), (2, True), (3, False), (3, True))


def deal(refs, at, flat, ids, plan):
    half = flat.shape[1] // 2
    for ref, (which, other) in zip(refs, plan, strict=True):
        part = flat[:, half_at(ids, other, half, which)]
        if at is None:
            ref[...] = part
        else:
            ref[at] = part


def enc_one_kernel(width, ids, own, far, w_ref, pre_ref, sum_ref, flat, buf):
    pixels, chans = flat.shape
    band = pixels // 2
    side = ids[0]
    flat[half_at(ids, False, band), :] = own[side].astype(F32)
    flat[half_at(ids, True, band), :] = far[side].astype(F32)
    clear_rims(buf, width)
    fill(buf, flat[...], width, 0, chans)
    pre = conv(buf, (w_ref,), pixels, width)
    pre_ref[...] = pre
    pre_ref.flush()
    put_sums(sum_ref, (pre, pre * pre))


def enc_two_kernel(
    width, count, ids, labels, st1, pre1, gain1, bias1, aw_ref, w_first, w_ref,
    hid_own, hid_next, hid_core, hid_cross, pre2_ref, att_ref, sum_ref, flat, buf,
):
    pixels, chans = pre1.shape
    mom = moments(st1, 0, count)
    hidden = silu(normed(pre1[...], mom) * row_of(gain1) + row_of(bias1))
    clear_rims(buf, width)
    fill(buf, hidden, width, 0, chans)
    flat[...] = hidden
    hids = (hid_own, hid_next, hid_core, hid_cross)
    deal(hids, None, flat, ids, PLACES)
    for ref in hids:
        ref.flush()
    att = dot(hidden.astype(BF16), aw_ref[...])
    att_ref[...] = att
    att_ref.flush()
    pre = conv(buf, (w_ref,), pixels, width, w_first)
    pre2_ref[...] = pre
    pre2_ref.flush()
    put_sums(sum_ref, (pre, pre * pre, att, att * att))


def dec_one_kernel(
    width, count, ids, labels, st2, pre2, att_pre, gain2, bias2, gain_a, bias_a, aw_ref, mask, w_own, w_far,
    own, following, core, cross, shared_ref, gate_ref, pre3_ref, sum_ref, flat, hid, buf,
):
    pixels, chans = pre2.shape
    half = chans // 2
    shared = silu(normed(pre2[...], moments(st2, 0, count)) * row_of(gain2) + row_of(bias2))
    shared_ref[...] = shared
    shared_ref.flush()
    hid[...] = silu(normed(att_pre[...], moments(st2, 2, count)) * row_of(gain_a) + row_of(bias_a))
    gate = jax.nn.sigmoid(dot(hid[...].astype(BF16), aw_ref[...]))
    gate_ref[...] = gate
    gate_ref.flush()
    flat[...] = gate * shared * mask[...]
    clear_rims(buf, width)
    for other in (False, True):
        fill(buf, flat[:, half_at(ids, other, half)], width, 3 * half * other, half)
    parts = (own, following, core, cross)
    deal(parts, 0, flat, ids, CORES)
    deal(parts, 1, hid, ids, PLACES)
    for ref in parts:
        ref.flush()
    pre = conv(buf, (w_own, w_far), pixels, width)
    pre3_ref[...] = pre
    pre3_ref.flush()
    put_sums(sum_ref, (pre, pre * pre))


def dec_two_kernel(
    width, count, ids, st3, pre3, params, w_own, w_far, pre4_ref, sum_ref, keep_ref, send_ref, flat, buf
):
    pixels, chans = pre3.shape
    half = chans // 2
    flat[...] = silu(normed(pre3[...], moments(st3, 0, count)) * params[0:1, :] + params[1:2, :])
    clear_rims(buf, width)
    for other, ref in ((False, keep_ref), (True, send_ref)):
        part = flat[:, half_at(ids, other, half)]
        fill(buf, part, width, 3 * half * other, half)
        ref[...] = part.astype(BF16)
        ref.flush()
    pre = conv(buf, (w_own, w_far), pixels, width)
    pre4_ref[...] = pre
    pre4_ref.flush()
    put_sums(sum_ref, (pre, pre * pre))


def turn_kernel(ids, og_own, og_far, cot_ref, flat):
    half = flat.shape[1] // 2
    flat[:, half_at(ids, False, half)] = og_own[...].astype(F32).T
    flat[:, half_at(ids, True, half)] = og_far[...].astype(F32).T
    cot_ref[...] = flat[...]


def top_kernel(count, ids, st4, pre4, params, cot, dact_ref, sum_ref):
    xhat = normed(pre4[...], moments(st4, 0, count))
    dact = cot[...].astype(F32) * slope(xhat * params[2:3, :] + params[3:4, :])
    put_sums(sum_ref, (dact, dact * xhat))
    dact_ref[...] = dact


def decode_kernel(count, ids, st4, pre4, params, keep_ref, send_ref, out):
    half = out.shape[1] // 2
    out[...] = silu(normed(pre4[...], moments(st4, 0, count)) * params[2:3, :] + params[3:4, :])
    for other, ref in ((False, keep_ref), (True, send_ref)):
        ref[...] = out[:, half_at(ids, other, half)].T


def dec_two_back_kernel(
    width, count, ids, st4, st4b, pre4, dact4, params, w_own, w_far, st3, pre3,
    dz_own, dz_next, dz_core, dz_cross, dact_ref, sum_ref, tot_ref, flat, dz_flat, buf,
):
    pixels, chans = pre4.shape
    half = chans // 2
    total = gather_sums(st4b)
    tot_ref[...] = total
    tot_ref.flush()
    dz = norm_back(dact4[...], pre4[...], moments(st4, 0, count), params[2:3, :], total, 0, count)
    dz_flat[...] = dz
    parts = (dz_own, dz_next, dz_core, dz_cross)
    deal(parts, None, dz_flat, ids, PLACES)
    for ref in parts:
        ref.flush()
    clear_rims(buf, width)
    fill(buf, dz, width, 0, chans)
    back = conv_back(buf, (w_own, w_far), pixels, width)
    flat[:, half_at(ids, False, half)] = back[:, :half]
    flat[:, half_at(ids, True, half)] = back[:, half:]
    xhat = normed(pre3[...], moments(st3, 0, count))
    dact = flat[...] * slope(xhat * params[0:1, :] + params[1:2, :])
    dact_ref[...] = dact
    dact_ref.flush()
    put_sums(sum_ref, (dact, dact * xhat))


def dec_one_back_kernel(
    width, count, ids, labels, st3, st3b, pre3, dact3, params, w_own, w_far, mask, gate_ref, shared_ref, aw_ref,
    st2, att_pre, pre2, gain_a, bias_a, gain2, bias2,
    own, following, core, cross, datt_ref, dact2_ref, sum_ref, tot_ref, flat, dlog, dz_flat, buf,
):
    pixels, chans = pre3.shape
    half = chans // 2
    total = gather_sums(st3b)
    tot_ref[...] = total
    tot_ref.flush()
    dz = norm_back(dact3[...], pre3[...], moments(st3, 0, count), params[0:1, :], total, 0, count)
    dz_flat[...] = dz
    parts = (own, following, core, cross)
    deal(parts, 0, dz_flat, ids, PLACES)
    clear_rims(buf, width)
    fill(buf, dz, width, 0, chans)
    back = conv_back(buf, (w_own, w_far), pixels, width)
    flat[:, half_at(ids, False, half)] = back[:, :half]
    flat[:, half_at(ids, True, half)] = back[:, half:]
    grad = (flat[...] * mask[...]).astype(BF16).astype(F32)
    gate = gate_ref[...].astype(F32)
    dlog[...] = grad * shared_ref[...].astype(F32) * gate * (1.0 - gate)
    deal(parts, 1, dlog, ids, CORES)
    for ref in parts:
        ref.flush()
    dhid = dot_nt(dlog[...].astype(BF16), aw_ref[...])
    att_hat = normed(att_pre[...], moments(st2, 2, count))
    datt = dhid * slope(att_hat * row_of(gain_a) + row_of(bias_a))
    datt_ref[...] = datt
    datt_ref.flush()
    xhat2 = normed(pre2[...], moments(st2, 0, count))
    dact2 = grad * gate * slope(xhat2 * row_of(gain2) + row_of(bias2))
    dact2_ref[...] = dact2
    dact2_ref.flush()
    put_sums(sum_ref, (dact2, dact2 * xhat2, datt, datt * att_hat))


def enc_two_back_kernel(
    width, count, ids, labels, st2, st2b, att_pre, datt_ref, gain_a, pre2, dact2, gain2, aw_ref, w_ref,
    st1, pre1, gain1, bias1,
    own, core, dact_ref, sum_ref, tot_ref, flat, datt, buf,
):
    pixels, chans = pre2.shape
    total = gather_sums(st2b)
    tot_ref[...] = total
    tot_ref.flush()
    dz = norm_back(dact2[...], pre2[...], moments(st2, 0, count), row_of(gain2), total, 0, count)
    flat[...] = dz
    deal((own, core), 0, flat, ids, CORES[1:3])
    clear_rims(buf, width)
    fill(buf, dz, width, 0, chans)
    datt[...] = norm_back(
        datt_ref[...], att_pre[...], moments(st2, 2, count), row_of(gain_a), total, 2, count
    )
    deal((own, core), 1, datt, ids, CORES[1:3])
    own.flush()
    core.flush()
    dhid = dot_nt(datt[...].astype(BF16), aw_ref[...])
    dhid = dhid + conv_back(buf, (w_ref,), pixels, width)
    xhat = normed(pre1[...], moments(st1, 0, count))
    dact = dhid * slope(xhat * row_of(gain1) + row_of(bias1))
    dact_ref[...] = dact
    dact_ref.flush()
    put_sums(sum_ref, (dact, dact * xhat))


def enc_one_back_kernel(
    width, count, ids, st1, st1b, pre1, dact1, gain1, w_ref, dz_keep, dz_send, fg_keep, fg_send, tot_ref, flat, back, buf
):
    pixels, chans = pre1.shape
    half = chans // 2
    total = gather_sums(st1b)
    tot_ref[...] = total
    tot_ref.flush()
    dz = norm_back(dact1[...], pre1[...], moments(st1, 0, count), row_of(gain1), total, 0, count)
    flat[...] = dz
    for other, ref in ((False, dz_keep), (True, dz_send)):
        ref[...] = flat[:, half_at(ids, other, half)].astype(BF16)
        ref.flush()
    clear_rims(buf, width)
    fill(buf, dz, width, 0, chans)
    back[...] = conv_back(buf, (w_ref,), pixels, width)
    for other, ref in ((False, fg_keep), (True, fg_send)):
        ref[...] = back[half_at(ids, other, pixels // 2), :]


def lay_rows(ids, value, at, tmp, turned):
    rows = turned.shape[1]
    part = rows // SLABS
    tmp[at] = value.astype(F32).T.astype(BF16)
    for slot, t in enumerate(KEPT + SENT):
        start = pl.multiple_of((ids[1] ^ t) * part, part)
        turned[at, slot * part : (slot + 1) * part, :] = tmp[at, pl.ds(start, part), :]


def store_slabs(pieces, row, part, value):
    low = value.astype(BF16)
    for kept, sent in pieces:
        if row < kept.shape[1]:
            break
        row -= kept.shape[1]
    for slot in range(SLABS):
        ref, at = (kept, slot) if slot < SLABS // 2 else (sent, slot - SLABS // 2)
        ref[at, row : row + part, :] = low[slot * part : (slot + 1) * part]


def conv_weights(ids, width, values, grads, pieces, tmp, turned, bufs):
    count, _, pixels = turned.shape
    chans = bufs.shape[2] // 3
    part = turned.shape[1] // SLABS
    for at in range(count):
        lay_rows(ids, values[at](), at, tmp, turned)
        clear_rims(bufs.at[at], width)
        fill(bufs.at[at], grads[at]().astype(F32), width, 0, chans)
    for i in range(3):
        for j in range(3):
            total = None
            for at in range(count):
                term = dot(turned[at], shifted(bufs.at[at], i, j, pixels, width, chans))
                total = term if total is None else total + term
            store_slabs(pieces, (3 * i + j) * part, part, total)


def task_weights(marks, tasks, turned, grads, pieces):
    part = turned.shape[1] // SLABS
    terms = [dot(turned[at], grad()) for at, grad in enumerate(grads)]
    for task in range(tasks):
        total = None
        for mark, term in zip(marks, terms, strict=True):
            term = term * (mark == task).astype(F32)
            total = term if total is None else total + term
        store_slabs(pieces, (9 + task) * part, part, total)


def frame_marks(ids, labels, labels_next):
    side = ids[0]
    return labels[side], labels[1 - side], labels_next[side], labels_next[1 - side]


def pairs_of(refs):
    return [refs[k : k + 2] for k in range(0, len(refs), 2)]


def whole_of(ref):
    return lambda: ref[...]


def layer_of(ref, k):
    return lambda: ref[k]


def grad_dec_two_kernel(width, ids, *refs):
    kept, sent, tmp, turned, bufs = refs[8:]
    values, grads = [whole_of(r) for r in refs[:4]], [whole_of(r) for r in refs[4:8]]
    conv_weights(ids, width, values, grads, ((kept, sent),), tmp, turned, bufs)


def grad_dec_one_kernel(width, tasks, ids, labels, labels_next, *refs):
    values, grads = refs[:4], refs[4:8]
    pieces = pairs_of(refs[8:-5])
    tmp, turned, tmp_att, turned_att, bufs = refs[-5:]
    conv_weights(
        ids, width, [layer_of(r, 0) for r in values], [layer_of(r, 0) for r in grads],
        pieces, tmp, turned, bufs,
    )
    for at in range(4):
        lay_rows(ids, values[at][1], at, tmp_att, turned_att)
    marks = frame_marks(ids, labels, labels_next)
    task_weights(marks, tasks, turned_att, [layer_of(r, 1) for r in grads], pieces)


def grad_enc_two_kernel(width, tasks, ids, labels, labels_next, *refs):
    values, grads = refs[:4], refs[4:8]
    pieces = pairs_of(refs[8:-3])
    tmp, turned, bufs = refs[-3:]
    conv_weights(
        ids, width, [whole_of(r) for r in values], [layer_of(r, 0) for r in grads],
        pieces, tmp, turned, bufs,
    )
    marks = frame_marks(ids, labels, labels_next)
    task_weights(marks, tasks, turned, [layer_of(r, 1) for r in grads], pieces)


def grad_enc_one_kernel(width, ids, own, far, own_next, far_next, *refs):
    grads = [whole_of(r) for r in refs[:4]]
    kept, sent, flat, tmp, turned, bufs = refs[4:]
    band, chans = flat.shape[1] // 2, flat.shape[2]
    side = ids[0]

    def frame(at, near_band, far_band, which):
        def read():
            flat[at, half_at(ids, False, band), :] = near_band[which].astype(F32)
            flat[at, half_at(ids, True, band), :] = far_band[which].astype(F32)
            return flat[at, :, half_at(ids, False, chans // 2, 2)]

        return read

    values = [
        frame(0, own, far, side),
        frame(1, own, far, 1 - side),
        frame(2, own_next, far_next, side),
        frame(3, own_next, far_next, 1 - side),
    ]
    conv_weights(ids, width, values, grads, ((kept, sent),), tmp, turned, bufs)


def spread_kernel(by_lanes, slots, ids, *refs):
    n_pieces = len(slots)
    outs = refs[2 * n_pieces :]
    base = 0
    for out, lanes_too in zip(outs, (by_lanes, False), strict=False):
        layers, rows, lanes = out.shape
        split = lanes // 2 if lanes_too else lanes
        height = rows if lanes_too else rows // 2
        part = height // SLABS
        for layer in range(layers):
            line, piece = base + layer * part, 0
            while line >= refs[piece].shape[1]:
                line -= refs[piece].shape[1]
                piece += 1
            for other in (False, True):
                ref = refs[n_pieces + piece] if other else refs[piece]
                side = 1 - ids[2] if other else ids[2]
                for at, t in enumerate(slots[piece]):
                    start = (ids[1] ^ t) * part
                    if not lanes_too:
                        start = start + side * height
                    where = pl.ds(pl.multiple_of(start, part), part)
                    span = pl.ds(pl.multiple_of(side * split, split), split) if lanes_too else slice(None)
                    out[layer, where, span] = ref[at, line : line + part, :].astype(F32)
            out.flush(layer)
        base += layers * part


def arr(shape, kind=F32):
    return jax.ShapeDtypeStruct(shape, kind)


class Source:
    def __init__(self, pieces, buf):
        self.pieces, self.buf, self.shape = pieces, buf, buf.shape
        self.waiting = [True] * len(pieces)

    def start(self):
        for piece, wanted in zip(self.pieces, self.waiting, strict=True):
            if wanted:
                piece.start()

    def __getitem__(self, at):
        first = at[0] if isinstance(at, tuple) else at
        cut_one = len(self.pieces) > 1 and isinstance(first, int)
        for k in [first] if cut_one else range(len(self.pieces)):
            if self.waiting[k]:
                self.pieces[k].wait()
                self.waiting[k] = False
        return self.buf[at]

    def finish(self):
        for k, piece in enumerate(self.pieces):
            if self.waiting[k]:
                piece.wait()


class Target:
    def __init__(self, pieces, buf):
        self.pieces, self.buf, self.shape = pieces, buf, buf.shape
        self.sent = [False] * len(pieces)

    def __setitem__(self, at, value):
        self.buf[at] = value.astype(self.buf.dtype)

    def __getitem__(self, at):
        return self.buf[at]

    def flush(self, k=0):
        if k < len(self.pieces) and not self.sent[k]:
            self.pieces[k].start()
            self.sent[k] = True

    def finish(self):
        for k, piece in enumerate(self.pieces):
            self.flush(k)
        for piece in self.pieces:
            piece.wait()


def near(array):
    return array, "near"


def far(array):
    return array, "far"


def cut(array):
    return array, "cut"


def rest(array):
    return array, "rest"


def pick(array):
    return array, "pick"


def both(array):
    return array, "both"


def held(array, kind):
    return pltpu.with_memory_space_constraint(array, pltpu.VMEM if kind == "near" else pltpu.HBM)


def call(body, name, scalars, args, outs, scratch=(), flops=0):
    smem, vmem = pl.BlockSpec(memory_space=pltpu.SMEM), pl.BlockSpec(memory_space=pltpu.VMEM)
    hbm = pl.BlockSpec(memory_space=pltpu.HBM)
    moved = sum(a.size * a.dtype.itemsize for a, _ in list(args) + list(outs))
    arrays = list(args) + list(outs)
    pieces = [a.shape[0] if kind in ("cut", "rest") else 1 for a, kind in arrays]
    kinds = [kind for _, kind in arrays]
    bufs = [
        pltpu.VMEM(a.shape[1:] if kind == "pick" else a.shape, a.dtype)
        for a, kind in arrays
        if kind not in ("near", "both")
    ]
    places, shapes = [], []
    for a, kind in outs:
        if kind in ("near", "both"):
            places.append(vmem)
            shapes.append(pltpu.VMEM(a.shape, a.dtype))
        if kind != "near":
            places.append(hbm)
            shapes.append(pltpu.HBM(a.shape, a.dtype))
    held_bytes = sum(jnp.dtype(b.dtype).itemsize * math.prod(b.shape) for b in bufs + list(scratch))
    n_sems = max(1, sum(p for p, kind in zip(pieces, kinds, strict=True) if kind != "near"))

    def kernel(*refs):
        refs = list(refs)

        def take(count):
            taken = refs[:count]
            del refs[:count]
            return taken

        given = take(len(scalars))
        ins, results = take(len(args)), take(len(shapes))
        local, (sems,) = take(len(bufs)), take(1)
        items, slot = [], 0
        for k, kind in enumerate(kinds):
            is_out = k >= len(args)
            if kind == "near":
                items.append(Target((), results.pop(0)) if is_out else ins[k])
                continue
            inside = results.pop(0) if kind == "both" else local.pop(0)
            outside = results.pop(0) if is_out else ins[k]
            if kind == "pick":
                outside = outside.at[given[1][given[0][0]]]
            copies = []
            for piece in range(pieces[k]):
                apart = kind in ("cut", "rest")
                ends = (outside.at[piece], inside.at[piece]) if apart else (outside, inside)
                left, right = reversed(ends) if is_out else ends
                copies.append(pltpu.make_async_copy(left, right, sems.at[slot]))
                slot += 1
            items.append((Target if is_out else Source)(copies, inside))
            if kind == "rest":
                items[-1].waiting[0] = False
        for item in items:
            if isinstance(item, Source):
                item.start()
        body(*given, *items, *refs)
        for item in items:
            if isinstance(item, (Source, Target)):
                item.finish()

    return pl.pallas_call(
        kernel,
        out_shape=shapes,
        in_specs=[smem] * len(scalars) + [vmem if kind == "near" else hbm for _, kind in args],
        out_specs=places,
        scratch_shapes=bufs + [pltpu.SemaphoreType.DMA((n_sems,))] + list(scratch),
        name=name,
        compiler_params=pltpu.CompilerParams(vmem_limit_bytes=held_bytes + 8 * MIB),
        cost_estimate=pl.CostEstimate(flops=4 * flops, bytes_accessed=4 * moved, transcendentals=0),
    )(*scalars, *[held(a, kind) for a, kind in args])


def fetch_kernel(source, target, sems):
    copies = [pltpu.make_async_copy(source.at[k], target.at[k], sems.at[k]) for k in range(target.shape[0])]
    for copy in copies:
        copy.start()
    for copy in copies:
        copy.wait()


def fetch(weight, count):
    shape = (count,) + weight.shape[1:]
    return pl.pallas_call(
        fetch_kernel,
        out_shape=pltpu.VMEM(shape, weight.dtype),
        in_specs=[pl.BlockSpec(memory_space=pltpu.HBM)],
        out_specs=pl.BlockSpec(memory_space=pltpu.VMEM),
        scratch_shapes=[pltpu.SemaphoreType.DMA((count,))],
        name="fetch",
        compiler_params=pltpu.CompilerParams(vmem_limit_bytes=MIB),
        cost_estimate=pl.CostEstimate(flops=0, bytes_accessed=4 * math.prod(shape), transcendentals=0),
    )(held(weight, "far"))


def swap_cores(value):
    return lax.ppermute(value, "row", [(0, 1), (1, 0)])


def exchange(value, masks):
    count, cores = lax.axis_size("dp"), lax.axis_size("row")
    pairs = [
        (d * cores + r, (d ^ masks[r]) * cores + r) for d in range(count) for r in range(cores)
    ]
    return lax.ppermute(value, ("dp", "row"), pairs)


FIRST, SECOND, Z_NEAR, Z_FAR = (1, 2), (2, 1), (4, 4), (8, 8)


def cross(value):
    count = lax.axis_size("dp")
    pairs = [(d * 2 + r, (d ^ FIRST[1 - r]) * 2 + 1 - r) for d in range(count) for r in range(2)]
    return lax.ppermute(value, ("dp", "row"), pairs)


def dealt(to_next, to_core, to_cross):
    return swap_cores(to_core), exchange(to_next, FIRST), cross(to_cross)


def add(left, right):
    return (left.astype(F32) + right.astype(F32)).astype(BF16)


class Piece:
    def __init__(self, slabs, gather):
        kept, sent = slabs
        self.gather = (SECOND, Z_NEAR) if gather == "second" else (Z_NEAR, SECOND)
        self.slots = range(SLABS) if gather == "second" else KEPT + SENT
        self.low, self.high, self.state = kept[:2], kept[2:], 0
        self.coming = exchange(sent, SECOND)

    def step(self, order):
        got = order.after(self.coming)
        if self.state == 0:
            self.low = add(self.low, got[:2])
            self.coming = exchange(add(self.high, got[2:]), Z_NEAR)
        elif self.state == 1:
            self.low = add(self.low, got)
            self.coming = exchange(self.low, Z_FAR)
        elif self.state == 2:
            self.low = add(self.low, jnp.concatenate([got[1:], got[:1]]))
            bit = 16
            while bit < lax.axis_size("dp"):
                self.low = add(self.low, exchange(self.low, (bit, bit)))
                bit *= 2
            self.coming = exchange(self.low, self.gather[0])
        elif self.state < 5:
            self.low = jnp.concatenate([self.low, got])
            self.coming = exchange(self.low, (self.gather[1], FIRST)[self.state - 3])
        else:
            self.far_half = got
        self.state += 1
        order.done(self.low if self.state < 6 else got)


B_PARTS, C_PARTS = 2, 2
GATHER = {"a": "z", "b": "z", "c": "z", "d": "z"}
MIDDLE = "baB"
TAIL = "bBcCabdBcbCaBdcbBCcbdCBcdC12cdC3d4"


class Order:
    def __init__(self):
        self.last = None

    def after(self, value):
        return value if self.last is None else tie(self.last, value)[1]

    def done(self, value):
        self.last = value


def tie(*values):
    return lax.optimization_barrier(values)


def spread(ids, pieces, outs, by_lanes, name):
    parts = [far(p.low) for p in pieces] + [far(p.far_half) for p in pieces]
    return call(
        functools.partial(spread_kernel, by_lanes, [p.slots for p in pieces]), name, (ids,), parts,
        [cut(o) for o in outs],
    )


def all_sums(value):
    return lax.all_to_all(value, "dp", 0, 0, tiled=False)


def shards(
    frames,
    enc_w1,
    enc_gain1,
    enc_bias1,
    enc_w2,
    enc_gain2,
    enc_bias2,
    att_w1,
    att_gain,
    att_bias,
    att_w,
    dec_w1,
    dec_gain1,
    dec_bias1,
    dec_w2,
    dec_gain2,
    dec_bias2,
    labels,
    pool_index,
    out_grad,
):
    band_rows, width, in_chan = frames.shape[1:]
    chans = enc_w1.shape[3]
    half = dec_w1.shape[2]
    height = 2 * pool_index.shape[1]
    pixels = height * width
    band = band_rows * width
    tasks = att_w.shape[0]
    n_dp = lax.axis_size("dp")
    count = float(pixels * n_dp)
    core = lax.axis_index("row")
    chip = lax.axis_index("dp")
    bit_x, bit_y = chip & 1, (chip >> 1) & 1
    first = jnp.where(core == 0, bit_x, bit_y)
    second = jnp.where(core == 0, bit_y, bit_x)
    place = 4 * ((chip >> 2) & 1) + 2 * second + ((chip >> 3) & 1)
    ids = jnp.stack([core, place, first, second]).astype(jnp.int32)

    own_bands = frames.reshape(2, band, in_chan)
    far_bands, w_one, w_two = tie(
        swap_cores(own_bands), dec_w1.reshape(3, 3 * half, chans), dec_w2.reshape(3, 3 * half, chans)
    )
    d1_own, d2_own = w_one, w_two
    d1_far = swap_cores(d1_own)
    d2_far = swap_cores(d2_own)
    index = lax.dynamic_index_in_dim(pool_index, core, 0, keepdims=False)
    index = jnp.repeat(jnp.repeat(index, 2, axis=0), 2, axis=1)
    cell = 2 * (jnp.arange(height)[:, None] % 2) + jnp.arange(width)[None, :] % 2
    mask = (index == cell).astype(F32).reshape(pixels, 1)
    e1 = enc_w1.reshape(3, 3 * in_chan, chans)
    e2 = enc_w2.reshape(3, 3 * chans, chans)

    full = arr((pixels, chans), BF16)
    part = arr((pixels, half), BF16)
    pair = arr((2, pixels, half), BF16)
    two = arr((n_dp, 2, chans))
    four = arr((n_dp, 4, chans))
    flat = pltpu.VMEM((pixels, chans), F32)
    buf = pltpu.VMEM((pixels + 2 * width, 3 * chans), BF16)
    work = 2 * pixels * 9 * chans * chans

    pre1, sums = call(
        functools.partial(enc_one_kernel, width), "enc_one", (ids,),
        [far(own_bands), far(far_bands), near(fetch(e1, 3))], [far(full), near(two)],
        (pltpu.VMEM((pixels, in_chan), F32), pltpu.VMEM((pixels + 2 * width, 3 * in_chan), BF16)), work // 2,
    )
    sums, w_near, labels_then, out_then, bands_then, far_then, *vectors = tie(
        sums, e2, labels, out_grad, own_bands, far_bands, dec_gain1, dec_bias1, dec_gain2, dec_bias2
    )
    st1 = all_sums(sums)
    params_own = jnp.stack(vectors)
    params_far = swap_cores(params_own)
    params = jnp.where(
        core == 0,
        jnp.concatenate([params_own, params_far], axis=1),
        jnp.concatenate([params_far, params_own], axis=1),
    )
    labels_next = exchange(labels_then, FIRST)
    own_next, far_next = exchange(bands_then, FIRST), exchange(far_then, FIRST)
    og_own = lax.dynamic_index_in_dim(out_then, core, 1, keepdims=False)
    og_far = swap_cores(lax.dynamic_index_in_dim(out_then, 1 - core, 1, keepdims=False))
    hid1_own, hid1_next, hid1_core, hid1_cross, pre2, att_pre, sums = call(
        functools.partial(enc_two_kernel, width, count), "enc_two", (ids, labels),
        [near(st1), far(pre1), near(enc_gain1), near(enc_bias1), pick(att_w1), near(fetch(w_near, 1)), rest(e2)],
        [far(part)] * 4 + [far(full), far(full), near(four)], (flat, buf), work,
    )
    sums, w_own = tie(sums, d1_own)
    st2 = all_sums(sums)
    hid1_far = dealt(hid1_next, hid1_core, hid1_cross)
    up_own, up_next, up_core, up_cross, shared, gate, pre3, sums = call(
        functools.partial(dec_one_kernel, width, count), "dec_one", (ids, labels),
        [near(st2), far(pre2), far(att_pre), near(enc_gain2), near(enc_bias2), near(att_gain), near(att_bias),
         pick(att_w), near(mask), near(fetch(w_own, 3)), cut(d1_far)],
        [far(pair)] * 4 + [far(full), far(full), far(full), near(two)], (flat, flat, buf), work,
    )
    sums, w_own = tie(sums, d2_own)
    st3 = all_sums(sums)
    up_far = dealt(up_next, up_core, up_cross)
    pre4, sums, hidden3_own, hidden3_send = call(
        functools.partial(dec_two_kernel, width, count), "dec_two", (ids,),
        [near(st3), far(pre3), near(params), near(fetch(w_own, 3)), cut(d2_far)],
        [near(full), near(two), far(part), far(part)], (flat, buf), work,
    )
    sums, og_own, og_far = tie(sums, og_own, og_far)
    st4, hid1_far, labels_next = tie(all_sums(sums), hid1_far, labels_next)
    (cot,) = call(turn_kernel, "turn", (ids,), [far(og_own), far(og_far)], [near(full)], (flat,))
    hid3_far = dealt(hidden3_own, hidden3_send, hidden3_send)
    turned = arr((half, pixels), BF16)
    dact4, sums = call(
        functools.partial(top_kernel, count), "top", (ids,),
        [near(st4), near(pre4), near(params), near(cot)], [near(full), near(two)],
    )
    st4b = all_sums(sums)
    sums_done, pre4_again = tie(sums, pre4)
    dec_own, dec_send = call(
        functools.partial(decode_kernel, count), "decode", (ids,),
        [near(st4), near(pre4_again), near(params)], [far(turned), far(turned)], (flat,),
    )
    st4b, up_far, own_next, far_next, dec_own = tie(st4b, up_far, own_next, far_next, dec_own)
    dec_far = swap_cores(dec_send)
    dz4_own, dz4_next, dz4_core, dz4_cross, dact3, sums, tot4 = call(
        functools.partial(dec_two_back_kernel, width, count), "dec_two_back", (ids,),
        [near(st4), near(st4b), near(pre4), near(dact4), near(params), cut(d2_own), cut(d2_far), near(st3),
         far(pre3)],
        [near(part)] + [far(part)] * 3 + [near(full), near(two), far(arr((2, chans)))], (flat, flat, buf), work,
    )
    dz4_far = dealt(dz4_next, dz4_core, dz4_cross)
    tmp = pltpu.VMEM((4, half, pixels), BF16)
    bufs = pltpu.VMEM((4, pixels + 2 * width, 3 * half), BF16)

    def slabs(rows):
        return [far(arr((SLABS // 2, rows, half), BF16))] * 2

    slab = half // SLABS
    a = call(
        functools.partial(grad_dec_two_kernel, width), "grad_dec_two", (ids,),
        [far(v) for v in (hidden3_own,) + hid3_far] + [near(dz4_own)] + [far(v) for v in dz4_far],
        slabs(9 * slab), (tmp, tmp, bufs), work,
    )
    st3b, a = tie(all_sums(sums), a)
    order = Order()
    a = Piece(a, GATHER["a"])
    dz3_own, dz3_next, dz3_core, dz3_cross, datt, dact2, sums, tot3 = call(
        functools.partial(dec_one_back_kernel, width, count), "dec_one_back", (ids, labels),
        [near(st3), near(st3b), far(pre3), near(dact3), near(params), cut(d1_own), cut(d1_far), near(mask),
         far(gate), far(shared), pick(att_w), near(st2), far(att_pre), far(pre2),
         near(att_gain), near(att_bias), near(enc_gain2), near(enc_bias2)],
        [far(pair)] * 4 + [near(full), near(full), near(four), far(arr((2, chans)))],
        (flat, flat, flat, buf), work,
    )
    order.done(tot3)
    st2b, dz3_next, dz3_core, dz3_cross = tie(all_sums(sums), dz3_next, dz3_core, dz3_cross)
    dz3_far = dealt(dz3_next, dz3_core, dz3_cross)
    order.done(st2b)
    a.step(order)
    dz2_own, dz2_core, dact1, sums, tot2 = call(
        functools.partial(enc_two_back_kernel, width, count), "enc_two_back", (ids, labels),
        [near(st2), near(st2b), far(att_pre), near(datt), near(att_gain), far(pre2), near(dact2),
         near(enc_gain2), pick(att_w1), cut(e2), near(st1), far(pre1), near(enc_gain1), near(enc_bias1)],
        [far(pair), far(pair), near(full), near(two), far(arr((4, chans)))],
        (flat, flat, buf), work,
    )
    order.done(tot2)
    dz2_far = dealt(dz2_own, dz2_core, dz2_core)
    a.step(order)
    rows = (9 + tasks) * slab
    b = call(
        functools.partial(grad_dec_one_kernel, width, tasks), "grad_dec_one", (ids, labels, labels_next),
        [far(v) for v in (order.after(up_own),) + up_far + (dz3_own,) + dz3_far],
        slabs(rows // B_PARTS) * B_PARTS, (tmp, tmp, tmp, tmp, bufs), work,
    )
    order.done(b)
    pieces = {"a": a}
    pieces.update(zip("bB", (Piece(pair, GATHER["b"]) for pair in pairs_of(b)), strict=False))
    st1b = order.after(all_sums(sums))
    band_grad = arr((band, in_chan))
    dz1_own, dz1_send, fg_own, fg_send, tot1 = call(
        functools.partial(enc_one_back_kernel, width, count), "enc_one_back", (ids,),
        [near(st1), near(st1b), far(pre1), near(dact1), near(enc_gain1), cut(e1)],
        [far(part), far(part), far(band_grad), far(band_grad), far(arr((2, chans)))],
        (flat, pltpu.VMEM((pixels, in_chan), F32), buf), work // 2,
    )
    order.done(tot1)
    dz1_far = dealt(dz1_own, dz1_send, dz1_send)
    a.step(order)
    c = call(
        functools.partial(grad_enc_two_kernel, width, tasks), "grad_enc_two", (ids, labels, labels_next),
        [far(v) for v in (order.after(hid1_own),) + hid1_far + (dz2_own,) + dz2_far],
        slabs(rows // C_PARTS) * C_PARTS, (tmp, tmp, bufs), work,
    )
    order.done(c)
    pieces.update(zip("cC", (Piece(pair, GATHER["c"]) for pair in pairs_of(c)), strict=False))
    for name in MIDDLE:
        pieces[name].step(order)
    low = pltpu.VMEM((4, in_chan // 2, pixels), BF16)
    d = call(
        functools.partial(grad_enc_one_kernel, width), "grad_enc_one", (ids,),
        [far(v) for v in (own_bands, far_bands, own_next, far_next, order.after(dz1_own)) + dz1_far],
        slabs(9 * slab // 2), (pltpu.VMEM((4, pixels, in_chan), F32), low, low, bufs), work // 2,
    )
    order.done(d)
    pieces["d"] = Piece(d, GATHER["d"])
    dec_shape, enc_shape, task_shape = arr((9, half, chans)), arr((9, chans, half)), arr((tasks, chans, half))
    results = {
        "1": ("a", (dec_shape,), True, "spread_dec_two"),
        "2": ("bB"[:B_PARTS], (dec_shape, task_shape), True, "spread_dec_one"),
        "3": ("cC"[:C_PARTS], (enc_shape, task_shape), False, "spread_enc_two"),
        "4": ("d", (arr((9, in_chan, half)),), False, "spread_enc_one"),
    }
    for name in TAIL:
        if name in pieces:
            pieces[name].step(order)
            continue
        names, shapes, by_lanes, title = results[name]
        results[name] = spread(order.after(ids), [pieces[n] for n in names], shapes, by_lanes, title)
        order.done(results[name][0])
    (dec2_grad,), (dec1_grad, att_grad) = results["1"], results["2"]
    (enc2_grad, att1_grad), (enc1_grad,) = results["3"], results["4"]

    fg_far = swap_cores(fg_send)
    bands = jnp.where(core == 0, jnp.stack([fg_own, fg_far]), jnp.stack([fg_far, fg_own]))
    decoded = jnp.where(
        core == 0, jnp.stack([dec_own, dec_far], axis=1), jnp.stack([dec_far, dec_own], axis=1)
    )
    totals = jnp.concatenate([tot1, tot2, tot3, tot4])
    totals = totals + swap_cores(totals)
    dec_totals = lax.dynamic_slice_in_dim(totals[6:10], core * half, half, 1)
    return (
        decoded,
        bands.reshape(2, band_rows, width, in_chan),
        enc1_grad.reshape(3, 3, in_chan, half),
        totals[1],
        totals[0],
        enc2_grad.reshape(3, 3, chans, half),
        totals[3],
        totals[2],
        att1_grad,
        totals[5],
        totals[4],
        att_grad,
        dec1_grad.reshape(3, 3, half, chans),
        dec_totals[1],
        dec_totals[0],
        dec2_grad.reshape(3, 3, half, chans),
        dec_totals[3],
        dec_totals[2],
    )


def solution(mesh):
    return jax.shard_map(
        shards,
        mesh=mesh,
        in_specs=(
            P("dp", "row", None, None),
            P(),
            P(),
            P(),
            P(),
            P(),
            P(),
            P(),
            P(),
            P(),
            P(),
            P(None, None, "row", None),
            P("row"),
            P("row"),
            P(None, None, "row", None),
            P("row"),
            P("row"),
            P("dp"),
            P("dp", None, None),
            P("row", "dp", None),
        ),
        out_specs=(
            P("row", "dp", None),
            P("dp", "row", None, None),
            P(None, None, None, "row"),
            P(),
            P(),
            P(None, None, None, "row"),
            P(),
            P(),
            P(None, None, "row"),
            P(),
            P(),
            P(None, None, "row"),
            P(None, None, "row", None),
            P("row"),
            P("row"),
            P(None, None, "row", None),
            P("row"),
            P("row"),
        ),
        check_vma=False,
    )
```
